32 devices in a mesh: groups: 2 (over x), dp: 16 (over z, y, core).
Axes of the slice: x: 2, y: 2, z: 4, core: 2. Of those that a mesh axis runs over, the one named last changes fastest.
Arguments:
- acts: bfloat16 [12288, 8192], P(('groups', 'dp')), parts along dimension 0, may hold values from -6 to 6
- grad_out: bfloat16 [12288, 1024], P(('groups', 'dp')), parts along dimension 0, may hold values from -0.29882812 to 0.29882812
- low_acts: bfloat16 [12288, 64], P(('groups', 'dp')), parts along dimension 0, may hold values from -6 to 6
- up_weight: bfloat16 [64, 64, 1024], P('dp'), may hold values from -0.1875 to 0.1875
- block_adapter: int32 [96], P('groups'), parts along dimension 0, may hold values from 0 to 63
- block_fill: int32 [96], P(('groups', 'dp')), parts along dimension 0, may hold values from 32 to 128
- owner_slot: int32 [64], replicated, may hold values from 0 to 63, each once
Outputs:
- grad_down: bfloat16 [128, 64, 8192], P(('groups', 'dp')), parts along dimension 0
- grad_up: bfloat16 [128, 64, 1024], P(('groups', 'dp')), parts along dimension 0
The draws below stay inside these ranges and needn't reach their ends.
There are 2 independent parts, one for each index of `groups`. The reference program is written for one: setup_inputs(seed, part) draws one part's arguments, and reference() takes and returns one part's arrays. A program takes and returns all parts, laid end to end along the dimension named above; an argument that names none is the same for every part. Nothing has to cross between parts.
All inputs are finite; a program needn't handle non-finite values.
Results may differ from the reference program's by a relative error of at most 0.0049.
Values may be sent and summed in bfloat16 or wider, within the bound.
No kernel may reach another device: no remote copies, remote signals or barrier semaphores. Data moves between devices by JAX's collectives and lax.ppermute only.
A program may use at most 128 MiB of HBM per device.

```python
import math
import jax
import jax.numpy as jnp
import numpy as np
from jax import lax

D = 8192
DOUT = 1024
R = 64
BLOCK = 128
ADAPTERS = 64
BLOCKS = 48
TOKENS = 6144


def draw_block_fill(key, part):
    key = jax.random.fold_in(key, 7)
    filled = jax.random.randint(key, (BLOCKS,), BLOCK // 4, BLOCK + BLOCK // 2)
    filled = jnp.minimum(filled, BLOCK)
    filled = filled.at[0].set(BLOCK).at[1].set(BLOCK // 4)
    return filled.astype(jnp.int32)


def place_ends(drawn, stream_key, low, top_value):
    shape = drawn.shape
    spot = [jax.random.randint(jax.random.fold_in(stream_key, axis), (), 0, shape[axis]) for axis in range(len(shape))]
    drawn = drawn.at[tuple(spot)].set(low)
    longest = shape.index(max(shape))
    spot[longest] = (spot[longest] + 1) % shape[longest]
    return drawn.at[tuple(spot)].set(top_value)


def levels(stream_key, dims, cuts, smallest, largest):
    gain = 1.0
    for position, parts in cuts:
        draws = jax.random.uniform(jax.random.fold_in(jax.random.fold_in(stream_key, 6), position), (parts,), jnp.float32, smallest / len(cuts), largest / len(cuts))
        gain = gain * jnp.repeat(jnp.exp(draws), dims[position] // parts).reshape((-1,) + (1,) * (len(dims) - 1 - position))
    return gain


def rank_table(amount, skew):
    loads = [(1 << 20) // math.isqrt(grade ** skew) + 1 for grade in range(1, amount + 1)]
    spread = 1 + sum(loads) // (1 << 30)
    return np.cumsum(np.array([max(1, weight // spread) for weight in loads]))


def ranked(rng, shape, number_of, lean):
    table = rank_table(number_of, lean)
    ticket = jax.random.randint(jax.random.fold_in(rng, 1), shape, 0, int(table[number_of - 1]))
    standing = jnp.searchsorted(jnp.asarray(table, jnp.int32), ticket, side="right")
    return jax.random.permutation(jax.random.fold_in(rng, 2), number_of)[standing].astype(jnp.int32)


def centred(own_key, shape, width, bound, shards=(), kind=jnp.bfloat16):
    result = width * jax.random.normal(own_key, shape, jnp.float32)
    if shards:
        result = result * levels(own_key, shape, shards, -0.22, 0.18)
    return jnp.clip(result, -bound, bound).astype(kind)


def setup_inputs(seed: int = 0, part: int = 0) -> dict:
    seeds = jax.random.split(jax.random.key(seed), 8)
    part_splits = jax.random.split(jax.random.fold_in(seeds[7], part), 8)
    return {
        "acts": centred(part_splits[0], (TOKENS, D), 1.0, 6.0, ((0, 16),)),
        "grad_out": centred(part_splits[1], (TOKENS, DOUT), 0.05, 0.29882812, ((0, 16),)),
        "low_acts": centred(part_splits[2], (TOKENS, R), 1.0, 6.0, ((0, 16),)),
        "up_weight": centred(seeds[3], (ADAPTERS, R, DOUT), DOUT ** -0.5, 0.1875, ((0, 16),)),
        "block_adapter": place_ends(ranked(part_splits[4], (BLOCKS,), ADAPTERS, 2), jax.random.fold_in(part_splits[4], 3), 0, ADAPTERS - 1).astype(jnp.int32),
        "block_fill": draw_block_fill(jax.random.fold_in(jax.random.fold_in(seeds[7], part), 71), part),
        "owner_slot": jax.random.permutation(seeds[6], ADAPTERS).astype(jnp.int32),
    }


adapter_scale_factor = 2.0


def reference(acts, grad_out, low_acts, up_weight, block_adapter, block_fill, owner_slot):
    blocks = block_adapter.shape[0]
    positions = jnp.arange(BLOCK, dtype=jnp.int32)
    live = (positions[None, :] < block_fill[:, None]).astype(jnp.bfloat16)
    masked_gradient = grad_out.reshape(blocks, BLOCK, DOUT) * live[:, :, None]
    slot_of = owner_slot[block_adapter].astype(jnp.int32)
    act_blocks = acts.reshape(blocks, BLOCK, D)
    reduced_rank_blocks = low_acts.reshape(blocks, BLOCK, R)

    def step(adapter_index, carry):
        sum_down, sum_up = carry
        slot = slot_of[adapter_index]
        value_weight = up_weight[slot]
        reduced_rank_gradient = (adapter_scale_factor * jnp.dot(masked_gradient[adapter_index], value_weight.T, preferred_element_type=jnp.float32)).astype(jnp.bfloat16)
        term_down = jnp.dot(reduced_rank_gradient.T, act_blocks[adapter_index], preferred_element_type=jnp.float32)
        up_gradient_term = adapter_scale_factor * jnp.dot(reduced_rank_blocks[adapter_index].T, masked_gradient[adapter_index], preferred_element_type=jnp.float32)
        sum_down = sum_down.at[slot].add(term_down)
        sum_up = sum_up.at[slot].add(up_gradient_term)
        return sum_down, sum_up

    start = (jnp.zeros((ADAPTERS, R, D), jnp.float32), jnp.zeros((ADAPTERS, R, DOUT), jnp.float32))
    sum_down, sum_up = lax.fori_loop(0, blocks, step, start)
    return sum_down.astype(jnp.bfloat16), sum_up.astype(jnp.bfloat16)
```

```python
import functools

import jax
import jax.numpy as jnp
from jax import lax
from jax.experimental import pallas as pl
from jax.experimental.pallas import tpu as pltpu
from jax.sharding import PartitionSpec as P

BLOCK = 128
SCALE = 2.0
CHUNKS = 2
BF16 = jnp.bfloat16
F32 = jnp.float32
VMEM_LIMIT = 48 * 1024 * 1024


def params():
    return pltpu.CompilerParams(vmem_limit_bytes=VMEM_LIMIT)


def spec():
    return pl.BlockSpec(memory_space=pltpu.VMEM)


def pick_kernel(slot_ref, parts_ref, out_ref):
    def step(b, carry):
        out_ref[b] = parts_ref[slot_ref[b]]
        return carry

    lax.fori_loop(0, out_ref.shape[0], step, 0)


def pick(slot_of, parts):
    blocks = slot_of.shape[0]
    return pl.pallas_call(
        pick_kernel,
        out_shape=jax.ShapeDtypeStruct((blocks,) + parts.shape[1:], BF16),
        in_specs=[pl.BlockSpec(memory_space=pltpu.SMEM), spec()],
        out_specs=spec(),
        compiler_params=params(),
    )(slot_of, parts)


def low_kernel(lane_groups, fill_ref, parts_ref, grad_ref, out_ref, weight):
    parts, blocks, rows, lanes = parts_ref.shape
    for b in range(blocks):
        for p in range(parts):
            g, l = p // lane_groups, p % lane_groups
            weight[b, g * rows : (g + 1) * rows, l * lanes : (l + 1) * lanes] = parts_ref[p, b]
    for b in range(blocks):
        low = SCALE * lax.dot_general(
            weight[b],
            grad_ref[b * BLOCK : (b + 1) * BLOCK, :],
            (((1,), (1,)), ((), ())),
            preferred_element_type=F32,
        )
        live = lax.broadcasted_iota(jnp.int32, low.shape, 1) < fill_ref[b]
        out_ref[b] = jnp.where(live, low, 0.0).astype(BF16)


def rank_cotangent(fill, parts, grad, lane_groups, rank):
    blocks = fill.shape[0]
    return pl.pallas_call(
        functools.partial(low_kernel, lane_groups),
        out_shape=jax.ShapeDtypeStruct((blocks, rank, BLOCK), BF16),
        in_specs=[pl.BlockSpec(memory_space=pltpu.SMEM), spec(), spec()],
        out_specs=spec(),
        scratch_shapes=[pltpu.VMEM((blocks, rank, grad.shape[1]), BF16)],
        compiler_params=params(),
    )(fill, parts, grad)


def up_kernel(fill_ref, low_ref, grad_ref, out_ref):
    parts, blocks, rank, width = out_ref.shape
    for b in range(blocks):
        low = low_ref[:, b * BLOCK : (b + 1) * BLOCK].astype(F32)
        live = lax.broadcasted_iota(jnp.int32, low.shape, 1) < fill_ref[b]
        low = jnp.where(live, low, 0.0).astype(BF16)
        whole = SCALE * jnp.dot(
            low, grad_ref[b * BLOCK : (b + 1) * BLOCK, :], preferred_element_type=F32
        )
        for p in range(parts):
            out_ref[p, b] = whole[:, p * width : (p + 1) * width].astype(BF16)


def up_products(fill, low_t, grad, parts):
    blocks, rank = fill.shape[0], low_t.shape[0]
    return pl.pallas_call(
        up_kernel,
        out_shape=jax.ShapeDtypeStruct((parts, blocks, rank, grad.shape[1] // parts), BF16),
        in_specs=[pl.BlockSpec(memory_space=pltpu.SMEM), spec(), spec()],
        out_specs=spec(),
        compiler_params=params(),
    )(fill, low_t, grad)


def down_kernel(low_ref, acts_ref, out_ref):
    for b in range(low_ref.shape[0]):
        out_ref[0, b] = jnp.dot(
            low_ref[b], acts_ref[b * BLOCK : (b + 1) * BLOCK, :], preferred_element_type=F32
        ).astype(BF16)


def down_products(low_t, acts, parts, chunk):
    blocks, rank, _ = low_t.shape
    rows, width = acts.shape[0], acts.shape[1] // (parts * CHUNKS)
    return pl.pallas_call(
        down_kernel,
        grid=(parts,),
        out_shape=jax.ShapeDtypeStruct((parts, blocks, rank, width), BF16),
        in_specs=[
            pl.BlockSpec(low_t.shape, lambda p: (0, 0, 0)),
            pl.BlockSpec((rows, width), lambda p: (0, chunk * parts + p)),
        ],
        out_specs=pl.BlockSpec((1, blocks, rank, width), lambda p: (p, 0, 0, 0)),
        compiler_params=params(),
        cost_estimate=pl.CostEstimate(
            flops=2 * rows * rank * width * parts,
            bytes_accessed=2 * parts * width * (rows + blocks * rank),
            transcendentals=0,
        ),
    )(low_t, acts)


def sum_kernel(blocks, targets, table_ref, held_ref, *refs):
    extra_ref, out_ref = refs if len(refs) == 2 else (None, refs[0])
    first, last = blocks, blocks + targets

    def step(t, carry):
        def add(j, total):
            return total + held_ref[table_ref[j]].astype(F32)

        total = lax.fori_loop(
            table_ref[first + t], table_ref[last + t], add, jnp.zeros(out_ref.shape[1:], F32)
        )
        if extra_ref is not None:
            place = last + targets

            def add_extra(j, total):
                return total + extra_ref[j].astype(F32)

            total = lax.fori_loop(
                table_ref[place + t], table_ref[place + targets + t], add_extra, total
            )
        out_ref[t] = total.astype(BF16)
        return carry

    lax.fori_loop(0, targets, step, 0)


def slot_sums(table, held, targets, extra=None):
    operands = (held,) if extra is None else (held, extra)
    size = held.shape[1] * held.shape[2]
    moved = 2 * size * (targets + sum(x.shape[0] for x in operands))
    return pl.pallas_call(
        functools.partial(sum_kernel, held.shape[0], targets),
        out_shape=jax.ShapeDtypeStruct((targets,) + held.shape[1:], BF16),
        in_specs=[pl.BlockSpec(memory_space=pltpu.SMEM)] + [spec()] * len(operands),
        out_specs=spec(),
        compiler_params=params(),
        cost_estimate=pl.CostEstimate(
            flops=size * held.shape[0], bytes_accessed=moved, transcendentals=0
        ),
    )(table, *operands)


def place_kernel(got_ref, *refs):
    refs[-1][...] = got_ref[0]


def place(got, columns, chunk, into=None):
    parts, slots, rank, width = got.shape
    return pl.pallas_call(
        place_kernel,
        grid=(parts,),
        out_shape=jax.ShapeDtypeStruct((slots, rank, columns), BF16),
        in_specs=[pl.BlockSpec((1, slots, rank, width), lambda p: (p, 0, 0, 0))]
        + ([] if into is None else [pl.BlockSpec(memory_space=pl.ANY)]),
        out_specs=pl.BlockSpec((slots, rank, width), lambda p: (0, 0, chunk * parts + p)),
        input_output_aliases={} if into is None else {1: 0},
        compiler_params=params(),
        cost_estimate=pl.CostEstimate(
            flops=0, bytes_accessed=4 * parts * slots * rank * width, transcendentals=0
        ),
    )(*((got,) if into is None else (got, into)))


def body(devices, acts, grad_out, low_acts, up_weight, block_adapter, block_fill, owner_slot):
    own_blocks = block_fill.shape[0]
    blocks, adapters = block_adapter.shape[0], owner_slot.shape[0]
    own_slots, rank, out_width = up_weight.shape
    model_width = acts.shape[1]
    half_devices = devices // 2
    half_blocks, half_slots = blocks // 2, adapters // 2
    groups = [list(range(half_devices)), list(range(half_devices, devices))]
    across = [(i, (i + half_devices) % devices) for i in range(devices)]
    half = lax.axis_index("dp") // half_devices

    def within(x):
        return lax.all_to_all(x, "dp", 0, 0, axis_index_groups=groups, tiled=True)

    ids = jnp.arange(adapters, dtype=jnp.int32)
    slot_of = jnp.sum(
        jnp.where(block_adapter[:, None] == ids[None, :], owner_slot[None, :], 0), axis=1
    )

    lane_groups = min(devices // 4, out_width // 128)
    row_groups = devices // lane_groups
    rows, lanes = rank // row_groups, out_width // lane_groups
    pieces = up_weight.reshape(own_slots, row_groups, rows, lane_groups, lanes)
    pieces = pieces.transpose(1, 3, 0, 2, 4).reshape(devices, own_slots, rows, lanes)
    part = lax.all_to_all(pieces, "dp", 0, 0, tiled=True).reshape(adapters, rows, lanes)
    picked = pick(slot_of, part).reshape(devices, own_blocks, rows, lanes)
    weights = lax.all_to_all(picked, "dp", 0, 0, tiled=True)

    up_held = within(up_products(block_fill, low_acts.T, grad_out, half_devices))
    up_held = up_held.reshape(half_blocks, rank, -1)

    mine = lax.dynamic_slice_in_dim(slot_of, half * half_blocks, half_blocks)
    spots = jnp.arange(half_blocks, dtype=jnp.int32)
    before = (mine[None, :] < mine[:, None]) | (
        (mine[None, :] == mine[:, None]) & (spots[None, :] < spots[:, None])
    )
    spot_of = jnp.sum(before.astype(jnp.int32), axis=1)
    order = jnp.sum(jnp.where(spot_of[None, :] == spots[:, None], spots[None, :], 0), axis=1)
    start = jnp.sum((mine[None, :] < ids[:, None]).astype(jnp.int32), axis=1)
    count = jnp.sum((mine[None, :] == ids[:, None]).astype(jnp.int32), axis=1)
    by_half = slot_of.reshape(2, half_blocks)
    has = jnp.any(by_half[:, :, None] == ids[None, None, :], axis=1)
    crosses = has & ((ids[None, :] // half_slots) != jnp.arange(2, dtype=jnp.int32)[:, None])
    earlier = (ids[None, :] < ids[:, None])[None, :, :]
    place_of = jnp.sum((crosses[:, None, :] & earlier).astype(jnp.int32), axis=2)
    needed = lax.pmax(jnp.max(jnp.sum(crosses.astype(jnp.int32), axis=1)), "groups")

    my_cross = lax.dynamic_index_in_dim(crosses, half, 0, False)
    my_place = lax.dynamic_index_in_dim(place_of, half, 0, False)
    hot = my_cross[None, :] & (my_place[None, :] == spots[:, None])
    send_first = jnp.sum(jnp.where(hot, start[None, :], 0), axis=1)
    send_last = jnp.sum(jnp.where(hot, (start + count)[None, :], 0), axis=1)

    own = half * half_slots
    keep_first = lax.dynamic_slice_in_dim(start, own, half_slots)
    keep_last = keep_first + lax.dynamic_slice_in_dim(count, own, half_slots)
    got = lax.dynamic_index_in_dim(crosses, 1 - half, 0, False)
    got = lax.dynamic_slice_in_dim(got, own, half_slots).astype(jnp.int32)
    got_first = lax.dynamic_index_in_dim(place_of, 1 - half, 0, False)
    got_first = lax.dynamic_slice_in_dim(got_first, own, half_slots)
    keep_table = jnp.concatenate([order, keep_first, keep_last, got_first, got_first + got])

    low_t = rank_cotangent(block_fill, weights, grad_out, lane_groups, rank)

    def rest(capacity, acts, low_t, up_held, order, send_first, send_last, keep_table):
        send_table = jnp.concatenate([order, send_first[:capacity], send_last[:capacity]])

        def finish(held):
            crossing = slot_sums(send_table, held, capacity)
            arrived = lax.ppermute(crossing, "dp", across)
            kept = slot_sums(keep_table, held, half_slots, arrived)
            return within(kept.reshape(half_devices, own_slots, rank, -1))

        held = [
            within(down_products(low_t, acts, half_devices, c)).reshape(half_blocks, rank, -1)
            for c in range(CHUNKS)
        ]
        up = place(finish(up_held), out_width, 0) if out_width // half_devices >= 128 else (
            finish(up_held).transpose(1, 2, 0, 3).reshape(own_slots, rank, out_width)
        )
        down = None
        for c in range(CHUNKS):
            down = place(finish(held[c]), model_width, c, down)
        return down, up

    limit = min(half_blocks, half_slots)
    capacities = sorted({-(-limit * k // 24) for k in (8, 10, 12, 16, 24)})
    index = sum((needed > c).astype(jnp.int32) for c in capacities[:-1])
    return lax.switch(
        index,
        [functools.partial(rest, c) for c in capacities],
        acts, low_t, up_held, order, send_first, send_last, keep_table,
    )


def solution(mesh):
    placed = (
        P(("groups", "dp"), None),
        P(("groups", "dp"), None),
        P(("groups", "dp"), None),
        P("dp", None, None),
        P("groups"),
        P(("groups", "dp")),
        P(),
    )
    return jax.shard_map(
        functools.partial(body, mesh.shape["dp"]),
        mesh=mesh,
        in_specs=placed,
        out_specs=(P(("groups", "dp"), None, None), P(("groups", "dp"), None, None)),
        check_vma=False,
    )
```

```python
import functools

import jax
import jax.numpy as jnp
from jax import lax
from jax.experimental import pallas as pl
from jax.experimental.pallas import tpu as pltpu
from jax.sharding import PartitionSpec as P

BLOCK = 128
SCALE = 2.0
CHUNKS = 2
BF16 = jnp.bfloat16
F32 = jnp.float32
VMEM_LIMIT = 48 * 1024 * 1024


def params():
    return pltpu.CompilerParams(vmem_limit_bytes=VMEM_LIMIT)


def spec():
    return pl.BlockSpec(memory_space=pltpu.VMEM)


def pick_kernel(slot_ref, parts_ref, out_ref):
    def step(b, carry):
        out_ref[b] = parts_ref[slot_ref[b]]
        return carry

    lax.fori_loop(0, out_ref.shape[0], step, 0)


def pick(slot_of, parts):
    blocks = slot_of.shape[0]
    return pl.pallas_call(
        pick_kernel,
        out_shape=jax.ShapeDtypeStruct((blocks,) + parts.shape[1:], BF16),
        in_specs=[pl.BlockSpec(memory_space=pltpu.SMEM), spec()],
        out_specs=spec(),
        compiler_params=params(),
    )(slot_of, parts)


def low_kernel(lane_groups, fill_ref, parts_ref, grad_ref, out_ref, weight):
    parts, blocks, rows, lanes = parts_ref.shape
    for b in range(blocks):
        for p in range(parts):
            g, l = p // lane_groups, p % lane_groups
            weight[b, g * rows : (g + 1) * rows, l * lanes : (l + 1) * lanes] = parts_ref[p, b]
    for b in range(blocks):
        low = SCALE * lax.dot_general(
            weight[b],
            grad_ref[b * BLOCK : (b + 1) * BLOCK, :],
            (((1,), (1,)), ((), ())),
            preferred_element_type=F32,
        )
        live = lax.broadcasted_iota(jnp.int32, low.shape, 1) < fill_ref[b]
        low = jnp.where(live, low, 0.0).astype(BF16)
        for d in range(out_ref.shape[0]):
            out_ref[d, b] = low


def rank_cotangent(fill, parts, grad, lane_groups, rank, copies):
    blocks = fill.shape[0]
    return pl.pallas_call(
        functools.partial(low_kernel, lane_groups),
        out_shape=jax.ShapeDtypeStruct((copies, blocks, rank, BLOCK), BF16),
        in_specs=[pl.BlockSpec(memory_space=pltpu.SMEM), spec(), spec()],
        out_specs=spec(),
        scratch_shapes=[pltpu.VMEM((blocks, rank, grad.shape[1]), BF16)],
        compiler_params=params(),
    )(fill, parts, grad)


def up_kernel(fill_ref, low_ref, grad_ref, out_ref):
    parts, blocks, rank, width = out_ref.shape
    for b in range(blocks):
        low = low_ref[:, b * BLOCK : (b + 1) * BLOCK].astype(F32)
        live = lax.broadcasted_iota(jnp.int32, low.shape, 1) < fill_ref[b]
        low = jnp.where(live, low, 0.0).astype(BF16)
        whole = SCALE * jnp.dot(
            low, grad_ref[b * BLOCK : (b + 1) * BLOCK, :], preferred_element_type=F32
        )
        for p in range(parts):
            out_ref[p, b] = whole[:, p * width : (p + 1) * width].astype(BF16)


def up_products(fill, low_t, grad, parts):
    blocks, rank = fill.shape[0], low_t.shape[0]
    return pl.pallas_call(
        up_kernel,
        out_shape=jax.ShapeDtypeStruct((parts, blocks, rank, grad.shape[1] // parts), BF16),
        in_specs=[pl.BlockSpec(memory_space=pltpu.SMEM), spec(), spec()],
        out_specs=spec(),
        compiler_params=params(),
    )(fill, low_t, grad)


def split_kernel(acts_ref, out_ref):
    out_ref[0] = acts_ref[...]


def split(acts, parts, chunk):
    rows, width = acts.shape[0], acts.shape[1] // (parts * CHUNKS)
    return pl.pallas_call(
        split_kernel,
        grid=(parts,),
        out_shape=jax.ShapeDtypeStruct((parts, rows, width), BF16),
        in_specs=[pl.BlockSpec((rows, width), lambda p: (0, chunk * parts + p))],
        out_specs=pl.BlockSpec((1, rows, width), lambda p: (p, 0, 0)),
        compiler_params=params(),
        cost_estimate=pl.CostEstimate(
            flops=0, bytes_accessed=4 * parts * rows * width, transcendentals=0
        ),
    )(acts)


def down_kernel(low_ref, acts_ref, out_ref):
    for b in range(low_ref.shape[1]):
        out_ref[0, b] = jnp.dot(
            low_ref[0, b], acts_ref[b * BLOCK : (b + 1) * BLOCK, :], preferred_element_type=F32
        ).astype(BF16)


def down_products(low_t, acts, parts, chunk):
    _, blocks, rank, _ = low_t.shape
    rows, width = acts.shape[0], acts.shape[1] // (parts * CHUNKS)
    return pl.pallas_call(
        down_kernel,
        grid=(parts,),
        out_shape=jax.ShapeDtypeStruct((parts, blocks, rank, width), BF16),
        in_specs=[
            pl.BlockSpec((1,) + low_t.shape[1:], lambda p: (0, 0, 0, 0)),
            pl.BlockSpec((rows, width), lambda p: (0, chunk * parts + p)),
        ],
        out_specs=pl.BlockSpec((1, blocks, rank, width), lambda p: (p, 0, 0, 0)),
        compiler_params=params(),
        cost_estimate=pl.CostEstimate(
            flops=2 * rows * rank * width * parts,
            bytes_accessed=2 * parts * width * (rows + blocks * rank),
            transcendentals=0,
        ),
    )(low_t, acts)


def sum_kernel(blocks, targets, taken, table_ref, *refs):
    held_ref, extra_ref, out_ref = refs[-3], refs[-2], refs[-1]
    rank, whole = out_ref.shape[1:]
    width = held_ref.shape[2]
    first, last = blocks, blocks + targets
    place = last + targets

    def step(t, carry):
        begin, end = table_ref[first + t], table_ref[last + t]

        def add(j, total):
            return total + held_ref[table_ref[j]].astype(F32)

        def extras(low, high, total):
            def add_extra(j, total):
                return total + extra_ref[j, :, low:high].astype(F32)

            if extra_ref is None:
                return total
            return lax.fori_loop(
                table_ref[place + t], table_ref[place + targets + t], add_extra, total
            )

        total = lax.fori_loop(begin, end, add, jnp.zeros((rank, width), F32))
        out_ref[t, :, whole - width :] = extras(whole - width, whole, total).astype(BF16)
        if taken:
            low_ref, rows_ref = refs[0], refs[1]

            def multiply(j, total):
                b = table_ref[j]
                return total + jnp.dot(low_ref[b], rows_ref[b], preferred_element_type=F32)

            total = lax.fori_loop(begin, end, multiply, jnp.zeros((rank, whole - width), F32))
            out_ref[t, :, : whole - width] = extras(0, whole - width, total).astype(BF16)
        return carry

    lax.fori_loop(0, targets, step, 0)


def sum_only_kernel(blocks, targets, taken, table_ref, *refs):
    sum_kernel(blocks, targets, taken, table_ref, *refs[:-1], None, refs[-1])


def slot_sums(table, held, targets, extra=None, taken=()):
    blocks, rank, width = held.shape
    whole = width + (taken[1].shape[2] if taken else 0)
    operands = tuple(taken) + (held,) + (() if extra is None else (extra,))
    moved = 2 * targets * rank * whole + 2 * sum(x.size for x in operands)
    return pl.pallas_call(
        functools.partial(
            sum_only_kernel if extra is None else sum_kernel, blocks, targets, bool(taken)
        ),
        out_shape=jax.ShapeDtypeStruct((targets, rank, whole), BF16),
        in_specs=[pl.BlockSpec(memory_space=pltpu.SMEM)] + [spec()] * len(operands),
        out_specs=spec(),
        compiler_params=params(),
        cost_estimate=pl.CostEstimate(
            flops=2 * BLOCK * rank * whole * blocks, bytes_accessed=moved, transcendentals=0
        ),
    )(table, *operands)


def place_kernel(got_ref, *refs):
    refs[-1][...] = got_ref[0]


def place(got, width, columns, chunk, into=None):
    parts, slots, rank, _ = got.shape
    return pl.pallas_call(
        place_kernel,
        grid=(parts,),
        out_shape=jax.ShapeDtypeStruct((slots, rank, columns), BF16),
        in_specs=[pl.BlockSpec((1, slots, rank, width), lambda p: (p, 0, 0, 0))]
        + ([] if into is None else [pl.BlockSpec(memory_space=pl.ANY)]),
        out_specs=pl.BlockSpec((slots, rank, width), lambda p: (0, 0, chunk * parts + p)),
        input_output_aliases={} if into is None else {1: 0},
        compiler_params=params(),
        cost_estimate=pl.CostEstimate(
            flops=0, bytes_accessed=4 * parts * slots * rank * width, transcendentals=0
        ),
    )(*((got,) if into is None else (got, into)))


def body(copies, devices, acts, grad_out, low_acts, up_weight, block_adapter, block_fill, owner_slot):
    own_blocks = block_fill.shape[0]
    blocks, adapters = block_adapter.shape[0], owner_slot.shape[0]
    own_slots, rank, out_width = up_weight.shape
    model_width = acts.shape[1]
    half_devices = devices // 2
    half_blocks, half_slots = blocks // 2, adapters // 2
    groups = [list(range(half_devices)), list(range(half_devices, devices))]
    across = [(i, (i + half_devices) % devices) for i in range(devices)]
    half = lax.axis_index("dp") // half_devices

    def within(x):
        return lax.all_to_all(x, "dp", 0, 0, axis_index_groups=groups, tiled=True)

    ids = jnp.arange(adapters, dtype=jnp.int32)
    slot_of = jnp.sum(
        jnp.where(block_adapter[:, None] == ids[None, :], owner_slot[None, :], 0), axis=1
    )

    lane_groups = min(devices // 4, out_width // 128)
    row_groups = devices // lane_groups
    rows, lanes = rank // row_groups, out_width // lane_groups
    pieces = up_weight.reshape(own_slots, row_groups, rows, lane_groups, lanes)
    pieces = pieces.transpose(1, 3, 0, 2, 4).reshape(devices, own_slots, rows, lanes)
    part = lax.all_to_all(pieces, "dp", 0, 0, tiled=True).reshape(adapters, rows, lanes)
    picked = pick(slot_of, part).reshape(devices, own_blocks, rows, lanes)
    weights = lax.all_to_all(picked, "dp", 0, 0, tiled=True)

    up_held = within(up_products(block_fill, low_acts.T, grad_out, half_devices))
    up_held = up_held.reshape(half_blocks, rank, -1)

    mine = lax.dynamic_slice_in_dim(slot_of, half * half_blocks, half_blocks)
    spots = jnp.arange(half_blocks, dtype=jnp.int32)
    before = (mine[None, :] < mine[:, None]) | (
        (mine[None, :] == mine[:, None]) & (spots[None, :] < spots[:, None])
    )
    spot_of = jnp.sum(before.astype(jnp.int32), axis=1)
    order = jnp.sum(jnp.where(spot_of[None, :] == spots[:, None], spots[None, :], 0), axis=1)
    start = jnp.sum((mine[None, :] < ids[:, None]).astype(jnp.int32), axis=1)
    count = jnp.sum((mine[None, :] == ids[:, None]).astype(jnp.int32), axis=1)
    by_half = slot_of.reshape(2, half_blocks)
    has = jnp.any(by_half[:, :, None] == ids[None, None, :], axis=1)
    crosses = has & ((ids[None, :] // half_slots) != jnp.arange(2, dtype=jnp.int32)[:, None])
    earlier = (ids[None, :] < ids[:, None])[None, :, :]
    place_of = jnp.sum((crosses[:, None, :] & earlier).astype(jnp.int32), axis=2)
    mine_needed = jnp.max(jnp.sum(crosses.astype(jnp.int32), axis=1)).reshape(1, 1)
    needed = mine_needed
    for k in range(1, copies):
        shift = [(i, (i + k) % copies) for i in range(copies)]
        needed = jnp.maximum(needed, lax.ppermute(mine_needed, "groups", shift))
    needed = needed[0, 0]

    my_cross = lax.dynamic_index_in_dim(crosses, half, 0, False)
    my_place = lax.dynamic_index_in_dim(place_of, half, 0, False)
    hot = my_cross[None, :] & (my_place[None, :] == spots[:, None])
    send_first = jnp.sum(jnp.where(hot, start[None, :], 0), axis=1)
    send_last = jnp.sum(jnp.where(hot, (start + count)[None, :], 0), axis=1)

    own = half * half_slots
    keep_first = lax.dynamic_slice_in_dim(start, own, half_slots)
    keep_last = keep_first + lax.dynamic_slice_in_dim(count, own, half_slots)
    got = lax.dynamic_index_in_dim(crosses, 1 - half, 0, False)
    got = lax.dynamic_slice_in_dim(got, own, half_slots).astype(jnp.int32)
    got_first = lax.dynamic_index_in_dim(place_of, 1 - half, 0, False)
    got_first = lax.dynamic_slice_in_dim(got_first, own, half_slots)
    keep_table = jnp.concatenate([order, keep_first, keep_last, got_first, got_first + got])

    low_t = rank_cotangent(block_fill, weights, grad_out, lane_groups, rank, half_devices)
    all_low = within(low_t).reshape(half_blocks, rank, BLOCK)
    rows_held = within(split(acts, half_devices, 0)).reshape(half_blocks, BLOCK, -1)
    held = within(down_products(low_t, acts, half_devices, 1)).reshape(half_blocks, rank, -1)

    def rest(capacity, all_low, rows_held, held, up_held, order, send_first, send_last, keep_table):
        send_table = jnp.concatenate([order, send_first[:capacity], send_last[:capacity]])

        def finish(held, taken=()):
            crossing = slot_sums(send_table, held, capacity, None, taken)
            arrived = lax.ppermute(crossing, "dp", across)
            kept = slot_sums(keep_table, held, half_slots, arrived, taken)
            return within(kept.reshape(half_devices, own_slots, rank, -1))

        first = finish(up_held, (all_low, rows_held))
        second = finish(held)
        width = rows_held.shape[2]
        up = first[:, :, :, width:].transpose(1, 2, 0, 3).reshape(own_slots, rank, out_width)
        down = place(first, width, model_width, 0)
        down = place(second, width, model_width, 1, down)
        return down, up

    limit = min(half_blocks, half_slots)
    capacities = sorted({-(-limit * k // 24) for k in (8, 10, 12, 16, 24)})
    index = sum((needed > c).astype(jnp.int32) for c in capacities[:-1])
    return lax.switch(
        index,
        [functools.partial(rest, c) for c in capacities],
        all_low, rows_held, held, up_held, order, send_first, send_last, keep_table,
    )


def solution(mesh):
    placed = (
        P(("groups", "dp"), None),
        P(("groups", "dp"), None),
        P(("groups", "dp"), None),
        P("dp", None, None),
        P("groups"),
        P(("groups", "dp")),
        P(),
    )
    return jax.shard_map(
        functools.partial(body, mesh.shape["groups"], mesh.shape["dp"]),
        mesh=mesh,
        in_specs=placed,
        out_specs=(P(("groups", "dp"), None, None), P(("groups", "dp"), None, None)),
        check_vma=False,
    )
```

```python
import functools

import jax
import jax.numpy as jnp
from jax import lax
from jax.experimental import pallas as pl
from jax.experimental.pallas import tpu as pltpu
from jax.sharding import PartitionSpec as P

BLOCK = 128
SCALE = 2.0
CHUNKS = 2
BF16 = jnp.bfloat16
F32 = jnp.float32
VMEM_LIMIT = 48 * 1024 * 1024


def params():
    return pltpu.CompilerParams(vmem_limit_bytes=VMEM_LIMIT)


def spec():
    return pl.BlockSpec(memory_space=pltpu.VMEM)


def pick_kernel(slot_ref, parts_ref, out_ref):
    def step(b, carry):
        out_ref[b] = parts_ref[slot_ref[b]]
        return carry

    lax.fori_loop(0, out_ref.shape[0], step, 0)


def pick(slot_of, parts):
    blocks = slot_of.shape[0]
    return pl.pallas_call(
        pick_kernel,
        out_shape=jax.ShapeDtypeStruct((blocks,) + parts.shape[1:], BF16),
        in_specs=[pl.BlockSpec(memory_space=pltpu.SMEM), spec()],
        out_specs=spec(),
        compiler_params=params(),
    )(slot_of, parts)


def rank_kernel(lane_groups, fill_ref, parts_ref, low_ref, grad_ref, out_ref, weight):
    parts, blocks, rows, lanes = parts_ref.shape
    copies, width = out_ref.shape[0], out_ref.shape[-1]
    for b in range(blocks):
        for p in range(parts):
            g, l = p // lane_groups, p % lane_groups
            weight[b, g * rows : (g + 1) * rows, l * lanes : (l + 1) * lanes] = parts_ref[p, b]
    for b in range(blocks):
        grad = grad_ref[b * BLOCK : (b + 1) * BLOCK, :]
        turned = SCALE * lax.dot_general(
            weight[b], grad, (((1,), (1,)), ((), ())), preferred_element_type=F32
        )
        live = lax.broadcasted_iota(jnp.int32, turned.shape, 1) < fill_ref[b]
        turned = jnp.where(live, turned, 0.0).astype(BF16)
        for d in range(copies):
            out_ref[d, b] = turned


def up_kernel(fill_ref, low_ref, grad_ref, out_ref):
    parts, blocks, rank, width = out_ref.shape
    for b in range(blocks):
        low = low_ref[:, b * BLOCK : (b + 1) * BLOCK].astype(F32)
        live = lax.broadcasted_iota(jnp.int32, low.shape, 1) < fill_ref[b]
        low = jnp.where(live, low, 0.0).astype(BF16)
        whole = SCALE * jnp.dot(
            low, grad_ref[b * BLOCK : (b + 1) * BLOCK, :], preferred_element_type=F32
        )
        for p in range(parts):
            out_ref[p, b] = whole[:, p * width : (p + 1) * width].astype(BF16)


def rank_and_up_kernel(lane_groups, fill_ref, parts_ref, low_ref, grad_ref, out_ref, weight):
    rank_kernel(lane_groups, fill_ref, parts_ref, low_ref, grad_ref, out_ref, weight)
    blocks = fill_ref.shape[0]
    up_kernel(fill_ref, low_ref, grad_ref, out_ref.at[:, blocks:])


def rank_cotangent(fill, parts, low_t, grad, lane_groups, copies, with_up):
    blocks, rank = fill.shape[0], low_t.shape[0]
    return pl.pallas_call(
        functools.partial(rank_and_up_kernel if with_up else rank_kernel, lane_groups),
        out_shape=jax.ShapeDtypeStruct(
            (copies, (2 if with_up else 1) * blocks, rank, BLOCK), BF16
        ),
        in_specs=[pl.BlockSpec(memory_space=pltpu.SMEM), spec(), spec(), spec()],
        out_specs=spec(),
        scratch_shapes=[pltpu.VMEM((blocks, rank, grad.shape[1]), BF16)],
        compiler_params=params(),
    )(fill, parts, low_t, grad)


def up_products(fill, low_t, grad, parts):
    blocks, rank = fill.shape[0], low_t.shape[0]
    return pl.pallas_call(
        up_kernel,
        out_shape=jax.ShapeDtypeStruct((parts, blocks, rank, grad.shape[1] // parts), BF16),
        in_specs=[pl.BlockSpec(memory_space=pltpu.SMEM), spec(), spec()],
        out_specs=spec(),
        compiler_params=params(),
    )(fill, low_t, grad)


def down_kernel(low_ref, acts_ref, out_ref):
    for b in range(out_ref.shape[1]):
        out_ref[0, b] = jnp.dot(
            low_ref[0, b], acts_ref[b * BLOCK : (b + 1) * BLOCK, :], preferred_element_type=F32
        ).astype(BF16)


def down_products(low_t, acts, parts, chunk):
    rank, blocks = low_t.shape[2], acts.shape[0] // BLOCK
    rows, width = acts.shape[0], acts.shape[1] // (parts * CHUNKS)
    return pl.pallas_call(
        down_kernel,
        grid=(parts,),
        out_shape=jax.ShapeDtypeStruct((parts, blocks, rank, width), BF16),
        in_specs=[
            pl.BlockSpec((1,) + low_t.shape[1:], lambda p: (0, 0, 0, 0)),
            pl.BlockSpec((rows, width), lambda p: (0, chunk * parts + p)),
        ],
        out_specs=pl.BlockSpec((1, blocks, rank, width), lambda p: (p, 0, 0, 0)),
        compiler_params=params(),
        cost_estimate=pl.CostEstimate(
            flops=2 * rows * rank * width * parts,
            bytes_accessed=2 * parts * width * (rows + blocks * rank),
            transcendentals=0,
        ),
    )(low_t, acts)


def extras(extra_ref, table_ref, at, until, low, high, total):
    if extra_ref is None:
        return total

    def add(j, total):
        return total + extra_ref[j, :, low:high].astype(F32)

    return lax.fori_loop(table_ref[at], table_ref[until], add, total)


def held_kernel(blocks, has_extra, table_ref, held_ref, *refs):
    out_ref, extra_ref = refs[-1], refs[0] if has_extra else None
    targets, rank, width = out_ref.shape
    base = 3 * blocks

    def step(t, carry):
        def add(j, total):
            return total + held_ref[table_ref[j]].astype(F32)

        total = lax.fori_loop(
            table_ref[base + t],
            table_ref[base + targets + t],
            add,
            jnp.zeros((rank, width), F32),
        )
        total = extras(
            extra_ref,
            table_ref,
            base + 2 * targets + t,
            base + 3 * targets + t,
            0,
            width,
            total,
        )
        out_ref[t] = total.astype(BF16)
        return carry

    lax.fori_loop(0, targets, step, 0)


def held_sums(table, held, targets, extra=None):
    blocks, rank, width = held.shape
    operands = (held,) if extra is None else (held, extra)
    return pl.pallas_call(
        functools.partial(held_kernel, blocks, extra is not None),
        out_shape=jax.ShapeDtypeStruct((targets, rank, width), BF16),
        in_specs=[pl.BlockSpec(memory_space=pltpu.SMEM)] + [spec()] * len(operands),
        out_specs=spec(),
        compiler_params=params(),
        cost_estimate=pl.CostEstimate(
            flops=rank * width * blocks,
            bytes_accessed=2 * targets * rank * width + 2 * sum(x.size for x in operands),
            transcendentals=0,
        ),
    )(table, *operands)


def taken_kernel(blocks, has_extra, parts, has_up, table_ref, low_ref, *refs):
    up_ref, refs = (refs[0], refs[1:]) if has_up else (low_ref, refs)
    up_order, up_shift = (0, 0) if has_up else (blocks, blocks // parts)
    pieces, refs = refs[:parts], refs[parts:]
    extra_ref = refs[0] if has_extra else None
    out_ref, rows, sems = refs[-3:]
    each = blocks // parts
    copies = [
        pltpu.make_async_copy(piece, rows.at[pl.ds(k * each, each)], sems.at[k])
        for k, piece in enumerate(pieces)
    ]
    for copy in copies:
        copy.start()
    targets, rank, whole = out_ref.shape
    width = rows.shape[2]
    base = 3 * blocks
    for copy in copies:
        copy.wait()

    def step(t, carry):
        begin, end = table_ref[base + t], table_ref[base + targets + t]
        at, until = base + 2 * targets + t, base + 3 * targets + t

        def add(j, total):
            return total + up_ref[table_ref[up_order + j] + up_shift].astype(F32)

        total = lax.fori_loop(begin, end, add, jnp.zeros((rank, whole - width), F32))
        total = extras(extra_ref, table_ref, at, until, width, whole, total)
        out_ref[t, :, width:] = total.astype(BF16)

        def multiply(j, total):
            return total + jnp.dot(
                low_ref[table_ref[blocks + j]],
                rows[table_ref[2 * blocks + j]],
                preferred_element_type=F32,
            )

        total = lax.fori_loop(begin, end, multiply, jnp.zeros((rank, width), F32))
        total = extras(extra_ref, table_ref, at, until, 0, width, total)
        out_ref[t, :, :width] = total.astype(BF16)
        return carry

    lax.fori_loop(0, targets, step, 0)


def taken_sums(table, low, up, pieces, targets, extra=None, after=None):
    rank, parts, width = low.shape[1], len(pieces), pieces[0].shape[2]
    blocks = parts * pieces[0].shape[0]
    whole = width + (low if up is None else up).shape[2]
    vmem, anywhere = spec(), pl.BlockSpec(memory_space=pl.ANY)
    operands = [table, low] + ([] if up is None else [up]) + [*pieces]
    specs = [pl.BlockSpec(memory_space=pltpu.SMEM)] + [vmem] * (len(operands) - 1 - parts)
    specs += [anywhere] * parts
    if extra is not None:
        operands += [extra, after]
        specs += [vmem, anywhere]
    return pl.pallas_call(
        functools.partial(taken_kernel, blocks, extra is not None, parts, up is not None),
        out_shape=jax.ShapeDtypeStruct((targets, rank, whole), BF16),
        in_specs=specs,
        out_specs=vmem,
        scratch_shapes=[
            pltpu.VMEM((blocks, BLOCK, width), BF16),
            pltpu.SemaphoreType.DMA((parts,)),
        ],
        compiler_params=params(),
        cost_estimate=pl.CostEstimate(
            flops=2 * BLOCK * rank * whole * blocks,
            bytes_accessed=2 * targets * rank * whole + 2 * sum(x.size for x in operands[1:]),
            transcendentals=0,
        ),
    )(*operands)


def place_kernel(got_ref, *refs):
    refs[-1][...] = got_ref[0]


def place(got, width, columns, chunk, into=None):
    parts, slots, rank, _ = got.shape
    return pl.pallas_call(
        place_kernel,
        grid=(parts,),
        out_shape=jax.ShapeDtypeStruct((slots, rank, columns), BF16),
        in_specs=[pl.BlockSpec((1, slots, rank, width), lambda p: (p, 0, 0, 0))]
        + ([] if into is None else [pl.BlockSpec(memory_space=pl.ANY)]),
        out_specs=pl.BlockSpec((slots, rank, width), lambda p: (0, 0, chunk * parts + p)),
        input_output_aliases={} if into is None else {1: 0},
        compiler_params=params(),
        cost_estimate=pl.CostEstimate(
            flops=0, bytes_accessed=4 * parts * slots * rank * width, transcendentals=0
        ),
    )(*((got,) if into is None else (got, into)))


def body(copies, devices, acts, grad_out, low_acts, up_weight, block_adapter, block_fill, owner_slot):
    own_blocks = block_fill.shape[0]
    blocks, adapters = block_adapter.shape[0], owner_slot.shape[0]
    own_slots, rank, out_width = up_weight.shape
    model_width = acts.shape[1]
    half_devices = devices // 2
    half_blocks, half_slots = blocks // 2, adapters // 2
    groups = [list(range(half_devices)), list(range(half_devices, devices))]
    across = [(i, (i + half_devices) % devices) for i in range(devices)]
    half = lax.axis_index("dp") // half_devices

    def within(x):
        return lax.all_to_all(x, "dp", 0, 0, axis_index_groups=groups, tiled=True)

    ids = jnp.arange(adapters, dtype=jnp.int32)
    slot_of = jnp.sum(
        jnp.where(block_adapter[:, None] == ids[None, :], owner_slot[None, :], 0), axis=1
    )

    lane_groups = min(devices // 4, out_width // 128)
    row_groups = devices // lane_groups
    rows, lanes = rank // row_groups, out_width // lane_groups
    pieces = up_weight.reshape(own_slots, row_groups, rows, lane_groups, lanes)
    pieces = pieces.transpose(1, 3, 0, 2, 4).reshape(devices, own_slots, rows, lanes)
    part = lax.all_to_all(pieces, "dp", 0, 0, tiled=True).reshape(adapters, rows, lanes)
    picked = pick(slot_of, part).reshape(devices, own_blocks, rows, lanes)
    weights = lax.all_to_all(picked, "dp", 0, 0, tiled=True)

    place_in_half = lax.axis_index("dp") % half_devices
    width = model_width // (CHUNKS * half_devices)
    pieces = []
    for k in range(half_devices):
        piece = lax.dynamic_slice_in_dim(acts, (place_in_half ^ k) * width, width, axis=1)
        if k:
            piece = lax.ppermute(piece, "dp", [(i, i ^ k) for i in range(devices)])
        pieces.append(piece.reshape(own_blocks, BLOCK, width))

    mine = lax.dynamic_slice_in_dim(slot_of, half * half_blocks, half_blocks)
    spots = jnp.arange(half_blocks, dtype=jnp.int32)
    before = (mine[None, :] < mine[:, None]) | (
        (mine[None, :] == mine[:, None]) & (spots[None, :] < spots[:, None])
    )
    spot_of = jnp.sum(before.astype(jnp.int32), axis=1)
    order = jnp.sum(jnp.where(spot_of[None, :] == spots[:, None], spots[None, :], 0), axis=1)
    source, spot = order // own_blocks, order % own_blocks
    with_up = out_width // half_devices == BLOCK
    order = jnp.concatenate(
        [
            order,
            (2 if with_up else 1) * own_blocks * source + spot,
            (source ^ place_in_half) * own_blocks + spot,
        ]
    )
    start = jnp.sum((mine[None, :] < ids[:, None]).astype(jnp.int32), axis=1)
    count = jnp.sum((mine[None, :] == ids[:, None]).astype(jnp.int32), axis=1)
    by_half = slot_of.reshape(2, half_blocks)
    has = jnp.any(by_half[:, :, None] == ids[None, None, :], axis=1)
    crosses = has & ((ids[None, :] // half_slots) != jnp.arange(2, dtype=jnp.int32)[:, None])
    earlier = (ids[None, :] < ids[:, None])[None, :, :]
    place_of = jnp.sum((crosses[:, None, :] & earlier).astype(jnp.int32), axis=2)
    mine_needed = jnp.max(jnp.sum(crosses.astype(jnp.int32), axis=1)).reshape(1, 1)
    needed = mine_needed
    for k in range(1, copies):
        shift = [(i, (i + k) % copies) for i in range(copies)]
        needed = jnp.maximum(needed, lax.ppermute(mine_needed, "groups", shift))
    needed = needed[0, 0]

    my_cross = lax.dynamic_index_in_dim(crosses, half, 0, False)
    my_place = lax.dynamic_index_in_dim(place_of, half, 0, False)
    hot = my_cross[None, :] & (my_place[None, :] == spots[:, None])
    send_first = jnp.sum(jnp.where(hot, start[None, :], 0), axis=1)
    send_last = jnp.sum(jnp.where(hot, (start + count)[None, :], 0), axis=1)

    own = half * half_slots
    keep_first = lax.dynamic_slice_in_dim(start, own, half_slots)
    keep_last = keep_first + lax.dynamic_slice_in_dim(count, own, half_slots)
    got = lax.dynamic_index_in_dim(crosses, 1 - half, 0, False)
    got = lax.dynamic_slice_in_dim(got, own, half_slots).astype(jnp.int32)
    got_first = lax.dynamic_index_in_dim(place_of, 1 - half, 0, False)
    got_first = lax.dynamic_slice_in_dim(got_first, own, half_slots)
    keep_table = jnp.concatenate([order, keep_first, keep_last, got_first, got_first + got])

    low_t = rank_cotangent(
        block_fill, weights, low_acts.T, grad_out, lane_groups, half_devices, with_up
    )
    low = within(low_t).reshape(-1, rank, BLOCK)
    up_held = ()
    if not with_up:
        up_held = within(up_products(block_fill, low_acts.T, grad_out, half_devices))
        up_held = (up_held.reshape(half_blocks, rank, -1),)
    products = down_products(low_t, acts, half_devices, 1)

    def rest(capacity, low, up_held, products, order, send_first, send_last, keep_table, *pieces):
        up_held = up_held[0] if up_held else None
        send_table = jnp.concatenate([order, send_first[:capacity], send_last[:capacity]])
        held = within(products).reshape(half_blocks, rank, -1)
        sent_a = taken_sums(send_table, low, up_held, pieces, capacity)
        came_a = lax.ppermute(sent_a, "dp", across)
        sent_b = held_sums(send_table, held, capacity)
        came_b = lax.ppermute(sent_b, "dp", across)
        kept_a = taken_sums(keep_table, low, up_held, pieces, half_slots, came_a, sent_b)
        first = within(kept_a.reshape(half_devices, own_slots, rank, -1))
        kept_b = held_sums(keep_table, held, half_slots, came_b)
        second = within(kept_b.reshape(half_devices, own_slots, rank, -1))
        up = first[:, :, :, width:].transpose(1, 2, 0, 3).reshape(own_slots, rank, out_width)
        down = place(first, width, model_width, 0)
        down = place(second, width, model_width, 1, down)
        return down, up

    limit = min(half_blocks, half_slots)
    capacities = sorted({-(-limit * k // 24) for k in (8, 9, 10, 11, 12, 14, 16, 24)})
    index = sum((needed > c).astype(jnp.int32) for c in capacities[:-1])
    return lax.switch(
        index,
        [functools.partial(rest, c) for c in capacities],
        low, up_held, products, order, send_first, send_last, keep_table, *pieces,
    )


def solution(mesh):
    placed = (
        P(("groups", "dp"), None),
        P(("groups", "dp"), None),
        P(("groups", "dp"), None),
        P("dp", None, None),
        P("groups"),
        P(("groups", "dp")),
        P(),
    )
    return jax.shard_map(
        functools.partial(body, mesh.shape["groups"], mesh.shape["dp"]),
        mesh=mesh,
        in_specs=placed,
        out_specs=(P(("groups", "dp"), None, None), P(("groups", "dp"), None, None)),
        check_vma=False,
    )
```

```python
import functools

import jax
import jax.numpy as jnp
from jax import lax
from jax.experimental import pallas as pl
from jax.experimental.pallas import tpu as pltpu
from jax.sharding import PartitionSpec as P

BLOCK = 128
SCALE = 2.0
CHUNKS = 2
BF16 = jnp.bfloat16
F32 = jnp.float32
VMEM_LIMIT = 48 * 1024 * 1024
SMALL, LARGE = 1 << 20, 1 << 38


def params():
    return pltpu.CompilerParams(vmem_limit_bytes=VMEM_LIMIT)


def spec():
    return pl.BlockSpec(memory_space=pltpu.VMEM)


def pick_kernel(slot_ref, parts_ref, out_ref):
    def step(b, carry):
        out_ref[b] = parts_ref[slot_ref[b]]
        return carry

    lax.fori_loop(0, out_ref.shape[0], step, 0)


def pick(slot_of, parts):
    blocks = slot_of.shape[0]
    return pl.pallas_call(
        pick_kernel,
        out_shape=jax.ShapeDtypeStruct((blocks,) + parts.shape[1:], BF16),
        in_specs=[pl.BlockSpec(memory_space=pltpu.SMEM), spec()],
        out_specs=spec(),
        compiler_params=params(),
    )(slot_of, parts)


def rank_kernel(lane_groups, fill_ref, parts_ref, grad_ref, out_ref, weight):
    parts, blocks, rows, lanes = parts_ref.shape
    for b in range(blocks):
        for p in range(parts):
            g, l = p // lane_groups, p % lane_groups
            weight[b, g * rows : (g + 1) * rows, l * lanes : (l + 1) * lanes] = parts_ref[p, b]
    for b in range(blocks):
        turned = SCALE * lax.dot_general(
            weight[b],
            grad_ref[b * BLOCK : (b + 1) * BLOCK, :],
            (((1,), (1,)), ((), ())),
            preferred_element_type=F32,
        )
        live = lax.broadcasted_iota(jnp.int32, turned.shape, 1) < fill_ref[b]
        out_ref[b] = jnp.where(live, turned, 0.0).astype(BF16)


def rank_cotangent(fill, parts, grad, lane_groups, rank):
    blocks = fill.shape[0]
    return pl.pallas_call(
        functools.partial(rank_kernel, lane_groups),
        out_shape=jax.ShapeDtypeStruct((blocks, rank, BLOCK), BF16),
        in_specs=[pl.BlockSpec(memory_space=pltpu.SMEM), spec(), spec()],
        out_specs=spec(),
        scratch_shapes=[pltpu.VMEM((blocks, rank, grad.shape[1]), BF16)],
        compiler_params=params(),
    )(fill, parts, grad)


def down_kernel(low_ref, acts_ref, out_ref):
    width = acts_ref.shape[1]
    for b in range(low_ref.shape[0]):
        out_ref[0, b, :, :width] = jnp.dot(
            low_ref[b], acts_ref[b * BLOCK : (b + 1) * BLOCK, :], preferred_element_type=F32
        ).astype(BF16)


def both_kernel(fill_ref, low_ref, acts_ref, low_acts_ref, grad_ref, out_ref):
    down_kernel(low_ref, acts_ref, out_ref)
    width = acts_ref.shape[1]
    for b in range(low_ref.shape[0]):
        saved = low_acts_ref[:, b * BLOCK : (b + 1) * BLOCK].astype(F32)
        live = lax.broadcasted_iota(jnp.int32, saved.shape, 1) < fill_ref[b]
        out_ref[0, b, :, width:] = (
            SCALE
            * jnp.dot(
                jnp.where(live, saved, 0.0).astype(BF16),
                grad_ref[b * BLOCK : (b + 1) * BLOCK, :],
                preferred_element_type=F32,
            )
        ).astype(BF16)


def products(low_t, acts, parts, chunk, up=None):
    blocks, rank, _ = low_t.shape
    rows, width = acts.shape[0], acts.shape[1] // (parts * CHUNKS)
    operands = [low_t, acts]
    specs = [
        pl.BlockSpec(low_t.shape, lambda p: (0, 0, 0)),
        pl.BlockSpec((rows, width), lambda p: (0, chunk * parts + p)),
    ]
    whole = width
    if up is not None:
        fill, low_acts_t, grad = up
        up_width = grad.shape[1] // parts
        whole = width + up_width
        if up_width % 128:
            grad = grad.reshape(rows, parts, up_width).transpose(1, 0, 2)
            grad_spec = pl.BlockSpec((None, rows, up_width), lambda p: (p, 0, 0))
        else:
            grad_spec = pl.BlockSpec((rows, up_width), lambda p: (0, p))
        operands = [fill] + operands + [low_acts_t, grad]
        specs = [pl.BlockSpec(memory_space=pltpu.SMEM)] + specs
        specs += [pl.BlockSpec(low_acts_t.shape, lambda p: (0, 0)), grad_spec]
    return pl.pallas_call(
        down_kernel if up is None else both_kernel,
        grid=(parts,),
        out_shape=jax.ShapeDtypeStruct((parts, blocks, rank, whole), BF16),
        in_specs=specs,
        out_specs=pl.BlockSpec((1, blocks, rank, whole), lambda p: (p, 0, 0, 0)),
        compiler_params=params(),
        cost_estimate=pl.CostEstimate(
            flops=2 * rows * rank * whole * parts,
            bytes_accessed=2 * parts * whole * (rows + blocks * rank),
            transcendentals=0,
        ),
    )(*operands)


def sum_kernel(blocks, has_extra, table_ref, held_ref, *refs):
    out_ref = refs[-1]
    targets, rank, width = out_ref.shape

    def step(t, carry):
        def add(j, total):
            return total + held_ref[table_ref[j]].astype(F32)

        def add_extra(j, total):
            return total + refs[0][j].astype(F32)

        at = blocks + t
        zero = jnp.zeros((rank, width), F32)
        total = lax.fori_loop(table_ref[at], table_ref[at + targets], add, zero)
        if has_extra:
            at = at + 2 * targets
            total = lax.fori_loop(table_ref[at], table_ref[at + targets], add_extra, total)
        out_ref[t] = total.astype(BF16)
        return carry

    lax.fori_loop(0, targets, step, 0)


def slot_sums(table, held, targets, weight, extra=None, after=None):
    blocks, rank, width = held.shape
    operands = [held] + ([] if extra is None else [extra])
    specs = [pl.BlockSpec(memory_space=pltpu.SMEM)] + [spec()] * len(operands)
    if after is not None:
        operands.append(after)
        specs.append(pl.BlockSpec(memory_space=pl.ANY))
    return pl.pallas_call(
        functools.partial(sum_kernel, blocks, extra is not None),
        out_shape=jax.ShapeDtypeStruct((targets, rank, width), BF16),
        in_specs=specs,
        out_specs=spec(),
        compiler_params=params(),
        cost_estimate=pl.CostEstimate(
            flops=weight, bytes_accessed=weight, transcendentals=0
        ),
    )(table, *operands)


def place_kernel(got_ref, *refs):
    refs[-1][...] = got_ref[0]


def place(got, width, columns, chunk, into=None):
    parts, slots, rank, _ = got.shape
    return pl.pallas_call(
        place_kernel,
        grid=(parts,),
        out_shape=jax.ShapeDtypeStruct((slots, rank, columns), BF16),
        in_specs=[pl.BlockSpec((1, slots, rank, width), lambda p: (p, 0, 0, 0))]
        + ([] if into is None else [pl.BlockSpec(memory_space=pl.ANY)]),
        out_specs=pl.BlockSpec((slots, rank, width), lambda p: (0, 0, chunk * parts + p)),
        input_output_aliases={} if into is None else {1: 0},
        compiler_params=params(),
        cost_estimate=pl.CostEstimate(
            flops=0, bytes_accessed=4 * parts * slots * rank * width, transcendentals=0
        ),
    )(*((got,) if into is None else (got, into)))


def body(copies, devices, acts, grad_out, low_acts, up_weight, block_adapter, block_fill, owner_slot):
    own_blocks = block_fill.shape[0]
    blocks, adapters = block_adapter.shape[0], owner_slot.shape[0]
    own_slots, rank, out_width = up_weight.shape
    model_width = acts.shape[1]
    half_devices = devices // 2
    half_blocks, half_slots = blocks // 2, adapters // 2
    groups = [list(range(half_devices)), list(range(half_devices, devices))]
    across = [(i, (i + half_devices) % devices) for i in range(devices)]
    half = lax.axis_index("dp") // half_devices

    def within(x):
        return lax.all_to_all(x, "dp", 0, 0, axis_index_groups=groups, tiled=True)

    ids = jnp.arange(adapters, dtype=jnp.int32)
    slot_of = jnp.sum(
        jnp.where(block_adapter[:, None] == ids[None, :], owner_slot[None, :], 0), axis=1
    )

    lane_groups = min(devices // 4, out_width // 128)
    row_groups = devices // lane_groups
    rows, lanes = rank // row_groups, out_width // lane_groups
    pieces = up_weight.reshape(own_slots, row_groups, rows, lane_groups, lanes)
    pieces = pieces.transpose(1, 3, 0, 2, 4).reshape(devices, own_slots, rows, lanes)
    part = lax.all_to_all(pieces, "dp", 0, 0, tiled=True).reshape(adapters, rows, lanes)
    picked = pick(slot_of, part).reshape(devices, own_blocks, rows, lanes)
    weights = lax.all_to_all(picked, "dp", 0, 0, tiled=True)

    mine = lax.dynamic_slice_in_dim(slot_of, half * half_blocks, half_blocks)
    spots = jnp.arange(half_blocks, dtype=jnp.int32)
    before = (mine[None, :] < mine[:, None]) | (
        (mine[None, :] == mine[:, None]) & (spots[None, :] < spots[:, None])
    )
    spot_of = jnp.sum(before.astype(jnp.int32), axis=1)
    order = jnp.sum(jnp.where(spot_of[None, :] == spots[:, None], spots[None, :], 0), axis=1)
    start = jnp.sum((mine[None, :] < ids[:, None]).astype(jnp.int32), axis=1)
    count = jnp.sum((mine[None, :] == ids[:, None]).astype(jnp.int32), axis=1)
    by_half = slot_of.reshape(2, half_blocks)
    has = jnp.any(by_half[:, :, None] == ids[None, None, :], axis=1)
    crosses = has & ((ids[None, :] // half_slots) != jnp.arange(2, dtype=jnp.int32)[:, None])
    earlier = (ids[None, :] < ids[:, None])[None, :, :]
    place_of = jnp.sum((crosses[:, None, :] & earlier).astype(jnp.int32), axis=2)
    mine_needed = jnp.max(jnp.sum(crosses.astype(jnp.int32), axis=1)).reshape(1, 1)
    needed = mine_needed
    for k in range(1, copies):
        shift = [(i, (i + k) % copies) for i in range(copies)]
        needed = jnp.maximum(needed, lax.ppermute(mine_needed, "groups", shift))
    needed = needed[0, 0]

    my_cross = lax.dynamic_index_in_dim(crosses, half, 0, False)
    my_place = lax.dynamic_index_in_dim(place_of, half, 0, False)
    hot = my_cross[None, :] & (my_place[None, :] == spots[:, None])
    send_first = jnp.sum(jnp.where(hot, start[None, :], 0), axis=1)
    send_last = jnp.sum(jnp.where(hot, (start + count)[None, :], 0), axis=1)

    own = half * half_slots
    keep_first = lax.dynamic_slice_in_dim(start, own, half_slots)
    keep_last = keep_first + lax.dynamic_slice_in_dim(count, own, half_slots)
    got = lax.dynamic_index_in_dim(crosses, 1 - half, 0, False)
    got = lax.dynamic_slice_in_dim(got, own, half_slots).astype(jnp.int32)
    got_first = lax.dynamic_index_in_dim(place_of, 1 - half, 0, False)
    got_first = lax.dynamic_slice_in_dim(got_first, own, half_slots)
    keep_table = jnp.concatenate([order, keep_first, keep_last, got_first, got_first + got])

    low_t = rank_cotangent(block_fill, weights, grad_out, lane_groups, rank)
    first = within(products(low_t, acts, half_devices, 0, (block_fill, low_acts.T, grad_out)))
    first = first.reshape(half_blocks, rank, -1)
    second = products(low_t, acts, half_devices, 1)
    width = second.shape[3]

    def rest(capacity, first, second, order, send_first, send_last, keep_table):
        send_table = jnp.concatenate([order, send_first[:capacity], send_last[:capacity]])
        second = within(second).reshape(half_blocks, rank, -1)
        sent_a = slot_sums(send_table, first, capacity, SMALL)
        came_a = lax.ppermute(sent_a, "dp", across)
        sent_b = slot_sums(send_table, second, capacity, SMALL)
        came_b = lax.ppermute(sent_b, "dp", across)
        kept_a = slot_sums(keep_table, first, half_slots, SMALL, came_a, sent_b)
        done_a = within(kept_a.reshape(half_devices, own_slots, rank, -1))
        kept_b = slot_sums(keep_table, second, half_slots, LARGE, came_b)
        done_b = within(kept_b.reshape(half_devices, own_slots, rank, -1))
        up = done_a[:, :, :, width:].transpose(1, 2, 0, 3).reshape(own_slots, rank, out_width)
        down = place(done_a, width, model_width, 0)
        down = place(done_b, width, model_width, 1, down)
        return down, up

    limit = min(half_blocks, half_slots)
    capacities = sorted({-(-limit * k // 24) for k in (8, 9, 10, 11, 12, 14, 16, 24)})
    index = sum((needed > c).astype(jnp.int32) for c in capacities[:-1])
    return lax.switch(
        index,
        [functools.partial(rest, c) for c in capacities],
        first, second, order, send_first, send_last, keep_table,
    )


def solution(mesh):
    placed = (
        P(("groups", "dp"), None),
        P(("groups", "dp"), None),
        P(("groups", "dp"), None),
        P("dp", None, None),
        P("groups"),
        P(("groups", "dp")),
        P(),
    )
    return jax.shard_map(
        functools.partial(body, mesh.shape["groups"], mesh.shape["dp"]),
        mesh=mesh,
        in_specs=placed,
        out_specs=(P(("groups", "dp"), None, None), P(("groups", "dp"), None, None)),
        check_vma=False,
    )
```

```python
import functools

import jax
import jax.numpy as jnp
from jax import lax
from jax.experimental import pallas as pl
from jax.experimental.pallas import tpu as pltpu
from jax.sharding import PartitionSpec as P

BLOCK = 128
SCALE = 2.0
CHUNKS = 2
BF16 = jnp.bfloat16
F32 = jnp.float32
VMEM_LIMIT = 48 * 1024 * 1024
SMALL, LARGE = 1 << 20, 1 << 38


def params():
    return pltpu.CompilerParams(vmem_limit_bytes=VMEM_LIMIT)


def spec():
    return pl.BlockSpec(memory_space=pltpu.VMEM)


def pick_kernel(slot_ref, parts_ref, *refs):
    out_ref = refs[-1]

    def step(b, carry):
        out_ref[b] = parts_ref[slot_ref[b]]
        return carry

    lax.fori_loop(0, out_ref.shape[0], step, 0)


def pick(slot_of, parts, after):
    blocks = slot_of.shape[0]
    return pl.pallas_call(
        pick_kernel,
        out_shape=jax.ShapeDtypeStruct((blocks,) + parts.shape[1:], BF16),
        in_specs=[pl.BlockSpec(memory_space=pltpu.SMEM), spec()]
        + [pl.BlockSpec(memory_space=pl.ANY)] * len(after),
        out_specs=spec(),
        compiler_params=params(),
    )(slot_of, parts, *after)


def rank_kernel(lane_groups, fill_ref, parts_ref, low_ref, grad_ref, *refs):
    out_ref, weight = refs[-2:]
    parts, blocks, rows, lanes = parts_ref.shape
    copies, width = out_ref.shape[0], out_ref.shape[-1]
    for b in range(blocks):
        for p in range(parts):
            g, l = p // lane_groups, p % lane_groups
            weight[b, g * rows : (g + 1) * rows, l * lanes : (l + 1) * lanes] = parts_ref[p, b]
    for b in range(blocks):
        grad = grad_ref[b * BLOCK : (b + 1) * BLOCK, :]
        turned = SCALE * lax.dot_general(
            weight[b], grad, (((1,), (1,)), ((), ())), preferred_element_type=F32
        )
        live = lax.broadcasted_iota(jnp.int32, turned.shape, 1) < fill_ref[b]
        turned = jnp.where(live, turned, 0.0).astype(BF16)
        for d in range(copies):
            out_ref[d, b] = turned


def up_kernel(fill_ref, low_ref, grad_ref, out_ref):
    parts, blocks, rank, width = out_ref.shape
    for b in range(blocks):
        low = low_ref[:, b * BLOCK : (b + 1) * BLOCK].astype(F32)
        live = lax.broadcasted_iota(jnp.int32, low.shape, 1) < fill_ref[b]
        low = jnp.where(live, low, 0.0).astype(BF16)
        whole = SCALE * jnp.dot(
            low, grad_ref[b * BLOCK : (b + 1) * BLOCK, :], preferred_element_type=F32
        )
        for p in range(parts):
            out_ref[p, b] = whole[:, p * width : (p + 1) * width].astype(BF16)


def rank_and_up_kernel(lane_groups, fill_ref, parts_ref, low_ref, grad_ref, *refs):
    out_ref, weight = refs[-2:]
    rank_kernel(lane_groups, fill_ref, parts_ref, low_ref, grad_ref, out_ref, weight)
    blocks = fill_ref.shape[0]
    up_kernel(fill_ref, low_ref, grad_ref, out_ref.at[:, blocks:])


def rank_cotangent(fill, parts, low_t, grad, lane_groups, copies, with_up, after):
    blocks, rank = fill.shape[0], low_t.shape[0]
    return pl.pallas_call(
        functools.partial(rank_and_up_kernel if with_up else rank_kernel, lane_groups),
        out_shape=jax.ShapeDtypeStruct(
            (copies, (2 if with_up else 1) * blocks, rank, BLOCK), BF16
        ),
        in_specs=[pl.BlockSpec(memory_space=pltpu.SMEM), spec(), spec(), spec()]
        + [pl.BlockSpec(memory_space=pl.ANY)] * len(after),
        out_specs=spec(),
        scratch_shapes=[pltpu.VMEM((blocks, rank, grad.shape[1]), BF16)],
        compiler_params=params(),
    )(fill, parts, low_t, grad, *after)


def up_products(fill, low_t, grad, parts):
    blocks, rank = fill.shape[0], low_t.shape[0]
    return pl.pallas_call(
        up_kernel,
        out_shape=jax.ShapeDtypeStruct((parts, blocks, rank, grad.shape[1] // parts), BF16),
        in_specs=[pl.BlockSpec(memory_space=pltpu.SMEM), spec(), spec()],
        out_specs=spec(),
        compiler_params=params(),
    )(fill, low_t, grad)


def down_kernel(low_ref, acts_ref, out_ref):
    for b in range(out_ref.shape[1]):
        out_ref[0, b] = jnp.dot(
            low_ref[0, b], acts_ref[b * BLOCK : (b + 1) * BLOCK, :], preferred_element_type=F32
        ).astype(BF16)


def down_products(low_t, acts, parts, chunk):
    rank, blocks = low_t.shape[2], acts.shape[0] // BLOCK
    rows, width = acts.shape[0], acts.shape[1] // (parts * CHUNKS)
    return pl.pallas_call(
        down_kernel,
        grid=(parts,),
        out_shape=jax.ShapeDtypeStruct((parts, blocks, rank, width), BF16),
        in_specs=[
            pl.BlockSpec((1,) + low_t.shape[1:], lambda p: (0, 0, 0, 0)),
            pl.BlockSpec((rows, width), lambda p: (0, chunk * parts + p)),
        ],
        out_specs=pl.BlockSpec((1, blocks, rank, width), lambda p: (p, 0, 0, 0)),
        compiler_params=params(),
        cost_estimate=pl.CostEstimate(
            flops=2 * rows * rank * width * parts,
            bytes_accessed=2 * parts * width * (rows + blocks * rank),
            transcendentals=0,
        ),
    )(low_t, acts)


def extras(extra_ref, table_ref, at, until, low, high, total):
    if extra_ref is None:
        return total

    def add(j, total):
        return total + extra_ref[j, :, low:high].astype(F32)

    return lax.fori_loop(table_ref[at], table_ref[until], add, total)


def held_kernel(blocks, has_extra, table_ref, held_ref, *refs):
    out_ref, extra_ref = refs[-1], refs[0] if has_extra else None
    targets, rank, width = out_ref.shape
    base = 3 * blocks

    def step(t, carry):
        def add(j, total):
            return total + held_ref[table_ref[j]].astype(F32)

        total = lax.fori_loop(
            table_ref[base + t],
            table_ref[base + targets + t],
            add,
            jnp.zeros((rank, width), F32),
        )
        total = extras(
            extra_ref,
            table_ref,
            base + 2 * targets + t,
            base + 3 * targets + t,
            0,
            width,
            total,
        )
        out_ref[t] = total.astype(BF16)
        return carry

    lax.fori_loop(0, targets, step, 0)


def held_sums(table, held, targets, weight, extra=None):
    blocks, rank, width = held.shape
    operands = (held,) if extra is None else (held, extra)
    return pl.pallas_call(
        functools.partial(held_kernel, blocks, extra is not None),
        out_shape=jax.ShapeDtypeStruct((targets, rank, width), BF16),
        in_specs=[pl.BlockSpec(memory_space=pltpu.SMEM)] + [spec()] * len(operands),
        out_specs=spec(),
        compiler_params=params(),
        cost_estimate=pl.CostEstimate(
            flops=weight, bytes_accessed=weight, transcendentals=0
        ),
    )(table, *operands)


def taken_kernel(blocks, has_extra, parts, has_up, table_ref, low_ref, *refs):
    up_ref, refs = (refs[0], refs[1:]) if has_up else (low_ref, refs)
    up_order, up_shift = (0, 0) if has_up else (blocks, blocks // parts)
    pieces, refs = refs[:parts], refs[parts:]
    extra_ref = refs[0] if has_extra else None
    out_ref, rows, sems = refs[-3:]
    each = blocks // parts
    copies = [
        pltpu.make_async_copy(piece, rows.at[pl.ds(k * each, each)], sems.at[k])
        for k, piece in enumerate(pieces)
    ]
    for copy in copies:
        copy.start()
    targets, rank, whole = out_ref.shape
    width = rows.shape[2]
    base = 3 * blocks
    for copy in copies:
        copy.wait()

    def step(t, carry):
        begin, end = table_ref[base + t], table_ref[base + targets + t]
        at, until = base + 2 * targets + t, base + 3 * targets + t

        def add(j, total):
            return total + up_ref[table_ref[up_order + j] + up_shift].astype(F32)

        total = lax.fori_loop(begin, end, add, jnp.zeros((rank, whole - width), F32))
        total = extras(extra_ref, table_ref, at, until, width, whole, total)
        out_ref[t, :, width:] = total.astype(BF16)

        def multiply(j, total):
            return total + jnp.dot(
                low_ref[table_ref[blocks + j]],
                rows[table_ref[2 * blocks + j]],
                preferred_element_type=F32,
            )

        total = lax.fori_loop(begin, end, multiply, jnp.zeros((rank, width), F32))
        total = extras(extra_ref, table_ref, at, until, 0, width, total)
        out_ref[t, :, :width] = total.astype(BF16)
        return carry

    lax.fori_loop(0, targets, step, 0)


def taken_sums(table, low, up, pieces, targets, extra=None, after=None):
    rank, parts, width = low.shape[1], len(pieces), pieces[0].shape[2]
    blocks = parts * pieces[0].shape[0]
    whole = width + (low if up is None else up).shape[2]
    vmem, anywhere = spec(), pl.BlockSpec(memory_space=pl.ANY)
    operands = [table, low] + ([] if up is None else [up]) + [*pieces]
    specs = [pl.BlockSpec(memory_space=pltpu.SMEM)] + [vmem] * (len(operands) - 1 - parts)
    specs += [anywhere] * parts
    if extra is not None:
        operands += [extra, after]
        specs += [vmem, anywhere]
    return pl.pallas_call(
        functools.partial(taken_kernel, blocks, extra is not None, parts, up is not None),
        out_shape=jax.ShapeDtypeStruct((targets, rank, whole), BF16),
        in_specs=specs,
        out_specs=vmem,
        scratch_shapes=[
            pltpu.VMEM((blocks, BLOCK, width), BF16),
            pltpu.SemaphoreType.DMA((parts,)),
        ],
        compiler_params=params(),
        cost_estimate=pl.CostEstimate(
            flops=SMALL, bytes_accessed=SMALL, transcendentals=0
        ),
    )(*operands)


def place_kernel(got_ref, *refs):
    refs[-1][...] = got_ref[0]


def place(got, width, columns, chunk, into=None):
    parts, slots, rank, _ = got.shape
    return pl.pallas_call(
        place_kernel,
        grid=(parts,),
        out_shape=jax.ShapeDtypeStruct((slots, rank, columns), BF16),
        in_specs=[pl.BlockSpec((1, slots, rank, width), lambda p: (p, 0, 0, 0))]
        + ([] if into is None else [pl.BlockSpec(memory_space=pl.ANY)]),
        out_specs=pl.BlockSpec((slots, rank, width), lambda p: (0, 0, chunk * parts + p)),
        input_output_aliases={} if into is None else {1: 0},
        compiler_params=params(),
        cost_estimate=pl.CostEstimate(
            flops=0, bytes_accessed=4 * parts * slots * rank * width, transcendentals=0
        ),
    )(*((got,) if into is None else (got, into)))


def body(copies, devices, acts, grad_out, low_acts, up_weight, block_adapter, block_fill, owner_slot):
    own_blocks = block_fill.shape[0]
    blocks, adapters = block_adapter.shape[0], owner_slot.shape[0]
    own_slots, rank, out_width = up_weight.shape
    model_width = acts.shape[1]
    half_devices = devices // 2
    half_blocks, half_slots = blocks // 2, adapters // 2
    groups = [list(range(half_devices)), list(range(half_devices, devices))]
    across = [(i, (i + half_devices) % devices) for i in range(devices)]
    half = lax.axis_index("dp") // half_devices

    def within(x):
        return lax.all_to_all(x, "dp", 0, 0, axis_index_groups=groups, tiled=True)

    ids = jnp.arange(adapters, dtype=jnp.int32)
    slot_of = jnp.sum(
        jnp.where(block_adapter[:, None] == ids[None, :], owner_slot[None, :], 0), axis=1
    )

    place_in_half = lax.axis_index("dp") % half_devices
    width = model_width // (CHUNKS * half_devices)
    early = half_devices // 2
    pieces = []
    for k in range(half_devices):
        piece = lax.dynamic_slice_in_dim(acts, (place_in_half ^ k) * width, width, axis=1)
        if k:
            piece = lax.ppermute(piece, "dp", [(i, i ^ k) for i in range(devices)])
        pieces.append(piece.reshape(own_blocks, BLOCK, width))

    lane_groups = min(devices // 4, out_width // 128)
    row_groups = devices // lane_groups
    rows, lanes = rank // row_groups, out_width // lane_groups
    shares = up_weight.reshape(own_slots, row_groups, rows, lane_groups, lanes)
    shares = shares.transpose(1, 3, 0, 2, 4).reshape(devices, own_slots, rows, lanes)
    part = lax.all_to_all(shares, "dp", 0, 0, tiled=True).reshape(adapters, rows, lanes)
    picked = pick(slot_of, part, pieces[1:early]).reshape(devices, own_blocks, rows, lanes)
    weights = lax.all_to_all(picked, "dp", 0, 0, tiled=True)

    mine = lax.dynamic_slice_in_dim(slot_of, half * half_blocks, half_blocks)
    spots = jnp.arange(half_blocks, dtype=jnp.int32)
    before = (mine[None, :] < mine[:, None]) | (
        (mine[None, :] == mine[:, None]) & (spots[None, :] < spots[:, None])
    )
    spot_of = jnp.sum(before.astype(jnp.int32), axis=1)
    order = jnp.sum(jnp.where(spot_of[None, :] == spots[:, None], spots[None, :], 0), axis=1)
    source, spot = order // own_blocks, order % own_blocks
    with_up = out_width // half_devices == BLOCK
    order = jnp.concatenate(
        [
            order,
            (2 if with_up else 1) * own_blocks * source + spot,
            (source ^ place_in_half) * own_blocks + spot,
        ]
    )
    start = jnp.sum((mine[None, :] < ids[:, None]).astype(jnp.int32), axis=1)
    count = jnp.sum((mine[None, :] == ids[:, None]).astype(jnp.int32), axis=1)
    by_half = slot_of.reshape(2, half_blocks)
    has = jnp.any(by_half[:, :, None] == ids[None, None, :], axis=1)
    crosses = has & ((ids[None, :] // half_slots) != jnp.arange(2, dtype=jnp.int32)[:, None])
    earlier = (ids[None, :] < ids[:, None])[None, :, :]
    place_of = jnp.sum((crosses[:, None, :] & earlier).astype(jnp.int32), axis=2)
    mine_needed = jnp.max(jnp.sum(crosses.astype(jnp.int32), axis=1)).reshape(1, 1)
    needed = mine_needed
    for k in range(1, copies):
        shift = [(i, (i + k) % copies) for i in range(copies)]
        needed = jnp.maximum(needed, lax.ppermute(mine_needed, "groups", shift))
    needed = needed[0, 0]

    my_cross = lax.dynamic_index_in_dim(crosses, half, 0, False)
    my_place = lax.dynamic_index_in_dim(place_of, half, 0, False)
    hot = my_cross[None, :] & (my_place[None, :] == spots[:, None])
    send_first = jnp.sum(jnp.where(hot, start[None, :], 0), axis=1)
    send_last = jnp.sum(jnp.where(hot, (start + count)[None, :], 0), axis=1)

    own = half * half_slots
    keep_first = lax.dynamic_slice_in_dim(start, own, half_slots)
    keep_last = keep_first + lax.dynamic_slice_in_dim(count, own, half_slots)
    got = lax.dynamic_index_in_dim(crosses, 1 - half, 0, False)
    got = lax.dynamic_slice_in_dim(got, own, half_slots).astype(jnp.int32)
    got_first = lax.dynamic_index_in_dim(place_of, 1 - half, 0, False)
    got_first = lax.dynamic_slice_in_dim(got_first, own, half_slots)
    keep_table = jnp.concatenate([order, keep_first, keep_last, got_first, got_first + got])

    low_t = rank_cotangent(
        block_fill, weights, low_acts.T, grad_out, lane_groups, half_devices, with_up, pieces[early:]
    )
    low = within(low_t).reshape(-1, rank, BLOCK)
    up_held = ()
    if not with_up:
        up_held = within(up_products(block_fill, low_acts.T, grad_out, half_devices))
        up_held = (up_held.reshape(half_blocks, rank, -1),)
    products = down_products(low_t, acts, half_devices, 1)

    def rest(capacity, low, up_held, products, order, send_first, send_last, keep_table, *pieces):
        up_held = up_held[0] if up_held else None
        send_table = jnp.concatenate([order, send_first[:capacity], send_last[:capacity]])
        held = within(products).reshape(half_blocks, rank, -1)
        sent_a = taken_sums(send_table, low, up_held, pieces, capacity)
        came_a = lax.ppermute(sent_a, "dp", across)
        sent_b = held_sums(send_table, held, capacity, SMALL)
        came_b = lax.ppermute(sent_b, "dp", across)
        kept_a = taken_sums(keep_table, low, up_held, pieces, half_slots, came_a, sent_b)
        first = within(kept_a.reshape(half_devices, own_slots, rank, -1))
        kept_b = held_sums(keep_table, held, half_slots, LARGE, came_b)
        second = within(kept_b.reshape(half_devices, own_slots, rank, -1))
        up = first[:, :, :, width:].transpose(1, 2, 0, 3).reshape(own_slots, rank, out_width)
        down = place(first, width, model_width, 0)
        down = place(second, width, model_width, 1, down)
        return down, up

    limit = min(half_blocks, half_slots)
    capacities = sorted({-(-limit * k // 24) for k in (8, 9, 10, 11, 12, 14, 16, 24)})
    index = sum((needed > c).astype(jnp.int32) for c in capacities[:-1])
    return lax.switch(
        index,
        [functools.partial(rest, c) for c in capacities],
        low, up_held, products, order, send_first, send_last, keep_table, *pieces,
    )


def solution(mesh):
    placed = (
        P(("groups", "dp"), None),
        P(("groups", "dp"), None),
        P(("groups", "dp"), None),
        P("dp", None, None),
        P("groups"),
        P(("groups", "dp")),
        P(),
    )
    return jax.shard_map(
        functools.partial(body, mesh.shape["groups"], mesh.shape["dp"]),
        mesh=mesh,
        in_specs=placed,
        out_specs=(P(("groups", "dp"), None, None), P(("groups", "dp"), None, None)),
        check_vma=False,
    )
```

```python
import functools

import jax
import jax.numpy as jnp
from jax import lax
from jax.experimental import pallas as pl
from jax.experimental.pallas import tpu as pltpu
from jax.sharding import PartitionSpec as P

BLOCK = 128
SCALE = 2.0
CHUNKS = 2
PARTS_A_STEP = 4
EARLY = 5
BF16 = jnp.bfloat16
F32 = jnp.float32
VMEM_LIMIT = 48 * 1024 * 1024
SMALL, LARGE = 1 << 20, 1 << 38


def params():
    return pltpu.CompilerParams(vmem_limit_bytes=VMEM_LIMIT)


def spec():
    return pl.BlockSpec(memory_space=pltpu.VMEM)


def pick_kernel(slot_ref, parts_ref, out_ref):
    def step(b, carry):
        out_ref[b] = parts_ref[slot_ref[b]]
        return carry

    lax.fori_loop(0, out_ref.shape[0], step, 0)


def pick(slot_of, parts):
    blocks = slot_of.shape[0]
    return pl.pallas_call(
        pick_kernel,
        out_shape=jax.ShapeDtypeStruct((blocks,) + parts.shape[1:], BF16),
        in_specs=[pl.BlockSpec(memory_space=pltpu.SMEM), spec()],
        out_specs=spec(),
        compiler_params=params(),
    )(slot_of, parts)


def rank_kernel(lane_groups, fill_ref, parts_ref, grad_ref, *refs):
    out_ref, weight = refs[-2:]
    parts, blocks, rows, lanes = parts_ref.shape
    for b in range(blocks):
        for p in range(parts):
            g, l = p // lane_groups, p % lane_groups
            weight[b, g * rows : (g + 1) * rows, l * lanes : (l + 1) * lanes] = parts_ref[p, b]
    for b in range(blocks):
        turned = SCALE * lax.dot_general(
            weight[b],
            grad_ref[b * BLOCK : (b + 1) * BLOCK, :],
            (((1,), (1,)), ((), ())),
            preferred_element_type=F32,
        )
        live = lax.broadcasted_iota(jnp.int32, turned.shape, 1) < fill_ref[b]
        out_ref[b] = jnp.where(live, turned, 0.0).astype(BF16)


def rank_cotangent(fill, parts, grad, lane_groups, rank, after):
    blocks = fill.shape[0]
    return pl.pallas_call(
        functools.partial(rank_kernel, lane_groups),
        out_shape=jax.ShapeDtypeStruct((blocks, rank, BLOCK), BF16),
        in_specs=[pl.BlockSpec(memory_space=pltpu.SMEM), spec(), spec()]
        + [pl.BlockSpec(memory_space=pl.ANY)] * len(after),
        out_specs=spec(),
        scratch_shapes=[pltpu.VMEM((blocks, rank, grad.shape[1]), BF16)],
        compiler_params=params(),
    )(fill, parts, grad, *after)


def up_kernel(fill_ref, low_ref, grad_ref, out_ref):
    parts, blocks, rank, width = out_ref.shape
    for b in range(blocks):
        low = low_ref[:, b * BLOCK : (b + 1) * BLOCK].astype(F32)
        live = lax.broadcasted_iota(jnp.int32, low.shape, 1) < fill_ref[b]
        low = jnp.where(live, low, 0.0).astype(BF16)
        whole = SCALE * jnp.dot(
            low, grad_ref[b * BLOCK : (b + 1) * BLOCK, :], preferred_element_type=F32
        )
        for p in range(parts):
            out_ref[p, b] = whole[:, p * width : (p + 1) * width].astype(BF16)


def up_products(fill, low_t, grad, parts):
    blocks, rank = fill.shape[0], low_t.shape[0]
    return pl.pallas_call(
        up_kernel,
        out_shape=jax.ShapeDtypeStruct((parts, blocks, rank, grad.shape[1] // parts), BF16),
        in_specs=[pl.BlockSpec(memory_space=pltpu.SMEM), spec(), spec()],
        out_specs=spec(),
        compiler_params=params(),
    )(fill, low_t, grad)


def down_kernel(low_ref, acts_ref, out_ref):
    parts, blocks, _, width = out_ref.shape
    for p in range(parts):
        for b in range(blocks):
            out_ref[p, b] = jnp.dot(
                low_ref[b],
                acts_ref[b * BLOCK : (b + 1) * BLOCK, p * width : (p + 1) * width],
                preferred_element_type=F32,
            ).astype(BF16)


def products(low_t, acts, parts, chunk):
    blocks, rank, _ = low_t.shape
    rows, width = acts.shape[0], acts.shape[1] // (parts * CHUNKS)
    steps = max(parts // PARTS_A_STEP, 1)
    each = parts // steps
    return pl.pallas_call(
        down_kernel,
        grid=(steps,),
        out_shape=jax.ShapeDtypeStruct((parts, blocks, rank, width), BF16),
        in_specs=[
            pl.BlockSpec(low_t.shape, lambda p: (0, 0, 0)),
            pl.BlockSpec((rows, width * each), lambda p: (0, chunk * steps + p)),
        ],
        out_specs=pl.BlockSpec((each, blocks, rank, width), lambda p: (p, 0, 0, 0)),
        compiler_params=params(),
        cost_estimate=pl.CostEstimate(
            flops=2 * rows * rank * width * parts,
            bytes_accessed=2 * parts * width * (rows + blocks * rank),
            transcendentals=0,
        ),
    )(low_t, acts)


def sum_kernel(blocks, count, has_extra, outs, table_ref, *refs):
    held, outs = refs[:count], refs[-outs:]
    extra_ref = refs[count] if has_extra else None
    targets = sum(out.shape[0] for out in outs)
    rank = outs[0].shape[1]
    base = blocks * count

    for n, out_ref in enumerate(outs):
        shift = n * out_ref.shape[0]

        def step(m, carry, out_ref=out_ref, shift=shift):
            at = base + shift + m
            low = 0
            for i, held_ref in enumerate(held):
                high = low + held_ref.shape[2]

                def add(j, total, i=i, held_ref=held_ref):
                    return total + held_ref[table_ref[i * blocks + j]].astype(F32)

                def add_extra(j, total, low=low, high=high):
                    return total + extra_ref[j, :, low:high].astype(F32)

                zero = jnp.zeros((rank, high - low), F32)
                total = lax.fori_loop(table_ref[at], table_ref[at + targets], add, zero)
                if has_extra:
                    total = lax.fori_loop(
                        table_ref[at + 2 * targets], table_ref[at + 3 * targets], add_extra, total
                    )
                out_ref[m, :, low:high] = total.astype(BF16)
                low = high
            return carry

        lax.fori_loop(0, out_ref.shape[0], step, 0)


def slot_sums(table, held, targets, hint, extra=None, outs=1, after=()):
    blocks, rank, _ = held[0].shape
    width = sum(x.shape[2] for x in held)
    operands = list(held) + ([] if extra is None else [extra])
    shape = jax.ShapeDtypeStruct((targets // outs, rank, width), BF16)
    return pl.pallas_call(
        functools.partial(sum_kernel, blocks, len(held), extra is not None, outs),
        out_shape=[shape] * outs,
        in_specs=[pl.BlockSpec(memory_space=pltpu.SMEM)]
        + [spec()] * len(operands)
        + [pl.BlockSpec(memory_space=pl.ANY)] * len(after),
        out_specs=[spec()] * outs,
        compiler_params=params(),
        cost_estimate=pl.CostEstimate(flops=hint, bytes_accessed=hint, transcendentals=0),
    )(table, *operands, *after)


def spread_kernel(width, place_ref, *refs):
    count = len(refs) - 3
    down_ref, up_ref, sems = refs[-3:]
    copies = []
    for k in range(count):
        spot = jnp.bitwise_xor(place_ref[0], k)
        up_width = refs[k].shape[2] - width
        copies.append(
            pltpu.make_async_copy(
                refs[k].at[:, :, :width],
                down_ref.at[:, :, pl.ds(pl.multiple_of(spot * width, 128), width)],
                sems.at[0, k],
            )
        )
        copies.append(
            pltpu.make_async_copy(
                refs[k].at[:, :, width:],
                up_ref.at[:, :, pl.ds(pl.multiple_of(spot * up_width, 128), up_width)],
                sems.at[1, k],
            )
        )
    for copy in copies:
        copy.start()
    for copy in copies:
        copy.wait()


def spread(place_in_half, got, width, model_width, out_width):
    slots, rank, whole = got[0].shape
    anywhere = pl.BlockSpec(memory_space=pl.ANY)
    return pl.pallas_call(
        functools.partial(spread_kernel, width),
        out_shape=[
            jax.ShapeDtypeStruct((slots, rank, model_width), BF16),
            jax.ShapeDtypeStruct((slots, rank, out_width), BF16),
        ],
        in_specs=[pl.BlockSpec(memory_space=pltpu.SMEM)] + [anywhere] * len(got),
        out_specs=[anywhere, anywhere],
        scratch_shapes=[pltpu.SemaphoreType.DMA((2, len(got)))],
        compiler_params=params(),
        cost_estimate=pl.CostEstimate(
            flops=0, bytes_accessed=4 * len(got) * slots * rank * whole, transcendentals=0
        ),
    )(place_in_half.reshape(1), *got)


def place_kernel(got_ref, *refs):
    refs[-1][...] = got_ref[0]


def place(got, width, columns, chunk, into=None):
    parts, slots, rank, _ = got.shape
    return pl.pallas_call(
        place_kernel,
        grid=(parts,),
        out_shape=jax.ShapeDtypeStruct((slots, rank, columns), BF16),
        in_specs=[pl.BlockSpec((1, slots, rank, width), lambda p: (p, 0, 0, 0))]
        + ([] if into is None else [pl.BlockSpec(memory_space=pl.ANY)]),
        out_specs=pl.BlockSpec((slots, rank, width), lambda p: (0, 0, chunk * parts + p)),
        input_output_aliases={} if into is None else {1: 0},
        compiler_params=params(),
        cost_estimate=pl.CostEstimate(
            flops=0, bytes_accessed=4 * parts * slots * rank * width, transcendentals=0
        ),
    )(*((got,) if into is None else (got, into)))


def body(copies, devices, acts, grad_out, low_acts, up_weight, block_adapter, block_fill, owner_slot):
    own_blocks = block_fill.shape[0]
    blocks, adapters = block_adapter.shape[0], owner_slot.shape[0]
    own_slots, rank, out_width = up_weight.shape
    model_width = acts.shape[1]
    half_devices = devices // 2
    half_blocks, half_slots = blocks // 2, adapters // 2
    groups = [list(range(half_devices)), list(range(half_devices, devices))]
    across = [(i, (i + half_devices) % devices) for i in range(devices)]
    half = lax.axis_index("dp") // half_devices

    def within(x):
        return lax.all_to_all(x, "dp", 0, 0, axis_index_groups=groups, tiled=True)

    def relative(x, k):
        return lax.ppermute(x, "dp", [(i, i ^ k) for i in range(devices)]) if k else x

    ids = jnp.arange(adapters, dtype=jnp.int32)
    slot_of = jnp.sum(
        jnp.where(block_adapter[:, None] == ids[None, :], owner_slot[None, :], 0), axis=1
    )

    place_in_half = lax.axis_index("dp") % half_devices
    by_permutes = half_devices <= 8 and out_width // half_devices % 128 == 0
    up_held = up_products(block_fill, low_acts.T, grad_out, half_devices)
    if by_permutes:
        up_pieces = [
            lax.dynamic_index_in_dim(up_held, place_in_half ^ k, 0, False)
            for k in range(half_devices)
        ]
        up_pieces = [relative(x, k) for k, x in enumerate(up_pieces)]
    else:
        up_pieces = [within(up_held).reshape(half_blocks, rank, -1)]

    lane_groups = min(devices // 4, out_width // 128)
    row_groups = devices // lane_groups
    rows, lanes = rank // row_groups, out_width // lane_groups
    pieces = up_weight.reshape(own_slots, row_groups, rows, lane_groups, lanes)
    pieces = pieces.transpose(1, 3, 0, 2, 4).reshape(devices, own_slots, rows, lanes)
    part = lax.all_to_all(pieces, "dp", 0, 0, tiled=True).reshape(adapters, rows, lanes)
    picked = pick(slot_of, part).reshape(devices, own_blocks, rows, lanes)
    weights = lax.all_to_all(picked, "dp", 0, 0, tiled=True)

    mine = lax.dynamic_slice_in_dim(slot_of, half * half_blocks, half_blocks)
    spots = jnp.arange(half_blocks, dtype=jnp.int32)
    before = (mine[None, :] < mine[:, None]) | (
        (mine[None, :] == mine[:, None]) & (spots[None, :] < spots[:, None])
    )
    spot_of = jnp.sum(before.astype(jnp.int32), axis=1)
    order = jnp.sum(jnp.where(spot_of[None, :] == spots[:, None], spots[None, :], 0), axis=1)
    start = jnp.sum((mine[None, :] < ids[:, None]).astype(jnp.int32), axis=1)
    count = jnp.sum((mine[None, :] == ids[:, None]).astype(jnp.int32), axis=1)
    by_half = slot_of.reshape(2, half_blocks)
    has = jnp.any(by_half[:, :, None] == ids[None, None, :], axis=1)
    crosses = has & ((ids[None, :] // half_slots) != jnp.arange(2, dtype=jnp.int32)[:, None])
    earlier = (ids[None, :] < ids[:, None])[None, :, :]
    place_of = jnp.sum((crosses[:, None, :] & earlier).astype(jnp.int32), axis=2)
    mine_needed = jnp.max(jnp.sum(crosses.astype(jnp.int32), axis=1)).reshape(1, 1)
    needed = mine_needed
    for k in range(1, copies):
        shift = [(i, (i + k) % copies) for i in range(copies)]
        needed = jnp.maximum(needed, lax.ppermute(mine_needed, "groups", shift))
    needed = needed[0, 0]

    my_cross = lax.dynamic_index_in_dim(crosses, half, 0, False)
    my_place = lax.dynamic_index_in_dim(place_of, half, 0, False)
    hot = my_cross[None, :] & (my_place[None, :] == spots[:, None])
    send_first = jnp.sum(jnp.where(hot, start[None, :], 0), axis=1)
    send_last = jnp.sum(jnp.where(hot, (start + count)[None, :], 0), axis=1)

    own = half * half_slots
    keep_first = lax.dynamic_slice_in_dim(start, own, half_slots)
    keep_last = keep_first + lax.dynamic_slice_in_dim(count, own, half_slots)
    got = lax.dynamic_index_in_dim(crosses, 1 - half, 0, False)
    got = lax.dynamic_slice_in_dim(got, own, half_slots).astype(jnp.int32)
    got_first = lax.dynamic_index_in_dim(place_of, 1 - half, 0, False)
    got_first = lax.dynamic_slice_in_dim(got_first, own, half_slots)
    keep_table = jnp.concatenate([order, keep_first, keep_last, got_first, got_first + got])

    if by_permutes:
        far = jnp.arange(half_devices, dtype=jnp.int32)
        hot = (far[:, None] ^ place_in_half) == far[None, :]
        keep = jnp.stack([keep_first, keep_last, got_first, got_first + got])
        keep = keep.reshape(4, 1, half_devices, own_slots)
        keep = jnp.sum(jnp.where(hot[None, :, :, None], keep, 0), axis=2).reshape(-1)
        source, spot = order // own_blocks, order % own_blocks
        up_order = (source ^ place_in_half) * own_blocks + spot
    else:
        keep, up_order = keep_table[half_blocks:], order
    orders = jnp.concatenate([order, up_order])
    keep_a_table = jnp.concatenate([orders, keep])

    low_t = rank_cotangent(block_fill, weights, grad_out, lane_groups, rank, up_pieces)
    up_held = jnp.concatenate(up_pieces)
    first = within(products(low_t, acts, half_devices, 0))
    first = first.reshape(half_blocks, rank, -1)
    second = products(low_t, acts, half_devices, 1)
    width = second.shape[3]

    def rest(
        capacity, first, up_held, second, orders, send_first, send_last, keep_a_table, keep_table
    ):
        ends = jnp.concatenate([send_first[:capacity], send_last[:capacity]])
        send_a_table = jnp.concatenate([orders, ends])
        send_b_table = jnp.concatenate([orders[:half_blocks], ends])
        second = within(second).reshape(half_blocks, rank, -1)
        both = [first, up_held]
        (sent_a,) = slot_sums(send_a_table, both, capacity, SMALL)
        came_a = lax.ppermute(sent_a, "dp", across)
        (sent_b,) = slot_sums(send_b_table, [second], capacity, SMALL)
        came_a, sent_b = lax.optimization_barrier((came_a, sent_b))
        came_b = lax.ppermute(sent_b, "dp", across)
        tied = ()
        if by_permutes:
            kept_a = slot_sums(keep_a_table, both, half_slots, SMALL, came_a, half_devices)
            done_a = [relative(x, k) for k, x in enumerate(kept_a)]
            tied = done_a[1:EARLY]
            down, up = spread(place_in_half, done_a, width, model_width, out_width)
        else:
            (kept_a,) = slot_sums(keep_a_table, both, half_slots, SMALL, came_a)
            done_a = within(kept_a.reshape(half_devices, own_slots, rank, -1))
            up = done_a[:, :, :, width:].transpose(1, 2, 0, 3).reshape(own_slots, rank, out_width)
            down = place(done_a, width, model_width, 0)
        (kept_b,) = slot_sums(keep_table, [second], half_slots, LARGE, came_b, 1, tied)
        done_b = within(kept_b.reshape(half_devices, own_slots, rank, -1))
        return place(done_b, width, model_width, 1, down), up

    limit = min(half_blocks, half_slots)
    capacities = sorted({-(-limit * k // 24) for k in (8, 9, 10, 11, 12, 14, 16, 24)})
    index = sum((needed > c).astype(jnp.int32) for c in capacities[:-1])
    return lax.switch(
        index,
        [functools.partial(rest, c) for c in capacities],
        first, up_held, second, orders, send_first, send_last, keep_a_table, keep_table,
    )


def solution(mesh):
    placed = (
        P(("groups", "dp"), None),
        P(("groups", "dp"), None),
        P(("groups", "dp"), None),
        P("dp", None, None),
        P("groups"),
        P(("groups", "dp")),
        P(),
    )
    return jax.shard_map(
        functools.partial(body, mesh.shape["groups"], mesh.shape["dp"]),
        mesh=mesh,
        in_specs=placed,
        out_specs=(P(("groups", "dp"), None, None), P(("groups", "dp"), None, None)),
        check_vma=False,
    )
```

```python
import functools

import jax
import jax.numpy as jnp
from jax import lax
from jax.experimental import pallas as pl
from jax.experimental.pallas import tpu as pltpu
from jax.sharding import PartitionSpec as P

BLOCK = 128
SCALE = 2.0
CHUNKS = 2
PARTS_A_STEP = 4
GROUPS = 8
BF16 = jnp.bfloat16
F32 = jnp.float32
VMEM_LIMIT = 48 * 1024 * 1024
SMALL, LARGE = 1 << 20, 1 << 38


def params():
    return pltpu.CompilerParams(vmem_limit_bytes=VMEM_LIMIT)


def spec():
    return pl.BlockSpec(memory_space=pltpu.VMEM)


def pick_kernel(slot_ref, parts_ref, out_ref):
    def step(b, carry):
        out_ref[b] = parts_ref[slot_ref[b]]
        return carry

    lax.fori_loop(0, out_ref.shape[0], step, 0)


def pick(slot_of, parts):
    blocks = slot_of.shape[0]
    return pl.pallas_call(
        pick_kernel,
        out_shape=jax.ShapeDtypeStruct((blocks,) + parts.shape[1:], BF16),
        in_specs=[pl.BlockSpec(memory_space=pltpu.SMEM), spec()],
        out_specs=spec(),
        compiler_params=params(),
    )(slot_of, parts)


def rank_kernel(lane_groups, fill_ref, parts_ref, grad_ref, *refs):
    out_ref, weight = refs[-2:]
    parts, blocks, rows, lanes = parts_ref.shape
    for b in range(blocks):
        for p in range(parts):
            g, l = p // lane_groups, p % lane_groups
            weight[b, g * rows : (g + 1) * rows, l * lanes : (l + 1) * lanes] = parts_ref[p, b]
    for b in range(blocks):
        turned = SCALE * lax.dot_general(
            weight[b],
            grad_ref[b * BLOCK : (b + 1) * BLOCK, :],
            (((1,), (1,)), ((), ())),
            preferred_element_type=F32,
        )
        live = lax.broadcasted_iota(jnp.int32, turned.shape, 1) < fill_ref[b]
        out_ref[b] = jnp.where(live, turned, 0.0).astype(BF16)


def rank_cotangent(fill, parts, grad, lane_groups, rank, after):
    blocks = fill.shape[0]
    return pl.pallas_call(
        functools.partial(rank_kernel, lane_groups),
        out_shape=jax.ShapeDtypeStruct((blocks, rank, BLOCK), BF16),
        in_specs=[pl.BlockSpec(memory_space=pltpu.SMEM), spec(), spec()]
        + [pl.BlockSpec(memory_space=pl.ANY)] * len(after),
        out_specs=spec(),
        scratch_shapes=[pltpu.VMEM((blocks, rank, grad.shape[1]), BF16)],
        compiler_params=params(),
    )(fill, parts, grad, *after)


def up_kernel(fill_ref, low_ref, grad_ref, out_ref):
    parts, blocks, rank, width = out_ref.shape
    for b in range(blocks):
        low = low_ref[:, b * BLOCK : (b + 1) * BLOCK].astype(F32)
        live = lax.broadcasted_iota(jnp.int32, low.shape, 1) < fill_ref[b]
        low = jnp.where(live, low, 0.0).astype(BF16)
        whole = SCALE * jnp.dot(
            low, grad_ref[b * BLOCK : (b + 1) * BLOCK, :], preferred_element_type=F32
        )
        for p in range(parts):
            out_ref[p, b] = whole[:, p * width : (p + 1) * width].astype(BF16)


def up_products(fill, low_t, grad, parts):
    blocks, rank = fill.shape[0], low_t.shape[0]
    return pl.pallas_call(
        up_kernel,
        out_shape=jax.ShapeDtypeStruct((parts, blocks, rank, grad.shape[1] // parts), BF16),
        in_specs=[pl.BlockSpec(memory_space=pltpu.SMEM), spec(), spec()],
        out_specs=spec(),
        compiler_params=params(),
    )(fill, low_t, grad)


def down_kernel(low_ref, acts_ref, out_ref):
    parts, blocks, _, width = out_ref.shape
    for p in range(parts):
        for b in range(blocks):
            out_ref[p, b] = jnp.dot(
                low_ref[b],
                acts_ref[b * BLOCK : (b + 1) * BLOCK, p * width : (p + 1) * width],
                preferred_element_type=F32,
            ).astype(BF16)


def products(low_t, acts, parts, chunk):
    blocks, rank, _ = low_t.shape
    rows, width = acts.shape[0], acts.shape[1] // (parts * CHUNKS)
    steps = max(parts // PARTS_A_STEP, 1)
    each = parts // steps
    return pl.pallas_call(
        down_kernel,
        grid=(steps,),
        out_shape=jax.ShapeDtypeStruct((parts, blocks, rank, width), BF16),
        in_specs=[
            pl.BlockSpec(low_t.shape, lambda p: (0, 0, 0)),
            pl.BlockSpec((rows, width * each), lambda p: (0, chunk * steps + p)),
        ],
        out_specs=pl.BlockSpec((each, blocks, rank, width), lambda p: (p, 0, 0, 0)),
        compiler_params=params(),
        cost_estimate=pl.CostEstimate(
            flops=2 * rows * rank * width * parts,
            bytes_accessed=2 * parts * width * (rows + blocks * rank),
            transcendentals=0,
        ),
    )(low_t, acts)


def sum_kernel(blocks, count, has_extra, outs, groups, table_ref, *refs):
    held = refs[:count]
    if groups:
        kept, sems = refs[-2:]
        refs = refs[:-2]
    dests = refs[-outs:]
    outs = dests
    if groups:
        size = kept.shape[0] // groups
        outs = [kept.at[pl.ds(n * size, size)] for n in range(groups)]
        if len(dests) == 1:
            dests = [dests[0].at[pl.ds(n * size, size)] for n in range(groups)]
    copies = []
    extra_ref = refs[count] if has_extra else None
    targets = sum(out.shape[0] for out in outs)
    rank = outs[0].shape[1]
    base = blocks * count

    for n, out_ref in enumerate(outs):
        shift = n * out_ref.shape[0]

        def step(m, carry, out_ref=out_ref, shift=shift):
            at = base + shift + m
            low = 0
            for i, held_ref in enumerate(held):
                high = low + held_ref.shape[2]

                def add(j, total, i=i, held_ref=held_ref):
                    return total + held_ref[table_ref[i * blocks + j]].astype(F32)

                def add_extra(j, total, low=low, high=high):
                    return total + extra_ref[j, :, low:high].astype(F32)

                zero = jnp.zeros((rank, high - low), F32)
                total = lax.fori_loop(table_ref[at], table_ref[at + targets], add, zero)
                if has_extra:
                    total = lax.fori_loop(
                        table_ref[at + 2 * targets], table_ref[at + 3 * targets], add_extra, total
                    )
                out_ref[m, :, low:high] = total.astype(BF16)
                low = high
            return carry

        lax.fori_loop(0, out_ref.shape[0], step, 0)
        if groups:
            copies.append(pltpu.make_async_copy(out_ref, dests[n], sems.at[n]))
            copies[-1].start()
    for copy in copies:
        copy.wait()


def slot_sums(table, held, targets, hint, extra=None, outs=1, after=(), groups=0):
    blocks, rank, _ = held[0].shape
    width = sum(x.shape[2] for x in held)
    operands = list(held) + ([] if extra is None else [extra])
    shape = jax.ShapeDtypeStruct((targets // outs, rank, width), BF16)
    return pl.pallas_call(
        functools.partial(sum_kernel, blocks, len(held), extra is not None, outs, groups),
        out_shape=[shape] * outs,
        in_specs=[pl.BlockSpec(memory_space=pltpu.SMEM)]
        + [spec()] * len(operands)
        + [pl.BlockSpec(memory_space=pl.ANY)] * len(after),
        out_specs=[pl.BlockSpec(memory_space=pltpu.HBM) if groups else spec()] * outs,
        scratch_shapes=[
            pltpu.VMEM((targets, rank, width), BF16),
            pltpu.SemaphoreType.DMA((groups,)),
        ]
        if groups
        else [],
        compiler_params=params(),
        cost_estimate=pl.CostEstimate(flops=hint, bytes_accessed=hint, transcendentals=0),
    )(table, *operands, *after)


def spread_kernel(width, place_ref, *refs):
    count = len(refs) - 3
    down_ref, up_ref, sems = refs[-3:]
    copies = []
    for k in range(count):
        spot = jnp.bitwise_xor(place_ref[0], k)
        up_width = refs[k].shape[2] - width
        copies.append(
            pltpu.make_async_copy(
                refs[k].at[:, :, :width],
                down_ref.at[:, :, pl.ds(pl.multiple_of(spot * width, 128), width)],
                sems.at[0, k],
            )
        )
        copies.append(
            pltpu.make_async_copy(
                refs[k].at[:, :, width:],
                up_ref.at[:, :, pl.ds(pl.multiple_of(spot * up_width, 128), up_width)],
                sems.at[1, k],
            )
        )
    for copy in copies:
        copy.start()
    for copy in copies:
        copy.wait()


def spread(place_in_half, got, width, model_width, out_width):
    slots, rank, whole = got[0].shape
    anywhere = pl.BlockSpec(memory_space=pl.ANY)
    return pl.pallas_call(
        functools.partial(spread_kernel, width),
        out_shape=[
            jax.ShapeDtypeStruct((slots, rank, model_width), BF16),
            jax.ShapeDtypeStruct((slots, rank, out_width), BF16),
        ],
        in_specs=[pl.BlockSpec(memory_space=pltpu.SMEM)] + [anywhere] * len(got),
        out_specs=[anywhere, anywhere],
        scratch_shapes=[pltpu.SemaphoreType.DMA((2, len(got)))],
        compiler_params=params(),
        cost_estimate=pl.CostEstimate(
            flops=0, bytes_accessed=4 * len(got) * slots * rank * whole, transcendentals=0
        ),
    )(place_in_half.reshape(1), *got)


def lay_kernel(first, got_ref, _, out_ref, sems):
    parts, _, _, width = got_ref.shape
    copies = [
        pltpu.make_async_copy(
            got_ref.at[p], out_ref.at[:, :, pl.ds((first + p) * width, width)], sems.at[p]
        )
        for p in range(parts)
    ]
    for copy in copies:
        copy.start()
    for copy in copies:
        copy.wait()


def lay(got, first, into):
    anywhere = pl.BlockSpec(memory_space=pl.ANY)
    return pl.pallas_call(
        functools.partial(lay_kernel, first),
        out_shape=jax.ShapeDtypeStruct(into.shape, BF16),
        in_specs=[anywhere, anywhere],
        out_specs=anywhere,
        input_output_aliases={1: 0},
        scratch_shapes=[pltpu.SemaphoreType.DMA((got.shape[0],))],
        compiler_params=params(),
        cost_estimate=pl.CostEstimate(flops=0, bytes_accessed=4 * got.size, transcendentals=0),
    )(got, into)


def place_kernel(got_ref, *refs):
    refs[-1][...] = got_ref[0]


def place(got, width, columns, chunk, into=None):
    parts, slots, rank, _ = got.shape
    return pl.pallas_call(
        place_kernel,
        grid=(parts,),
        out_shape=jax.ShapeDtypeStruct((slots, rank, columns), BF16),
        in_specs=[pl.BlockSpec((1, slots, rank, width), lambda p: (p, 0, 0, 0))]
        + ([] if into is None else [pl.BlockSpec(memory_space=pl.ANY)]),
        out_specs=pl.BlockSpec((slots, rank, width), lambda p: (0, 0, chunk * parts + p)),
        input_output_aliases={} if into is None else {1: 0},
        compiler_params=params(),
        cost_estimate=pl.CostEstimate(
            flops=0, bytes_accessed=4 * parts * slots * rank * width, transcendentals=0
        ),
    )(*((got,) if into is None else (got, into)))


def body(copies, devices, acts, grad_out, low_acts, up_weight, block_adapter, block_fill, owner_slot):
    own_blocks = block_fill.shape[0]
    blocks, adapters = block_adapter.shape[0], owner_slot.shape[0]
    own_slots, rank, out_width = up_weight.shape
    model_width = acts.shape[1]
    half_devices = devices // 2
    half_blocks, half_slots = blocks // 2, adapters // 2
    groups = [list(range(half_devices)), list(range(half_devices, devices))]
    across = [(i, (i + half_devices) % devices) for i in range(devices)]
    half = lax.axis_index("dp") // half_devices

    def within(x):
        return lax.all_to_all(x, "dp", 0, 0, axis_index_groups=groups, tiled=True)

    def relative(x, k):
        return lax.ppermute(x, "dp", [(i, i ^ k) for i in range(devices)]) if k else x

    ids = jnp.arange(adapters, dtype=jnp.int32)
    slot_of = jnp.sum(
        jnp.where(block_adapter[:, None] == ids[None, :], owner_slot[None, :], 0), axis=1
    )

    place_in_half = lax.axis_index("dp") % half_devices
    by_permutes = half_devices <= 8 and out_width // half_devices % 128 == 0
    up_held = up_products(block_fill, low_acts.T, grad_out, half_devices)
    if by_permutes:
        up_pieces = [
            lax.dynamic_index_in_dim(up_held, place_in_half ^ k, 0, False)
            for k in range(half_devices)
        ]
        up_pieces = [relative(x, k) for k, x in enumerate(up_pieces)]
    else:
        up_pieces = [within(up_held).reshape(half_blocks, rank, -1)]

    lane_groups = min(devices // 4, out_width // 128)
    row_groups = devices // lane_groups
    rows, lanes = rank // row_groups, out_width // lane_groups
    pieces = up_weight.reshape(own_slots, row_groups, rows, lane_groups, lanes)
    pieces = pieces.transpose(1, 3, 0, 2, 4).reshape(devices, own_slots, rows, lanes)
    part = lax.all_to_all(pieces, "dp", 0, 0, tiled=True).reshape(adapters, rows, lanes)
    picked = pick(slot_of, part).reshape(devices, own_blocks, rows, lanes)
    weights = lax.all_to_all(picked, "dp", 0, 0, tiled=True)

    mine = lax.dynamic_slice_in_dim(slot_of, half * half_blocks, half_blocks)
    spots = jnp.arange(half_blocks, dtype=jnp.int32)
    before = (mine[None, :] < mine[:, None]) | (
        (mine[None, :] == mine[:, None]) & (spots[None, :] < spots[:, None])
    )
    spot_of = jnp.sum(before.astype(jnp.int32), axis=1)
    order = jnp.sum(jnp.where(spot_of[None, :] == spots[:, None], spots[None, :], 0), axis=1)
    start = jnp.sum((mine[None, :] < ids[:, None]).astype(jnp.int32), axis=1)
    count = jnp.sum((mine[None, :] == ids[:, None]).astype(jnp.int32), axis=1)
    by_half = slot_of.reshape(2, half_blocks)
    has = jnp.any(by_half[:, :, None] == ids[None, None, :], axis=1)
    crosses = has & ((ids[None, :] // half_slots) != jnp.arange(2, dtype=jnp.int32)[:, None])
    earlier = (ids[None, :] < ids[:, None])[None, :, :]
    place_of = jnp.sum((crosses[:, None, :] & earlier).astype(jnp.int32), axis=2)
    mine_needed = jnp.max(jnp.sum(crosses.astype(jnp.int32), axis=1)).reshape(1, 1)
    needed = mine_needed
    for k in range(1, copies):
        shift = [(i, (i + k) % copies) for i in range(copies)]
        needed = jnp.maximum(needed, lax.ppermute(mine_needed, "groups", shift))
    needed = needed[0, 0]

    my_cross = lax.dynamic_index_in_dim(crosses, half, 0, False)
    my_place = lax.dynamic_index_in_dim(place_of, half, 0, False)
    hot = my_cross[None, :] & (my_place[None, :] == spots[:, None])
    send_first = jnp.sum(jnp.where(hot, start[None, :], 0), axis=1)
    send_last = jnp.sum(jnp.where(hot, (start + count)[None, :], 0), axis=1)

    own = half * half_slots
    keep_first = lax.dynamic_slice_in_dim(start, own, half_slots)
    keep_last = keep_first + lax.dynamic_slice_in_dim(count, own, half_slots)
    got = lax.dynamic_index_in_dim(crosses, 1 - half, 0, False)
    got = lax.dynamic_slice_in_dim(got, own, half_slots).astype(jnp.int32)
    got_first = lax.dynamic_index_in_dim(place_of, 1 - half, 0, False)
    got_first = lax.dynamic_slice_in_dim(got_first, own, half_slots)
    keep_table = jnp.concatenate([order, keep_first, keep_last, got_first, got_first + got])

    if by_permutes:
        far = jnp.arange(half_devices, dtype=jnp.int32)
        hot = (far[:, None] ^ place_in_half) == far[None, :]
        keep = jnp.stack([keep_first, keep_last, got_first, got_first + got])
        keep = keep.reshape(4, 1, half_devices, own_slots)
        keep = jnp.sum(jnp.where(hot[None, :, :, None], keep, 0), axis=2).reshape(-1)
        source, spot = order // own_blocks, order % own_blocks
        up_order = (source ^ place_in_half) * own_blocks + spot
    else:
        keep, up_order = keep_table[half_blocks:], order
    orders = jnp.concatenate([order, up_order])
    keep_a_table = jnp.concatenate([orders, keep])

    low_t = rank_cotangent(block_fill, weights, grad_out, lane_groups, rank, up_pieces)
    up_held = jnp.concatenate(up_pieces)
    first = within(products(low_t, acts, half_devices, 0))
    first = first.reshape(half_blocks, rank, -1)
    second = products(low_t, acts, half_devices, 1)
    width = second.shape[3]

    def rest(
        capacity, first, up_held, second, orders, send_first, send_last, keep_a_table, keep_table
    ):
        ends = jnp.concatenate([send_first[:capacity], send_last[:capacity]])
        send_a_table = jnp.concatenate([orders, ends])
        send_b_table = jnp.concatenate([orders[:half_blocks], ends])
        second = within(second).reshape(half_blocks, rank, -1)
        both = [first, up_held]
        (sent_a,) = slot_sums(send_a_table, both, capacity, SMALL)
        came_a = lax.ppermute(sent_a, "dp", across)
        (sent_b,) = slot_sums(send_b_table, [second], capacity, SMALL)
        came_a, sent_b = lax.optimization_barrier((came_a, sent_b))
        came_b = lax.ppermute(sent_b, "dp", across)
        tied = ()
        if by_permutes:
            kept_a = slot_sums(
                keep_a_table, both, half_slots, SMALL, came_a, half_devices, (), half_devices
            )
            done_a = [relative(x, k) for k, x in enumerate(kept_a)]
            tied = done_a[half_devices // 2 : half_devices - 1]
            down, up = spread(place_in_half, done_a, width, model_width, out_width)
        else:
            (kept_a,) = slot_sums(keep_a_table, both, half_slots, SMALL, came_a)
            done_a = within(kept_a.reshape(half_devices, own_slots, rank, -1))
            up = done_a[:, :, :, width:].transpose(1, 2, 0, 3).reshape(own_slots, rank, out_width)
            down = place(done_a, width, model_width, 0)
        (kept_b,) = slot_sums(keep_table, [second], half_slots, LARGE, came_b, 1, tied, GROUPS)
        done_b = within(kept_b.reshape(half_devices, own_slots, rank, -1))
        return lay(done_b, half_devices, down), up

    limit = min(half_blocks, half_slots)
    capacities = sorted({-(-limit * k // 24) for k in (8, 9, 10, 11, 12, 14, 16, 24)})
    index = sum((needed > c).astype(jnp.int32) for c in capacities[:-1])
    return lax.switch(
        index,
        [functools.partial(rest, c) for c in capacities],
        first, up_held, second, orders, send_first, send_last, keep_a_table, keep_table,
    )


def solution(mesh):
    placed = (
        P(("groups", "dp"), None),
        P(("groups", "dp"), None),
        P(("groups", "dp"), None),
        P("dp", None, None),
        P("groups"),
        P(("groups", "dp")),
        P(),
    )
    return jax.shard_map(
        functools.partial(body, mesh.shape["groups"], mesh.shape["dp"]),
        mesh=mesh,
        in_specs=placed,
        out_specs=(P(("groups", "dp"), None, None), P(("groups", "dp"), None, None)),
        check_vma=False,
    )
```

```python
import functools

import jax
import jax.numpy as jnp
from jax import lax
from jax.experimental import pallas as pl
from jax.experimental.pallas import tpu as pltpu
from jax.sharding import PartitionSpec as P

BLOCK = 128
SCALE = 2.0
CHUNKS = 2
PARTS_A_STEP = 4
GROUPS = 8
BF16 = jnp.bfloat16
F32 = jnp.float32
VMEM_LIMIT = 48 * 1024 * 1024
SMALL, LARGE = 1 << 20, 1 << 38


def params():
    return pltpu.CompilerParams(vmem_limit_bytes=VMEM_LIMIT)


def spec():
    return pl.BlockSpec(memory_space=pltpu.VMEM)


def pick_kernel(slot_ref, parts_ref, out_ref):
    def step(b, carry):
        out_ref[b] = parts_ref[slot_ref[b]]
        return carry

    lax.fori_loop(0, out_ref.shape[0], step, 0)


def pick(slot_of, parts):
    blocks = slot_of.shape[0]
    return pl.pallas_call(
        pick_kernel,
        out_shape=jax.ShapeDtypeStruct((blocks,) + parts.shape[1:], BF16),
        in_specs=[pl.BlockSpec(memory_space=pltpu.SMEM), spec()],
        out_specs=spec(),
        compiler_params=params(),
    )(slot_of, parts)


def rank_kernel(lane_groups, fill_ref, parts_ref, grad_ref, *refs):
    out_ref, weight = refs[-2:]
    parts, blocks, rows, lanes = parts_ref.shape
    for b in range(blocks):
        for p in range(parts):
            g, l = p // lane_groups, p % lane_groups
            weight[b, g * rows : (g + 1) * rows, l * lanes : (l + 1) * lanes] = parts_ref[p, b]
    for b in range(blocks):
        turned = SCALE * lax.dot_general(
            weight[b],
            grad_ref[b * BLOCK : (b + 1) * BLOCK, :],
            (((1,), (1,)), ((), ())),
            preferred_element_type=F32,
        )
        live = lax.broadcasted_iota(jnp.int32, turned.shape, 1) < fill_ref[b]
        out_ref[b] = jnp.where(live, turned, 0.0).astype(BF16)


def rank_cotangent(fill, parts, grad, lane_groups, rank, after):
    blocks = fill.shape[0]
    return pl.pallas_call(
        functools.partial(rank_kernel, lane_groups),
        out_shape=jax.ShapeDtypeStruct((blocks, rank, BLOCK), BF16),
        in_specs=[pl.BlockSpec(memory_space=pltpu.SMEM), spec(), spec()]
        + [pl.BlockSpec(memory_space=pl.ANY)] * len(after),
        out_specs=spec(),
        scratch_shapes=[pltpu.VMEM((blocks, rank, grad.shape[1]), BF16)],
        compiler_params=params(),
    )(fill, parts, grad, *after)


def up_kernel(fill_ref, low_ref, grad_ref, out_ref):
    parts, blocks, rank, width = out_ref.shape
    for b in range(blocks):
        low = low_ref[:, b * BLOCK : (b + 1) * BLOCK].astype(F32)
        live = lax.broadcasted_iota(jnp.int32, low.shape, 1) < fill_ref[b]
        low = jnp.where(live, low, 0.0).astype(BF16)
        whole = SCALE * jnp.dot(
            low, grad_ref[b * BLOCK : (b + 1) * BLOCK, :], preferred_element_type=F32
        )
        for p in range(parts):
            out_ref[p, b] = whole[:, p * width : (p + 1) * width].astype(BF16)


def up_products(fill, low_t, grad, parts):
    blocks, rank = fill.shape[0], low_t.shape[0]
    return pl.pallas_call(
        up_kernel,
        out_shape=jax.ShapeDtypeStruct((parts, blocks, rank, grad.shape[1] // parts), BF16),
        in_specs=[pl.BlockSpec(memory_space=pltpu.SMEM), spec(), spec()],
        out_specs=spec(),
        compiler_params=params(),
    )(fill, low_t, grad)


def down_kernel(low_ref, acts_ref, out_ref):
    parts, blocks, _, width = out_ref.shape
    for p in range(parts):
        for b in range(blocks):
            out_ref[p, b] = jnp.dot(
                low_ref[b],
                acts_ref[b * BLOCK : (b + 1) * BLOCK, p * width : (p + 1) * width],
                preferred_element_type=F32,
            ).astype(BF16)


def products(low_t, acts, parts, chunk):
    blocks, rank, _ = low_t.shape
    rows, width = acts.shape[0], acts.shape[1] // (parts * CHUNKS)
    steps = max(parts // PARTS_A_STEP, 1)
    each = parts // steps
    return pl.pallas_call(
        down_kernel,
        grid=(steps,),
        out_shape=jax.ShapeDtypeStruct((parts, blocks, rank, width), BF16),
        in_specs=[
            pl.BlockSpec(low_t.shape, lambda p: (0, 0, 0)),
            pl.BlockSpec((rows, width * each), lambda p: (0, chunk * steps + p)),
        ],
        out_specs=pl.BlockSpec((each, blocks, rank, width), lambda p: (p, 0, 0, 0)),
        compiler_params=params(),
        cost_estimate=pl.CostEstimate(
            flops=2 * rows * rank * width * parts,
            bytes_accessed=2 * parts * width * (rows + blocks * rank),
            transcendentals=0,
        ),
    )(low_t, acts)


def sum_kernel(blocks, count, has_extra, outs, groups, table_ref, *refs):
    held = refs[:count]
    if groups:
        kept, sems = refs[-2:]
        refs = refs[:-2]
    dests = refs[-outs:]
    outs = dests
    if groups:
        size = kept.shape[0] // groups
        outs = [kept.at[pl.ds(n * size, size)] for n in range(groups)]
        if len(dests) == 1:
            dests = [dests[0].at[pl.ds(n * size, size)] for n in range(groups)]
    copies = []
    extra_ref = refs[count] if has_extra else None
    targets = sum(out.shape[0] for out in outs)
    rank = outs[0].shape[1]
    base = blocks * count

    for n, out_ref in enumerate(outs):
        shift = n * out_ref.shape[0]

        def step(m, carry, out_ref=out_ref, shift=shift):
            at = base + shift + m
            low = 0
            for i, held_ref in enumerate(held):
                high = low + held_ref.shape[2]

                def add(j, total, i=i, held_ref=held_ref):
                    return total + held_ref[table_ref[i * blocks + j]].astype(F32)

                def add_extra(j, total, low=low, high=high):
                    return total + extra_ref[j, :, low:high].astype(F32)

                zero = jnp.zeros((rank, high - low), F32)
                total = lax.fori_loop(table_ref[at], table_ref[at + targets], add, zero)
                if has_extra:
                    total = lax.fori_loop(
                        table_ref[at + 2 * targets], table_ref[at + 3 * targets], add_extra, total
                    )
                out_ref[m, :, low:high] = total.astype(BF16)
                low = high
            return carry

        lax.fori_loop(0, out_ref.shape[0], step, 0)
        if groups:
            copies.append(pltpu.make_async_copy(out_ref, dests[n], sems.at[n]))
            copies[-1].start()
    for copy in copies:
        copy.wait()


def slot_sums(table, held, targets, hint, extra=None, outs=1, after=(), groups=0):
    blocks, rank, _ = held[0].shape
    width = sum(x.shape[2] for x in held)
    operands = list(held) + ([] if extra is None else [extra])
    shape = jax.ShapeDtypeStruct((targets // outs, rank, width), BF16)
    return pl.pallas_call(
        functools.partial(sum_kernel, blocks, len(held), extra is not None, outs, groups),
        out_shape=[shape] * outs,
        in_specs=[pl.BlockSpec(memory_space=pltpu.SMEM)]
        + [spec()] * len(operands)
        + [pl.BlockSpec(memory_space=pl.ANY)] * len(after),
        out_specs=[pl.BlockSpec(memory_space=pltpu.HBM) if groups else spec()] * outs,
        scratch_shapes=[
            pltpu.VMEM((targets, rank, width), BF16),
            pltpu.SemaphoreType.DMA((groups,)),
        ]
        if groups
        else [],
        compiler_params=params(),
        cost_estimate=pl.CostEstimate(flops=hint, bytes_accessed=hint, transcendentals=0),
    )(table, *operands, *after)


def copy_slots(got, out, columns, zero, landing_ref, sem, waits):
    slots, (_, low, high) = out.shape[0], columns
    if got.shape[0] == slots:
        copy = pltpu.make_async_copy(got.at[:, :, low:high], out.at[:, :, columns[0]], sem.at[0])
        copy.start()
        waits.append(copy)
        return
    for n in range(slots):
        to = out.at[n, :, columns[0]]
        none = pltpu.make_async_copy(zero.at[:, : high - low], to, sem.at[n])

        @pl.when(landing_ref[1 + n] >= 0)
        def _(n=n, to=to):
            spot = jnp.maximum(landing_ref[1 + n], 0)
            pltpu.make_async_copy(got.at[spot, :, low:high], to, sem.at[n]).start()

        @pl.when(landing_ref[1 + n] < 0)
        def _(none=none):
            none.start()

        waits.append(none)


def spread_kernel(width, landing_ref, *refs):
    count = len(refs) - 4
    down_ref, up_ref, zero, sems = refs[-4:]
    zero[...] = jnp.zeros_like(zero)
    waits = []
    for k in range(count):
        spot = jnp.bitwise_xor(landing_ref[0], k)
        whole = refs[k].shape[2]
        up_width = whole - width
        down_at = pl.ds(pl.multiple_of(spot * width, 128), width)
        up_at = pl.ds(pl.multiple_of(spot * up_width, 128), up_width)
        copy_slots(refs[k], down_ref, (down_at, 0, width), zero, landing_ref, sems.at[0, k], waits)
        copy_slots(refs[k], up_ref, (up_at, width, whole), zero, landing_ref, sems.at[1, k], waits)
    for wait in waits:
        wait.wait()


def spread(landing, got, slots, width, model_width, out_width):
    _, rank, whole = got[0].shape
    anywhere = pl.BlockSpec(memory_space=pl.ANY)
    return pl.pallas_call(
        functools.partial(spread_kernel, width),
        out_shape=[
            jax.ShapeDtypeStruct((slots, rank, model_width), BF16),
            jax.ShapeDtypeStruct((slots, rank, out_width), BF16),
        ],
        in_specs=[pl.BlockSpec(memory_space=pltpu.SMEM)] + [anywhere] * len(got),
        out_specs=[anywhere, anywhere],
        scratch_shapes=[
            pltpu.VMEM((rank, width), BF16),
            pltpu.SemaphoreType.DMA((2, len(got), slots)),
        ],
        compiler_params=params(),
        cost_estimate=pl.CostEstimate(
            flops=0, bytes_accessed=4 * len(got) * slots * rank * whole, transcendentals=0
        ),
    )(landing, *got)


def lay_kernel(first, landing_ref, got_ref, _, out_ref, zero, sems):
    parts, _, _, width = got_ref.shape
    zero[...] = jnp.zeros_like(zero)
    waits = []
    for p in range(parts):
        at = pl.ds((first + p) * width, width)
        copy_slots(got_ref.at[p], out_ref, (at, 0, width), zero, landing_ref, sems.at[p], waits)
    for wait in waits:
        wait.wait()


def lay(landing, got, first, into):
    parts, _, rank, width = got.shape
    anywhere = pl.BlockSpec(memory_space=pl.ANY)
    return pl.pallas_call(
        functools.partial(lay_kernel, first),
        out_shape=jax.ShapeDtypeStruct(into.shape, BF16),
        in_specs=[pl.BlockSpec(memory_space=pltpu.SMEM), anywhere, anywhere],
        out_specs=anywhere,
        input_output_aliases={2: 0},
        scratch_shapes=[
            pltpu.VMEM((rank, width), BF16),
            pltpu.SemaphoreType.DMA((parts, into.shape[0])),
        ],
        compiler_params=params(),
        cost_estimate=pl.CostEstimate(flops=0, bytes_accessed=4 * got.size, transcendentals=0),
    )(landing, got, into)


def place_kernel(got_ref, *refs):
    refs[-1][...] = got_ref[0]


def place(got, width, columns, chunk, into=None):
    parts, slots, rank, _ = got.shape
    return pl.pallas_call(
        place_kernel,
        grid=(parts,),
        out_shape=jax.ShapeDtypeStruct((slots, rank, columns), BF16),
        in_specs=[pl.BlockSpec((1, slots, rank, width), lambda p: (p, 0, 0, 0))]
        + ([] if into is None else [pl.BlockSpec(memory_space=pl.ANY)]),
        out_specs=pl.BlockSpec((slots, rank, width), lambda p: (0, 0, chunk * parts + p)),
        input_output_aliases={} if into is None else {1: 0},
        compiler_params=params(),
        cost_estimate=pl.CostEstimate(
            flops=0, bytes_accessed=4 * parts * slots * rank * width, transcendentals=0
        ),
    )(*((got,) if into is None else (got, into)))


def body(copies, devices, acts, grad_out, low_acts, up_weight, block_adapter, block_fill, owner_slot):
    own_blocks = block_fill.shape[0]
    blocks, adapters = block_adapter.shape[0], owner_slot.shape[0]
    own_slots, rank, out_width = up_weight.shape
    model_width = acts.shape[1]
    half_devices = devices // 2
    half_blocks, half_slots = blocks // 2, adapters // 2
    groups = [list(range(half_devices)), list(range(half_devices, devices))]
    across = [(i, (i + half_devices) % devices) for i in range(devices)]
    half = lax.axis_index("dp") // half_devices

    def within(x):
        return lax.all_to_all(x, "dp", 0, 0, axis_index_groups=groups, tiled=True)

    def relative(x, k):
        return lax.ppermute(x, "dp", [(i, i ^ k) for i in range(devices)]) if k else x

    ids = jnp.arange(adapters, dtype=jnp.int32)
    slot_of = jnp.sum(
        jnp.where(block_adapter[:, None] == ids[None, :], owner_slot[None, :], 0), axis=1
    )

    place_in_half = lax.axis_index("dp") % half_devices
    by_permutes = half_devices <= 8 and out_width // half_devices % 128 == 0
    up_held = up_products(block_fill, low_acts.T, grad_out, half_devices)
    if by_permutes:
        up_pieces = [
            lax.dynamic_index_in_dim(up_held, place_in_half ^ k, 0, False)
            for k in range(half_devices)
        ]
        up_pieces = [relative(x, k) for k, x in enumerate(up_pieces)]
    else:
        up_pieces = [within(up_held).reshape(half_blocks, rank, -1)]

    lane_groups = min(devices // 4, out_width // 128)
    row_groups = devices // lane_groups
    rows, lanes = rank // row_groups, out_width // lane_groups
    pieces = up_weight.reshape(own_slots, row_groups, rows, lane_groups, lanes)
    pieces = pieces.transpose(1, 3, 0, 2, 4).reshape(devices, own_slots, rows, lanes)
    part = lax.all_to_all(pieces, "dp", 0, 0, tiled=True).reshape(adapters, rows, lanes)
    picked = pick(slot_of, part).reshape(devices, own_blocks, rows, lanes)
    weights = lax.all_to_all(picked, "dp", 0, 0, tiled=True)

    mine = lax.dynamic_slice_in_dim(slot_of, half * half_blocks, half_blocks)
    spots = jnp.arange(half_blocks, dtype=jnp.int32)
    before = (mine[None, :] < mine[:, None]) | (
        (mine[None, :] == mine[:, None]) & (spots[None, :] < spots[:, None])
    )
    spot_of = jnp.sum(before.astype(jnp.int32), axis=1)
    order = jnp.sum(jnp.where(spot_of[None, :] == spots[:, None], spots[None, :], 0), axis=1)
    start = jnp.sum((mine[None, :] < ids[:, None]).astype(jnp.int32), axis=1)
    count = jnp.sum((mine[None, :] == ids[:, None]).astype(jnp.int32), axis=1)
    by_half = slot_of.reshape(2, half_blocks)
    has = jnp.any(by_half[:, :, None] == ids[None, None, :], axis=1)
    crosses = has & ((ids[None, :] // half_slots) != jnp.arange(2, dtype=jnp.int32)[:, None])
    earlier = (ids[None, :] < ids[:, None])[None, :, :]
    place_of = jnp.sum((crosses[:, None, :] & earlier).astype(jnp.int32), axis=2)
    used = jnp.any(has, axis=0).reshape(-1, own_slots)
    slot_ids = jnp.arange(own_slots, dtype=jnp.int32)
    rank_of = jnp.sum(
        (used[:, None, :] & (slot_ids[None, :] < slot_ids[:, None])[None]).astype(jnp.int32), axis=2
    )
    mine_needed = jnp.stack(
        [
            jnp.max(jnp.sum(crosses.astype(jnp.int32), axis=1)),
            jnp.max(jnp.sum(used.astype(jnp.int32), axis=1)),
        ]
    ).reshape(1, 2)
    needed = mine_needed
    for k in range(1, copies):
        shift = [(i, (i + k) % copies) for i in range(copies)]
        needed = jnp.maximum(needed, lax.ppermute(mine_needed, "groups", shift))
    needed, most = needed[0, 0], needed[0, 1]

    my_cross = lax.dynamic_index_in_dim(crosses, half, 0, False)
    my_place = lax.dynamic_index_in_dim(place_of, half, 0, False)
    hot = my_cross[None, :] & (my_place[None, :] == spots[:, None])
    send_first = jnp.sum(jnp.where(hot, start[None, :], 0), axis=1)
    send_last = jnp.sum(jnp.where(hot, (start + count)[None, :], 0), axis=1)

    own = half * half_slots
    keep_first = lax.dynamic_slice_in_dim(start, own, half_slots)
    keep_last = keep_first + lax.dynamic_slice_in_dim(count, own, half_slots)
    got = lax.dynamic_index_in_dim(crosses, 1 - half, 0, False)
    got = lax.dynamic_slice_in_dim(got, own, half_slots).astype(jnp.int32)
    got_first = lax.dynamic_index_in_dim(place_of, 1 - half, 0, False)
    got_first = lax.dynamic_slice_in_dim(got_first, own, half_slots)
    keep_table = jnp.concatenate([order, keep_first, keep_last, got_first, got_first + got])

    packed, packed_far, landing = keep_table, keep_table, keep_table
    if by_permutes:
        keep = jnp.stack([keep_first, keep_last, got_first, got_first + got])
        keep = keep.reshape(4, half_devices, 1, own_slots)
        half_used = lax.dynamic_slice_in_dim(used, half * half_devices, half_devices)
        half_rank = lax.dynamic_slice_in_dim(rank_of, half * half_devices, half_devices)
        chosen = half_used[:, None, :] & (half_rank[:, None, :] == slot_ids[None, :, None])
        packed = jnp.sum(jnp.where(chosen[None], keep, 0), axis=3)
        far = jnp.arange(half_devices, dtype=jnp.int32)
        hot = (far[:, None] ^ place_in_half) == far[None, :]
        packed_far = jnp.sum(
            jnp.where(hot[None, :, :, None], packed[:, None], 0), axis=2
        )
        mine_at = lax.axis_index("dp")
        landing = jnp.where(
            lax.dynamic_index_in_dim(used, mine_at, 0, False),
            lax.dynamic_index_in_dim(rank_of, mine_at, 0, False),
            -1,
        )
        landing = jnp.concatenate([place_in_half.reshape(1), landing])
        far = jnp.arange(half_devices, dtype=jnp.int32)
        hot = (far[:, None] ^ place_in_half) == far[None, :]
        keep = jnp.stack([keep_first, keep_last, got_first, got_first + got])
        keep = keep.reshape(4, 1, half_devices, own_slots)
        keep = jnp.sum(jnp.where(hot[None, :, :, None], keep, 0), axis=2).reshape(-1)
        source, spot = order // own_blocks, order % own_blocks
        up_order = (source ^ place_in_half) * own_blocks + spot
    else:
        keep, up_order = keep_table[half_blocks:], order
    orders = jnp.concatenate([order, up_order])
    keep_a_table = jnp.concatenate([orders, keep])

    low_t = rank_cotangent(block_fill, weights, grad_out, lane_groups, rank, up_pieces)
    up_held = jnp.concatenate(up_pieces)
    first = within(products(low_t, acts, half_devices, 0))
    first = first.reshape(half_blocks, rank, -1)
    second = products(low_t, acts, half_devices, 1)
    width = second.shape[3]

    def rest(
        capacity, slots, first, up_held, second, orders, send_first, send_last, keep_a_table,
        keep_table, packed, packed_far, landing
    ):
        if slots < own_slots:
            keep_a_table = jnp.concatenate([orders, packed_far[:, :, :slots].reshape(-1)])
            keep_table = jnp.concatenate([orders[:half_blocks], packed[:, :, :slots].reshape(-1)])
        targets = half_devices * slots
        ends = jnp.concatenate([send_first[:capacity], send_last[:capacity]])
        send_a_table = jnp.concatenate([orders, ends])
        send_b_table = jnp.concatenate([orders[:half_blocks], ends])
        second = within(second).reshape(half_blocks, rank, -1)
        both = [first, up_held]
        (sent_a,) = slot_sums(send_a_table, both, capacity, SMALL)
        came_a = lax.ppermute(sent_a, "dp", across)
        (sent_b,) = slot_sums(send_b_table, [second], capacity, SMALL)
        came_a, sent_b = lax.optimization_barrier((came_a, sent_b))
        came_b = lax.ppermute(sent_b, "dp", across)
        tied = ()
        if by_permutes:
            kept_a = slot_sums(
                keep_a_table, both, targets, SMALL, came_a, half_devices, (), half_devices
            )
            done_a = [relative(x, k) for k, x in enumerate(kept_a)]
            tied = [done_a[k] for k in (2, 3, 6, 7)]
            down, up = spread(
                landing, done_a, own_slots, width, model_width, out_width
            )
        else:
            (kept_a,) = slot_sums(keep_a_table, both, half_slots, SMALL, came_a)
            done_a = within(kept_a.reshape(half_devices, own_slots, rank, -1))
            up = done_a[:, :, :, width:].transpose(1, 2, 0, 3).reshape(own_slots, rank, out_width)
            down = place(done_a, width, model_width, 0)
        (kept_b,) = slot_sums(keep_table, [second], targets, LARGE, came_b, 1, tied, GROUPS)
        done_b = within(kept_b.reshape(half_devices, slots, rank, -1))
        if by_permutes:
            return lay(landing, done_b, half_devices, down), up
        return place(done_b, width, model_width, 1, down), up

    limit = min(half_blocks, half_slots)
    capacities = sorted({-(-limit * k // 24) for k in (8, 9, 10, 11, 12, 13, 15, 24)})
    index = sum((needed > c).astype(jnp.int32) for c in capacities[:-1])
    sizes = [own_slots]
    if by_permutes and own_slots > 1:
        sizes = [own_slots - 1, own_slots]
        index = 2 * index + (most >= own_slots).astype(jnp.int32)
    return lax.switch(
        index,
        [functools.partial(rest, c, n) for c in capacities for n in sizes],
        first, up_held, second, orders, send_first, send_last, keep_a_table, keep_table,
        packed, packed_far, landing,
    )


def solution(mesh):
    placed = (
        P(("groups", "dp"), None),
        P(("groups", "dp"), None),
        P(("groups", "dp"), None),
        P("dp", None, None),
        P("groups"),
        P(("groups", "dp")),
        P(),
    )
    return jax.shard_map(
        functools.partial(body, mesh.shape["groups"], mesh.shape["dp"]),
        mesh=mesh,
        in_specs=placed,
        out_specs=(P(("groups", "dp"), None, None), P(("groups", "dp"), None, None)),
        check_vma=False,
    )
```

```python
import functools

import jax
import jax.numpy as jnp
from jax import lax
from jax.experimental import pallas as pl
from jax.experimental.pallas import tpu as pltpu
from jax.sharding import PartitionSpec as P

BLOCK = 128
SCALE = 2.0
CHUNKS = 2
PARTS_A_STEP = 4
GROUPS = 8
BF16 = jnp.bfloat16
F32 = jnp.float32
VMEM_LIMIT = 48 * 1024 * 1024
SMALL, LARGE = 1 << 20, 1 << 38


def params():
    return pltpu.CompilerParams(vmem_limit_bytes=VMEM_LIMIT)


def spec():
    return pl.BlockSpec(memory_space=pltpu.VMEM)


def pick_kernel(slot_ref, parts_ref, out_ref):
    def step(b, carry):
        out_ref[b] = parts_ref[slot_ref[b]]
        return carry

    lax.fori_loop(0, out_ref.shape[0], step, 0)


def pick(slot_of, parts):
    blocks = slot_of.shape[0]
    return pl.pallas_call(
        pick_kernel,
        out_shape=jax.ShapeDtypeStruct((blocks,) + parts.shape[1:], BF16),
        in_specs=[pl.BlockSpec(memory_space=pltpu.SMEM), spec()],
        out_specs=spec(),
        compiler_params=params(),
    )(slot_of, parts)


def rank_kernel(lane_groups, fill_ref, parts_ref, grad_ref, *refs):
    out_ref, weight = refs[-2:]
    parts, blocks, rows, lanes = parts_ref.shape
    for b in range(blocks):
        for p in range(parts):
            g, l = p // lane_groups, p % lane_groups
            weight[b, g * rows : (g + 1) * rows, l * lanes : (l + 1) * lanes] = parts_ref[p, b]
    for b in range(blocks):
        turned = SCALE * lax.dot_general(
            weight[b],
            grad_ref[b * BLOCK : (b + 1) * BLOCK, :],
            (((1,), (1,)), ((), ())),
            preferred_element_type=F32,
        )
        live = lax.broadcasted_iota(jnp.int32, turned.shape, 1) < fill_ref[b]
        out_ref[b] = jnp.where(live, turned, 0.0).astype(BF16)


def rank_cotangent(fill, parts, grad, lane_groups, rank, after):
    blocks = fill.shape[0]
    return pl.pallas_call(
        functools.partial(rank_kernel, lane_groups),
        out_shape=jax.ShapeDtypeStruct((blocks, rank, BLOCK), BF16),
        in_specs=[pl.BlockSpec(memory_space=pltpu.SMEM), spec(), spec()]
        + [pl.BlockSpec(memory_space=pl.ANY)] * len(after),
        out_specs=spec(),
        scratch_shapes=[pltpu.VMEM((blocks, rank, grad.shape[1]), BF16)],
        compiler_params=params(),
    )(fill, parts, grad, *after)


def up_kernel(fill_ref, low_ref, grad_ref, out_ref):
    parts, blocks, rank, width = out_ref.shape
    for b in range(blocks):
        low = low_ref[:, b * BLOCK : (b + 1) * BLOCK].astype(F32)
        live = lax.broadcasted_iota(jnp.int32, low.shape, 1) < fill_ref[b]
        low = jnp.where(live, low, 0.0).astype(BF16)
        whole = SCALE * jnp.dot(
            low, grad_ref[b * BLOCK : (b + 1) * BLOCK, :], preferred_element_type=F32
        )
        for p in range(parts):
            out_ref[p, b] = whole[:, p * width : (p + 1) * width].astype(BF16)


def up_products(fill, low_t, grad, parts):
    blocks, rank = fill.shape[0], low_t.shape[0]
    return pl.pallas_call(
        up_kernel,
        out_shape=jax.ShapeDtypeStruct((parts, blocks, rank, grad.shape[1] // parts), BF16),
        in_specs=[pl.BlockSpec(memory_space=pltpu.SMEM), spec(), spec()],
        out_specs=spec(),
        compiler_params=params(),
    )(fill, low_t, grad)


def down_kernel(low_ref, acts_ref, out_ref):
    parts, blocks, _, width = out_ref.shape
    for p in range(parts):
        for b in range(blocks):
            out_ref[p, b] = jnp.dot(
                low_ref[b],
                acts_ref[b * BLOCK : (b + 1) * BLOCK, p * width : (p + 1) * width],
                preferred_element_type=F32,
            ).astype(BF16)


def products(low_t, acts, parts, chunk):
    blocks, rank, _ = low_t.shape
    rows, width = acts.shape[0], acts.shape[1] // (parts * CHUNKS)
    steps = max(parts // PARTS_A_STEP, 1)
    each = parts // steps
    return pl.pallas_call(
        down_kernel,
        grid=(steps,),
        out_shape=jax.ShapeDtypeStruct((parts, blocks, rank, width), BF16),
        in_specs=[
            pl.BlockSpec(low_t.shape, lambda p: (0, 0, 0)),
            pl.BlockSpec((rows, width * each), lambda p: (0, chunk * steps + p)),
        ],
        out_specs=pl.BlockSpec((each, blocks, rank, width), lambda p: (p, 0, 0, 0)),
        compiler_params=params(),
        cost_estimate=pl.CostEstimate(
            flops=2 * rows * rank * width * parts,
            bytes_accessed=2 * parts * width * (rows + blocks * rank),
            transcendentals=0,
        ),
    )(low_t, acts)


def sum_kernel(blocks, count, has_extra, outs, groups, table_ref, *refs):
    held = refs[:count]
    if groups:
        kept, sems = refs[-2:]
        refs = refs[:-2]
    dests = refs[-outs:]
    outs = dests
    if groups:
        size = kept.shape[0] // groups
        outs = [kept.at[pl.ds(n * size, size)] for n in range(groups)]
        if len(dests) == 1:
            dests = [dests[0].at[pl.ds(n * size, size)] for n in range(groups)]
    copies = []
    extra_ref = refs[count] if has_extra else None
    targets = sum(out.shape[0] for out in outs)
    rank = outs[0].shape[1]
    base = blocks * count

    for n, out_ref in enumerate(outs):
        shift = n * out_ref.shape[0]

        def step(m, carry, out_ref=out_ref, shift=shift):
            at = base + shift + m
            low = 0
            for i, held_ref in enumerate(held):
                high = low + held_ref.shape[2]

                def add(j, total, i=i, held_ref=held_ref):
                    return total + held_ref[table_ref[i * blocks + j]].astype(F32)

                def add_extra(j, total, low=low, high=high):
                    return total + extra_ref[j, :, low:high].astype(F32)

                zero = jnp.zeros((rank, high - low), F32)
                total = lax.fori_loop(table_ref[at], table_ref[at + targets], add, zero)
                if has_extra:
                    total = lax.fori_loop(
                        table_ref[at + 2 * targets], table_ref[at + 3 * targets], add_extra, total
                    )
                out_ref[m, :, low:high] = total.astype(BF16)
                low = high
            return carry

        lax.fori_loop(0, out_ref.shape[0], step, 0)
        if groups:
            copies.append(pltpu.make_async_copy(out_ref, dests[n], sems.at[n]))
            copies[-1].start()
    for copy in copies:
        copy.wait()


def slot_sums(table, held, targets, hint, extra=None, outs=1, after=(), groups=0):
    blocks, rank, _ = held[0].shape
    width = sum(x.shape[2] for x in held)
    operands = list(held) + ([] if extra is None else [extra])
    shape = jax.ShapeDtypeStruct((targets // outs, rank, width), BF16)
    return pl.pallas_call(
        functools.partial(sum_kernel, blocks, len(held), extra is not None, outs, groups),
        out_shape=[shape] * outs,
        in_specs=[pl.BlockSpec(memory_space=pltpu.SMEM)]
        + [spec()] * len(operands)
        + [pl.BlockSpec(memory_space=pl.ANY)] * len(after),
        out_specs=[pl.BlockSpec(memory_space=pltpu.HBM) if groups else spec()] * outs,
        scratch_shapes=[
            pltpu.VMEM((targets, rank, width), BF16),
            pltpu.SemaphoreType.DMA((groups,)),
        ]
        if groups
        else [],
        compiler_params=params(),
        cost_estimate=pl.CostEstimate(flops=hint, bytes_accessed=hint, transcendentals=0),
    )(table, *operands, *after)


def place_kernel(*refs):
    landing_ref, got_ref, out_ref = refs[0], refs[1], refs[-1]
    for n in range(out_ref.shape[0]):
        spot = landing_ref[n]
        value = got_ref[0, jnp.maximum(spot, 0)]
        out_ref[n] = jnp.where(spot >= 0, value, jnp.zeros_like(value))


def place_all_kernel(got_ref, *refs):
    refs[-1][...] = got_ref[0]


def place(got, landing, slots, width, column, columns, chunk, into=None):
    parts, held, rank, _ = got.shape
    operands = [got] if landing is None else [landing, got]
    specs = [pl.BlockSpec((1, held, rank, width), lambda p: (p, 0, 0, column))]
    if landing is not None:
        specs = [pl.BlockSpec(memory_space=pltpu.SMEM)] + specs
    if into is not None:
        operands.append(into)
        specs.append(pl.BlockSpec(memory_space=pl.ANY))
    return pl.pallas_call(
        place_all_kernel if landing is None else place_kernel,
        grid=(parts,),
        out_shape=jax.ShapeDtypeStruct((slots, rank, columns), BF16),
        in_specs=specs,
        out_specs=pl.BlockSpec((slots, rank, width), lambda p: (0, 0, chunk * parts + p)),
        input_output_aliases={} if into is None else {len(operands) - 1: 0},
        compiler_params=params(),
        cost_estimate=pl.CostEstimate(
            flops=0, bytes_accessed=4 * parts * slots * rank * width, transcendentals=0
        ),
    )(*operands)


def lay_kernel(first, got_ref, _, out_ref, sems):
    parts, _, _, width = got_ref.shape
    copies = [
        pltpu.make_async_copy(
            got_ref.at[p], out_ref.at[:, :, pl.ds((first + p) * width, width)], sems.at[p]
        )
        for p in range(parts)
    ]
    for copy in copies:
        copy.start()
    for copy in copies:
        copy.wait()


def lay(got, first, into):
    anywhere = pl.BlockSpec(memory_space=pl.ANY)
    return pl.pallas_call(
        functools.partial(lay_kernel, first),
        out_shape=jax.ShapeDtypeStruct(into.shape, BF16),
        in_specs=[anywhere, anywhere],
        out_specs=anywhere,
        input_output_aliases={1: 0},
        scratch_shapes=[pltpu.SemaphoreType.DMA((got.shape[0],))],
        compiler_params=params(),
        cost_estimate=pl.CostEstimate(flops=0, bytes_accessed=4 * got.size, transcendentals=0),
    )(got, into)


def body(copies, devices, acts, grad_out, low_acts, up_weight, block_adapter, block_fill, owner_slot):
    own_blocks = block_fill.shape[0]
    blocks, adapters = block_adapter.shape[0], owner_slot.shape[0]
    own_slots, rank, out_width = up_weight.shape
    model_width = acts.shape[1]
    half_devices = devices // 2
    half_blocks, half_slots = blocks // 2, adapters // 2
    groups = [list(range(half_devices)), list(range(half_devices, devices))]
    across = [(i, (i + half_devices) % devices) for i in range(devices)]
    half = lax.axis_index("dp") // half_devices

    def within(x):
        return lax.all_to_all(x, "dp", 0, 0, axis_index_groups=groups, tiled=True)

    def relative(x, k):
        return lax.ppermute(x, "dp", [(i, i ^ k) for i in range(devices)]) if k else x

    ids = jnp.arange(adapters, dtype=jnp.int32)
    slot_of = jnp.sum(
        jnp.where(block_adapter[:, None] == ids[None, :], owner_slot[None, :], 0), axis=1
    )

    place_in_half = lax.axis_index("dp") % half_devices
    by_permutes = half_devices <= 8 and out_width // half_devices % 128 == 0
    up_held = up_products(block_fill, low_acts.T, grad_out, half_devices)
    if by_permutes:
        up_pieces = [
            lax.dynamic_index_in_dim(up_held, place_in_half ^ k, 0, False)
            for k in range(half_devices)
        ]
        up_pieces = [relative(x, k) for k, x in enumerate(up_pieces)]
    else:
        up_pieces = [within(up_held).reshape(half_blocks, rank, -1)]

    lane_groups = min(devices // 4, out_width // 128)
    row_groups = devices // lane_groups
    rows, lanes = rank // row_groups, out_width // lane_groups
    pieces = up_weight.reshape(own_slots, row_groups, rows, lane_groups, lanes)
    pieces = pieces.transpose(1, 3, 0, 2, 4).reshape(devices, own_slots, rows, lanes)
    part = lax.all_to_all(pieces, "dp", 0, 0, tiled=True).reshape(adapters, rows, lanes)
    picked = pick(slot_of, part).reshape(devices, own_blocks, rows, lanes)
    weights = lax.all_to_all(picked, "dp", 0, 0, tiled=True)

    mine = lax.dynamic_slice_in_dim(slot_of, half * half_blocks, half_blocks)
    spots = jnp.arange(half_blocks, dtype=jnp.int32)
    before = (mine[None, :] < mine[:, None]) | (
        (mine[None, :] == mine[:, None]) & (spots[None, :] < spots[:, None])
    )
    spot_of = jnp.sum(before.astype(jnp.int32), axis=1)
    order = jnp.sum(jnp.where(spot_of[None, :] == spots[:, None], spots[None, :], 0), axis=1)
    start = jnp.sum((mine[None, :] < ids[:, None]).astype(jnp.int32), axis=1)
    count = jnp.sum((mine[None, :] == ids[:, None]).astype(jnp.int32), axis=1)
    by_half = slot_of.reshape(2, half_blocks)
    has = jnp.any(by_half[:, :, None] == ids[None, None, :], axis=1)
    crosses = has & ((ids[None, :] // half_slots) != jnp.arange(2, dtype=jnp.int32)[:, None])
    earlier = (ids[None, :] < ids[:, None])[None, :, :]
    place_of = jnp.sum((crosses[:, None, :] & earlier).astype(jnp.int32), axis=2)
    used = jnp.any(has, axis=0).reshape(-1, own_slots)
    slot_ids = jnp.arange(own_slots, dtype=jnp.int32)
    rank_of = jnp.sum(
        (used[:, None, :] & (slot_ids[None, :] < slot_ids[:, None])[None]).astype(jnp.int32), axis=2
    )
    mine_needed = jnp.stack(
        [
            jnp.max(jnp.sum(crosses.astype(jnp.int32), axis=1)),
            jnp.max(jnp.sum(used.astype(jnp.int32), axis=1)),
        ]
    ).reshape(1, 2)
    needed = mine_needed
    for k in range(1, copies):
        shift = [(i, (i + k) % copies) for i in range(copies)]
        needed = jnp.maximum(needed, lax.ppermute(mine_needed, "groups", shift))
    needed, most = needed[0, 0], needed[0, 1]

    my_cross = lax.dynamic_index_in_dim(crosses, half, 0, False)
    my_place = lax.dynamic_index_in_dim(place_of, half, 0, False)
    hot = my_cross[None, :] & (my_place[None, :] == spots[:, None])
    send_first = jnp.sum(jnp.where(hot, start[None, :], 0), axis=1)
    send_last = jnp.sum(jnp.where(hot, (start + count)[None, :], 0), axis=1)

    own = half * half_slots
    keep_first = lax.dynamic_slice_in_dim(start, own, half_slots)
    keep_last = keep_first + lax.dynamic_slice_in_dim(count, own, half_slots)
    got = lax.dynamic_index_in_dim(crosses, 1 - half, 0, False)
    got = lax.dynamic_slice_in_dim(got, own, half_slots).astype(jnp.int32)
    got_first = lax.dynamic_index_in_dim(place_of, 1 - half, 0, False)
    got_first = lax.dynamic_slice_in_dim(got_first, own, half_slots)
    keep_table = jnp.concatenate([order, keep_first, keep_last, got_first, got_first + got])

    keep = jnp.stack([keep_first, keep_last, got_first, got_first + got])
    keep = keep.reshape(4, half_devices, 1, own_slots)
    half_used = lax.dynamic_slice_in_dim(used, half * half_devices, half_devices)
    half_rank = lax.dynamic_slice_in_dim(rank_of, half * half_devices, half_devices)
    chosen = half_used[:, None, :] & (half_rank[:, None, :] == slot_ids[None, :, None])
    packed = jnp.sum(jnp.where(chosen[None], keep, 0), axis=3)
    mine_at = lax.axis_index("dp")
    landing = jnp.where(
        lax.dynamic_index_in_dim(used, mine_at, 0, False),
        lax.dynamic_index_in_dim(rank_of, mine_at, 0, False),
        -1,
    )
    up_order = order
    if by_permutes:
        source, spot = order // own_blocks, order % own_blocks
        up_order = (source ^ place_in_half) * own_blocks + spot
    orders = jnp.concatenate([order, up_order])

    low_t = rank_cotangent(block_fill, weights, grad_out, lane_groups, rank, up_pieces)
    up_held = jnp.concatenate(up_pieces)
    first = within(products(low_t, acts, half_devices, 0))
    first = first.reshape(half_blocks, rank, -1)
    second = products(low_t, acts, half_devices, 1)
    width = second.shape[3]

    def rest(
        capacity, slots, first, up_held, second, orders, send_first, send_last, keep_table, packed,
        landing
    ):
        if slots < own_slots:
            ends = packed[:, :, :slots].reshape(-1)
        else:
            ends, landing = keep_table[half_blocks:], None
        keep_a_table = jnp.concatenate([orders, ends])
        keep_b_table = jnp.concatenate([orders[:half_blocks], ends])
        targets = half_devices * slots
        ends = jnp.concatenate([send_first[:capacity], send_last[:capacity]])
        send_a_table = jnp.concatenate([orders, ends])
        send_b_table = jnp.concatenate([orders[:half_blocks], ends])
        second = within(second).reshape(half_blocks, rank, -1)
        both = [first, up_held]
        (sent_a,) = slot_sums(send_a_table, both, capacity, SMALL)
        came_a = lax.ppermute(sent_a, "dp", across)
        (sent_b,) = slot_sums(send_b_table, [second], capacity, SMALL)
        came_a, sent_b = lax.optimization_barrier((came_a, sent_b))
        came_b = lax.ppermute(sent_b, "dp", across)
        (kept_a,) = slot_sums(
            keep_a_table, both, targets, SMALL, came_a, 1, (), GROUPS if by_permutes else 0
        )
        done_a = within(kept_a.reshape(half_devices, slots, rank, -1))
        up_width = out_width // half_devices
        if up_width % 128:
            up = done_a[:, :, :, width:].transpose(1, 2, 0, 3).reshape(own_slots, rank, out_width)
        else:
            up = place(done_a, landing, own_slots, up_width, width // up_width, out_width, 0)
        down = place(done_a, landing, own_slots, width, 0, model_width, 0)
        (kept_b,) = slot_sums(keep_b_table, [second], targets, LARGE, came_b, 1, (), GROUPS)
        done_b = within(kept_b.reshape(half_devices, slots, rank, -1))
        if landing is None:
            return lay(done_b, half_devices, down), up
        return place(done_b, landing, own_slots, width, 0, model_width, 1, down), up

    limit = min(half_blocks, half_slots)
    capacities = sorted({-(-limit * k // 24) for k in (9, 10, 11, 13, 24)})
    index = sum((needed > c).astype(jnp.int32) for c in capacities[:-1])
    sizes = [own_slots]
    if own_slots > 1 and out_width // half_devices % 128 == 0:
        sizes = [own_slots - 1, own_slots]
        index = 2 * index + (most >= own_slots).astype(jnp.int32)
    return lax.switch(
        index,
        [functools.partial(rest, c, n) for c in capacities for n in sizes],
        first, up_held, second, orders, send_first, send_last, keep_table, packed, landing,
    )


def solution(mesh):
    placed = (
        P(("groups", "dp"), None),
        P(("groups", "dp"), None),
        P(("groups", "dp"), None),
        P("dp", None, None),
        P("groups"),
        P(("groups", "dp")),
        P(),
    )
    return jax.shard_map(
        functools.partial(body, mesh.shape["groups"], mesh.shape["dp"]),
        mesh=mesh,
        in_specs=placed,
        out_specs=(P(("groups", "dp"), None, None), P(("groups", "dp"), None, None)),
        check_vma=False,
    )
```

```python
import functools

import jax
import jax.numpy as jnp
from jax import lax
from jax.experimental import pallas as pl
from jax.experimental.pallas import tpu as pltpu
from jax.sharding import PartitionSpec as P

BLOCK = 128
SCALE = 2.0
CHUNKS = 2
PARTS_A_STEP = 4
GROUPS = 8
BF16 = jnp.bfloat16
F32 = jnp.float32
VMEM_LIMIT = 48 * 1024 * 1024
SMALL, LARGE = 1 << 20, 1 << 38


def params():
    return pltpu.CompilerParams(vmem_limit_bytes=VMEM_LIMIT)


def spec():
    return pl.BlockSpec(memory_space=pltpu.VMEM)


def pick_kernel(slot_ref, parts_ref, out_ref):
    def step(b, carry):
        out_ref[b] = parts_ref[slot_ref[b]]
        return carry

    lax.fori_loop(0, out_ref.shape[0], step, 0)


def pick(slot_of, parts):
    blocks = slot_of.shape[0]
    return pl.pallas_call(
        pick_kernel,
        out_shape=jax.ShapeDtypeStruct((blocks,) + parts.shape[1:], BF16),
        in_specs=[pl.BlockSpec(memory_space=pltpu.SMEM), spec()],
        out_specs=spec(),
        compiler_params=params(),
    )(slot_of, parts)


def rank_kernel(lane_groups, fill_ref, parts_ref, grad_ref, *refs):
    out_ref, weight = refs[-2:]
    parts, blocks, rows, lanes = parts_ref.shape
    for b in range(blocks):
        for p in range(parts):
            g, l = p // lane_groups, p % lane_groups
            weight[b, g * rows : (g + 1) * rows, l * lanes : (l + 1) * lanes] = parts_ref[p, b]
    for b in range(blocks):
        turned = SCALE * lax.dot_general(
            weight[b],
            grad_ref[b * BLOCK : (b + 1) * BLOCK, :],
            (((1,), (1,)), ((), ())),
            preferred_element_type=F32,
        )
        live = lax.broadcasted_iota(jnp.int32, turned.shape, 1) < fill_ref[b]
        out_ref[b] = jnp.where(live, turned, 0.0).astype(BF16)


def rank_cotangent(fill, parts, grad, lane_groups, rank, after):
    blocks = fill.shape[0]
    return pl.pallas_call(
        functools.partial(rank_kernel, lane_groups),
        out_shape=jax.ShapeDtypeStruct((blocks, rank, BLOCK), BF16),
        in_specs=[pl.BlockSpec(memory_space=pltpu.SMEM), spec(), spec()]
        + [pl.BlockSpec(memory_space=pl.ANY)] * len(after),
        out_specs=spec(),
        scratch_shapes=[pltpu.VMEM((blocks, rank, grad.shape[1]), BF16)],
        compiler_params=params(),
    )(fill, parts, grad, *after)


def up_kernel(fill_ref, low_ref, grad_ref, out_ref):
    parts, blocks, rank, width = out_ref.shape
    for b in range(blocks):
        low = low_ref[:, b * BLOCK : (b + 1) * BLOCK].astype(F32)
        live = lax.broadcasted_iota(jnp.int32, low.shape, 1) < fill_ref[b]
        low = jnp.where(live, low, 0.0).astype(BF16)
        whole = SCALE * jnp.dot(
            low, grad_ref[b * BLOCK : (b + 1) * BLOCK, :], preferred_element_type=F32
        )
        for p in range(parts):
            out_ref[p, b] = whole[:, p * width : (p + 1) * width].astype(BF16)


def up_products(fill, low_t, grad, parts):
    blocks, rank = fill.shape[0], low_t.shape[0]
    return pl.pallas_call(
        up_kernel,
        out_shape=jax.ShapeDtypeStruct((parts, blocks, rank, grad.shape[1] // parts), BF16),
        in_specs=[pl.BlockSpec(memory_space=pltpu.SMEM), spec(), spec()],
        out_specs=spec(),
        compiler_params=params(),
    )(fill, low_t, grad)


def down_kernel(low_ref, acts_ref, out_ref):
    parts, blocks, _, width = out_ref.shape
    for p in range(parts):
        for b in range(blocks):
            out_ref[p, b] = jnp.dot(
                low_ref[b],
                acts_ref[b * BLOCK : (b + 1) * BLOCK, p * width : (p + 1) * width],
                preferred_element_type=F32,
            ).astype(BF16)


def products(low_t, acts, parts, chunk):
    blocks, rank, _ = low_t.shape
    rows, width = acts.shape[0], acts.shape[1] // (parts * CHUNKS)
    steps = max(parts // PARTS_A_STEP, 1)
    each = parts // steps
    return pl.pallas_call(
        down_kernel,
        grid=(steps,),
        out_shape=jax.ShapeDtypeStruct((parts, blocks, rank, width), BF16),
        in_specs=[
            pl.BlockSpec(low_t.shape, lambda p: (0, 0, 0)),
            pl.BlockSpec((rows, width * each), lambda p: (0, chunk * steps + p)),
        ],
        out_specs=pl.BlockSpec((each, blocks, rank, width), lambda p: (p, 0, 0, 0)),
        compiler_params=params(),
        cost_estimate=pl.CostEstimate(
            flops=2 * rows * rank * width * parts,
            bytes_accessed=2 * parts * width * (rows + blocks * rank),
            transcendentals=0,
        ),
    )(low_t, acts)


def sum_kernel(blocks, count, has_extra, outs, groups, table_ref, *refs):
    held = refs[:count]
    if groups:
        kept, sems = refs[-2:]
        refs = refs[:-2]
    dests = refs[-outs:]
    outs = dests
    if groups:
        size = kept.shape[0] // groups
        outs = [kept.at[pl.ds(n * size, size)] for n in range(groups)]
        if len(dests) == 1:
            dests = [dests[0].at[pl.ds(n * size, size)] for n in range(groups)]
    copies = []
    extra_ref = refs[count] if has_extra else None
    targets = sum(out.shape[0] for out in outs)
    rank = outs[0].shape[1]
    base = blocks * count

    for n, out_ref in enumerate(outs):
        shift = n * out_ref.shape[0]

        def step(m, carry, out_ref=out_ref, shift=shift):
            at = base + shift + m
            low = 0
            for i, held_ref in enumerate(held):
                high = low + held_ref.shape[2]

                def add(j, total, i=i, held_ref=held_ref):
                    return total + held_ref[table_ref[i * blocks + j]].astype(F32)

                def add_extra(j, total, low=low, high=high):
                    return total + extra_ref[j, :, low:high].astype(F32)

                zero = jnp.zeros((rank, high - low), F32)
                total = lax.fori_loop(table_ref[at], table_ref[at + targets], add, zero)
                if has_extra:
                    total = lax.fori_loop(
                        table_ref[at + 2 * targets], table_ref[at + 3 * targets], add_extra, total
                    )
                out_ref[m, :, low:high] = total.astype(BF16)
                low = high
            return carry

        lax.fori_loop(0, out_ref.shape[0], step, 0)
        if groups:
            copies.append(pltpu.make_async_copy(out_ref, dests[n], sems.at[n]))
            copies[-1].start()
    for copy in copies:
        copy.wait()


def slot_sums(table, held, targets, hint, extra=None, outs=1, after=(), groups=0):
    blocks, rank, _ = held[0].shape
    width = sum(x.shape[2] for x in held)
    operands = list(held) + ([] if extra is None else [extra])
    shape = jax.ShapeDtypeStruct((targets // outs, rank, width), BF16)
    return pl.pallas_call(
        functools.partial(sum_kernel, blocks, len(held), extra is not None, outs, groups),
        out_shape=[shape] * outs,
        in_specs=[pl.BlockSpec(memory_space=pltpu.SMEM)]
        + [spec()] * len(operands)
        + [pl.BlockSpec(memory_space=pl.ANY)] * len(after),
        out_specs=[pl.BlockSpec(memory_space=pltpu.HBM) if groups else spec()] * outs,
        scratch_shapes=[
            pltpu.VMEM((targets, rank, width), BF16),
            pltpu.SemaphoreType.DMA((groups,)),
        ]
        if groups
        else [],
        compiler_params=params(),
        cost_estimate=pl.CostEstimate(flops=hint, bytes_accessed=hint, transcendentals=0),
    )(table, *operands, *after)


def place_kernel(*refs):
    landing_ref, got_ref, out_ref = refs[0], refs[1], refs[-1]
    for n in range(out_ref.shape[0]):
        spot = landing_ref[n]
        value = got_ref[0, jnp.maximum(spot, 0)]
        out_ref[n] = jnp.where(spot >= 0, value, jnp.zeros_like(value))


def place_all_kernel(got_ref, *refs):
    refs[-1][...] = got_ref[0]


def place(got, landing, slots, width, column, columns, chunk, into=None):
    parts, held, rank, _ = got.shape
    operands = [got] if landing is None else [landing, got]
    specs = [pl.BlockSpec((1, held, rank, width), lambda p: (p, 0, 0, column))]
    if landing is not None:
        specs = [pl.BlockSpec(memory_space=pltpu.SMEM)] + specs
    if into is not None:
        operands.append(into)
        specs.append(pl.BlockSpec(memory_space=pl.ANY))
    return pl.pallas_call(
        place_all_kernel if landing is None else place_kernel,
        grid=(parts,),
        out_shape=jax.ShapeDtypeStruct((slots, rank, columns), BF16),
        in_specs=specs,
        out_specs=pl.BlockSpec((slots, rank, width), lambda p: (0, 0, chunk * parts + p)),
        input_output_aliases={} if into is None else {len(operands) - 1: 0},
        compiler_params=params(),
        cost_estimate=pl.CostEstimate(
            flops=0, bytes_accessed=4 * parts * slots * rank * width, transcendentals=0
        ),
    )(*operands)


def lay_kernel(first, width, has_landing, *refs):
    landing_ref, refs = (refs[0], refs[1:]) if has_landing else (None, refs)
    got_ref, _, down_ref, up_ref, zero, sems = refs
    parts, held, rank, whole = got_ref.shape
    waits = []
    if has_landing:
        zero[...] = jnp.zeros_like(zero)
    for p in range(parts):
        for o, (out, low, high, at) in enumerate(
            [(down_ref, 0, width, first + p), (up_ref, width, whole, p)]
        ):
            columns = pl.ds(at * (high - low), high - low)
            if not has_landing:
                copy = pltpu.make_async_copy(
                    got_ref.at[p, :, :, low:high], out.at[:, :, columns], sems.at[o, p, 0]
                )
                copy.start()
                waits.append(copy)
                continue
            for n in range(out.shape[0]):
                to = out.at[n, :, columns]
                sem = sems.at[o, p, n]
                none = pltpu.make_async_copy(zero.at[:, : high - low], to, sem)

                @pl.when(landing_ref[n] >= 0)
                def _(p=p, n=n, to=to, sem=sem, low=low, high=high):
                    spot = jnp.maximum(landing_ref[n], 0)
                    pltpu.make_async_copy(got_ref.at[p, spot, :, low:high], to, sem).start()

                @pl.when(landing_ref[n] < 0)
                def _(none=none):
                    none.start()

                waits.append(none)
    for wait in waits:
        wait.wait()


def lay(got, landing, first, width, into, out_width):
    parts, _, rank, _ = got.shape
    anywhere = pl.BlockSpec(memory_space=pl.ANY)
    operands = ([] if landing is None else [landing]) + [got, into]
    specs = [] if landing is None else [pl.BlockSpec(memory_space=pltpu.SMEM)]
    return pl.pallas_call(
        functools.partial(lay_kernel, first, width, landing is not None),
        out_shape=[
            jax.ShapeDtypeStruct(into.shape, BF16),
            jax.ShapeDtypeStruct(into.shape[:2] + (out_width,), BF16),
        ],
        in_specs=specs + [anywhere, anywhere],
        out_specs=[anywhere, anywhere],
        input_output_aliases={len(operands) - 1: 0},
        scratch_shapes=[
            pltpu.VMEM((rank, width), BF16),
            pltpu.SemaphoreType.DMA((2, parts, into.shape[0])),
        ],
        compiler_params=params(),
        cost_estimate=pl.CostEstimate(flops=0, bytes_accessed=4 * got.size, transcendentals=0),
    )(*operands)


def body(copies, devices, acts, grad_out, low_acts, up_weight, block_adapter, block_fill, owner_slot):
    own_blocks = block_fill.shape[0]
    blocks, adapters = block_adapter.shape[0], owner_slot.shape[0]
    own_slots, rank, out_width = up_weight.shape
    model_width = acts.shape[1]
    half_devices = devices // 2
    half_blocks, half_slots = blocks // 2, adapters // 2
    groups = [list(range(half_devices)), list(range(half_devices, devices))]
    across = [(i, (i + half_devices) % devices) for i in range(devices)]
    half = lax.axis_index("dp") // half_devices

    def within(x):
        return lax.all_to_all(x, "dp", 0, 0, axis_index_groups=groups, tiled=True)

    def relative(x, k):
        return lax.ppermute(x, "dp", [(i, i ^ k) for i in range(devices)]) if k else x

    ids = jnp.arange(adapters, dtype=jnp.int32)
    slot_of = jnp.sum(
        jnp.where(block_adapter[:, None] == ids[None, :], owner_slot[None, :], 0), axis=1
    )

    place_in_half = lax.axis_index("dp") % half_devices
    by_permutes = half_devices <= 8 and out_width // half_devices % 128 == 0
    up_held = up_products(block_fill, low_acts.T, grad_out, half_devices)
    if by_permutes:
        up_pieces = [
            lax.dynamic_index_in_dim(up_held, place_in_half ^ k, 0, False)
            for k in range(half_devices)
        ]
        up_pieces = [relative(x, k) for k, x in enumerate(up_pieces)]
    else:
        up_pieces = [within(up_held).reshape(half_blocks, rank, -1)]

    lane_groups = min(devices // 4, out_width // 128)
    row_groups = devices // lane_groups
    rows, lanes = rank // row_groups, out_width // lane_groups
    pieces = up_weight.reshape(own_slots, row_groups, rows, lane_groups, lanes)
    pieces = pieces.transpose(1, 3, 0, 2, 4).reshape(devices, own_slots, rows, lanes)
    part = lax.all_to_all(pieces, "dp", 0, 0, tiled=True).reshape(adapters, rows, lanes)
    picked = pick(slot_of, part).reshape(devices, own_blocks, rows, lanes)
    weights = lax.all_to_all(picked, "dp", 0, 0, tiled=True)

    mine = lax.dynamic_slice_in_dim(slot_of, half * half_blocks, half_blocks)
    spots = jnp.arange(half_blocks, dtype=jnp.int32)
    before = (mine[None, :] < mine[:, None]) | (
        (mine[None, :] == mine[:, None]) & (spots[None, :] < spots[:, None])
    )
    spot_of = jnp.sum(before.astype(jnp.int32), axis=1)
    order = jnp.sum(jnp.where(spot_of[None, :] == spots[:, None], spots[None, :], 0), axis=1)
    start = jnp.sum((mine[None, :] < ids[:, None]).astype(jnp.int32), axis=1)
    count = jnp.sum((mine[None, :] == ids[:, None]).astype(jnp.int32), axis=1)
    by_half = slot_of.reshape(2, half_blocks)
    has = jnp.any(by_half[:, :, None] == ids[None, None, :], axis=1)
    crosses = has & ((ids[None, :] // half_slots) != jnp.arange(2, dtype=jnp.int32)[:, None])
    earlier = (ids[None, :] < ids[:, None])[None, :, :]
    place_of = jnp.sum((crosses[:, None, :] & earlier).astype(jnp.int32), axis=2)
    used = jnp.any(has, axis=0).reshape(-1, own_slots)
    slot_ids = jnp.arange(own_slots, dtype=jnp.int32)
    rank_of = jnp.sum(
        (used[:, None, :] & (slot_ids[None, :] < slot_ids[:, None])[None]).astype(jnp.int32), axis=2
    )
    mine_needed = jnp.stack(
        [
            jnp.max(jnp.sum(crosses.astype(jnp.int32), axis=1)),
            jnp.max(jnp.sum(used.astype(jnp.int32), axis=1)),
        ]
    ).reshape(1, 2)
    needed = mine_needed
    for k in range(1, copies):
        shift = [(i, (i + k) % copies) for i in range(copies)]
        needed = jnp.maximum(needed, lax.ppermute(mine_needed, "groups", shift))
    needed, most = needed[0, 0], needed[0, 1]

    my_cross = lax.dynamic_index_in_dim(crosses, half, 0, False)
    my_place = lax.dynamic_index_in_dim(place_of, half, 0, False)
    hot = my_cross[None, :] & (my_place[None, :] == spots[:, None])
    send_first = jnp.sum(jnp.where(hot, start[None, :], 0), axis=1)
    send_last = jnp.sum(jnp.where(hot, (start + count)[None, :], 0), axis=1)

    own = half * half_slots
    keep_first = lax.dynamic_slice_in_dim(start, own, half_slots)
    keep_last = keep_first + lax.dynamic_slice_in_dim(count, own, half_slots)
    got = lax.dynamic_index_in_dim(crosses, 1 - half, 0, False)
    got = lax.dynamic_slice_in_dim(got, own, half_slots).astype(jnp.int32)
    got_first = lax.dynamic_index_in_dim(place_of, 1 - half, 0, False)
    got_first = lax.dynamic_slice_in_dim(got_first, own, half_slots)
    keep_table = jnp.concatenate([order, keep_first, keep_last, got_first, got_first + got])

    keep = jnp.stack([keep_first, keep_last, got_first, got_first + got])
    keep = keep.reshape(4, half_devices, 1, own_slots)
    half_used = lax.dynamic_slice_in_dim(used, half * half_devices, half_devices)
    half_rank = lax.dynamic_slice_in_dim(rank_of, half * half_devices, half_devices)
    chosen = half_used[:, None, :] & (half_rank[:, None, :] == slot_ids[None, :, None])
    packed = jnp.sum(jnp.where(chosen[None], keep, 0), axis=3)
    mine_at = lax.axis_index("dp")
    landing = jnp.where(
        lax.dynamic_index_in_dim(used, mine_at, 0, False),
        lax.dynamic_index_in_dim(rank_of, mine_at, 0, False),
        -1,
    )
    up_order = order
    if by_permutes:
        source, spot = order // own_blocks, order % own_blocks
        up_order = (source ^ place_in_half) * own_blocks + spot
    orders = jnp.concatenate([order, up_order])

    low_t = rank_cotangent(block_fill, weights, grad_out, lane_groups, rank, up_pieces)
    up_held = jnp.concatenate(up_pieces)
    first = within(products(low_t, acts, half_devices, 0))
    first = first.reshape(half_blocks, rank, -1)
    second = products(low_t, acts, half_devices, 1)
    width = second.shape[3]

    def rest(
        capacity, slots, first, up_held, second, orders, send_first, send_last, keep_table, packed,
        landing
    ):
        if slots < own_slots:
            ends = packed[:, :, :slots].reshape(-1)
        else:
            ends, landing = keep_table[half_blocks:], None
        keep_a_table = jnp.concatenate([orders[:half_blocks], ends])
        keep_b_table = jnp.concatenate([orders, ends])
        targets = half_devices * slots
        ends = jnp.concatenate([send_first[:capacity], send_last[:capacity]])
        send_a_table = jnp.concatenate([orders[:half_blocks], ends])
        send_b_table = jnp.concatenate([orders, ends])
        groups = GROUPS if by_permutes else 0
        both = [within(second).reshape(half_blocks, rank, -1), up_held]
        (sent_a,) = slot_sums(send_a_table, [first], capacity, SMALL)
        came_a = lax.ppermute(sent_a, "dp", across)
        (sent_b,) = slot_sums(send_b_table, both, capacity, SMALL)
        came_a, sent_b = lax.optimization_barrier((came_a, sent_b))
        came_b = lax.ppermute(sent_b, "dp", across)
        (kept_a,) = slot_sums(keep_a_table, [first], targets, SMALL, came_a, 1, (), groups)
        done_a = within(kept_a.reshape(half_devices, slots, rank, -1))
        down = place(done_a, landing, own_slots, width, 0, model_width, 0)
        (kept_b,) = slot_sums(keep_b_table, both, targets, LARGE, came_b, 1, (), groups)
        done_b = within(kept_b.reshape(half_devices, slots, rank, -1))
        if by_permutes:
            return tuple(lay(done_b, landing, half_devices, width, down, out_width))
        up = done_b[:, :, :, width:].transpose(1, 2, 0, 3).reshape(own_slots, rank, out_width)
        return place(done_b, landing, own_slots, width, 0, model_width, 1, down), up

    limit = min(half_blocks, half_slots)
    capacities = sorted({-(-limit * k // 24) for k in (9, 10, 11, 13, 24)})
    index = sum((needed > c).astype(jnp.int32) for c in capacities[:-1])
    sizes = [own_slots]
    if own_slots > 1 and by_permutes:
        sizes = [own_slots - 1, own_slots]
        index = 2 * index + (most >= own_slots).astype(jnp.int32)
    return lax.switch(
        index,
        [functools.partial(rest, c, n) for c in capacities for n in sizes],
        first, up_held, second, orders, send_first, send_last, keep_table, packed, landing,
    )


def solution(mesh):
    placed = (
        P(("groups", "dp"), None),
        P(("groups", "dp"), None),
        P(("groups", "dp"), None),
        P("dp", None, None),
        P("groups"),
        P(("groups", "dp")),
        P(),
    )
    return jax.shard_map(
        functools.partial(body, mesh.shape["groups"], mesh.shape["dp"]),
        mesh=mesh,
        in_specs=placed,
        out_specs=(P(("groups", "dp"), None, None), P(("groups", "dp"), None, None)),
        check_vma=False,
    )
```

```python
import functools

import jax
import jax.numpy as jnp
from jax import lax
from jax.experimental import pallas as pl
from jax.experimental.pallas import tpu as pltpu
from jax.sharding import PartitionSpec as P

BLOCK = 128
SCALE = 2.0
CHUNKS = 2
PARTS_A_STEP = 4
GROUPS = 8
BF16 = jnp.bfloat16
F32 = jnp.float32
VMEM_LIMIT = 48 * 1024 * 1024
SMALL, LARGE = 1 << 20, 1 << 38


def params():
    return pltpu.CompilerParams(vmem_limit_bytes=VMEM_LIMIT)


def spec():
    return pl.BlockSpec(memory_space=pltpu.VMEM)


def cut_kernel(lane_groups, weight_ref, out_ref):
    parts, slots, rows, lanes = out_ref.shape
    for p in range(parts):
        g, l = p // lane_groups, p % lane_groups
        for n in range(slots):
            out_ref[p, n] = weight_ref[n, g * rows : (g + 1) * rows, l * lanes : (l + 1) * lanes]


def cut(weight, parts, lane_groups, rows, lanes):
    return pl.pallas_call(
        functools.partial(cut_kernel, lane_groups),
        out_shape=jax.ShapeDtypeStruct((parts, weight.shape[0], rows, lanes), BF16),
        in_specs=[spec()],
        out_specs=spec(),
        compiler_params=params(),
    )(weight)


def pick_kernel(slot_ref, parts_ref, out_ref):
    def step(b, carry):
        out_ref[b] = parts_ref[slot_ref[b]]
        return carry

    lax.fori_loop(0, out_ref.shape[0], step, 0)


def pick(slot_of, parts):
    blocks = slot_of.shape[0]
    return pl.pallas_call(
        pick_kernel,
        out_shape=jax.ShapeDtypeStruct((blocks,) + parts.shape[1:], BF16),
        in_specs=[pl.BlockSpec(memory_space=pltpu.SMEM), spec()],
        out_specs=spec(),
        compiler_params=params(),
    )(slot_of, parts)


def rank_kernel(lane_groups, fill_ref, parts_ref, grad_ref, *refs):
    out_ref, weight = refs[-2:]
    parts, blocks, rows, lanes = parts_ref.shape
    for b in range(blocks):
        for p in range(parts):
            g, l = p // lane_groups, p % lane_groups
            weight[b, g * rows : (g + 1) * rows, l * lanes : (l + 1) * lanes] = parts_ref[p, b]
    for b in range(blocks):
        turned = SCALE * lax.dot_general(
            weight[b],
            grad_ref[b * BLOCK : (b + 1) * BLOCK, :],
            (((1,), (1,)), ((), ())),
            preferred_element_type=F32,
        )
        live = lax.broadcasted_iota(jnp.int32, turned.shape, 1) < fill_ref[b]
        out_ref[b] = jnp.where(live, turned, 0.0).astype(BF16)


def rank_cotangent(fill, parts, grad, lane_groups, rank, after):
    blocks = fill.shape[0]
    return pl.pallas_call(
        functools.partial(rank_kernel, lane_groups),
        out_shape=jax.ShapeDtypeStruct((blocks, rank, BLOCK), BF16),
        in_specs=[pl.BlockSpec(memory_space=pltpu.SMEM), spec(), spec()]
        + [pl.BlockSpec(memory_space=pl.ANY)] * len(after),
        out_specs=spec(),
        scratch_shapes=[pltpu.VMEM((blocks, rank, grad.shape[1]), BF16)],
        compiler_params=params(),
    )(fill, parts, grad, *after)


def up_kernel(fill_ref, low_ref, grad_ref, out_ref):
    parts, blocks, rank, width = out_ref.shape
    for b in range(blocks):
        low = low_ref[:, b * BLOCK : (b + 1) * BLOCK].astype(F32)
        live = lax.broadcasted_iota(jnp.int32, low.shape, 1) < fill_ref[b]
        low = jnp.where(live, low, 0.0).astype(BF16)
        whole = SCALE * jnp.dot(
            low, grad_ref[b * BLOCK : (b + 1) * BLOCK, :], preferred_element_type=F32
        )
        for p in range(parts):
            out_ref[p, b] = whole[:, p * width : (p + 1) * width].astype(BF16)


def up_products(fill, low_t, grad, parts):
    blocks, rank = fill.shape[0], low_t.shape[0]
    return pl.pallas_call(
        up_kernel,
        out_shape=jax.ShapeDtypeStruct((parts, blocks, rank, grad.shape[1] // parts), BF16),
        in_specs=[pl.BlockSpec(memory_space=pltpu.SMEM), spec(), spec()],
        out_specs=spec(),
        compiler_params=params(),
    )(fill, low_t, grad)


def down_kernel(low_ref, acts_ref, out_ref):
    parts, blocks, _, width = out_ref.shape
    for p in range(parts):
        for b in range(blocks):
            out_ref[p, b] = jnp.dot(
                low_ref[b],
                acts_ref[b * BLOCK : (b + 1) * BLOCK, p * width : (p + 1) * width],
                preferred_element_type=F32,
            ).astype(BF16)


def products(low_t, acts, parts, chunk):
    blocks, rank, _ = low_t.shape
    rows, width = acts.shape[0], acts.shape[1] // (parts * CHUNKS)
    steps = max(parts // PARTS_A_STEP, 1)
    each = parts // steps
    return pl.pallas_call(
        down_kernel,
        grid=(steps,),
        out_shape=jax.ShapeDtypeStruct((parts, blocks, rank, width), BF16),
        in_specs=[
            pl.BlockSpec(low_t.shape, lambda p: (0, 0, 0)),
            pl.BlockSpec((rows, width * each), lambda p: (0, chunk * steps + p)),
        ],
        out_specs=pl.BlockSpec((each, blocks, rank, width), lambda p: (p, 0, 0, 0)),
        compiler_params=params(),
        cost_estimate=pl.CostEstimate(
            flops=2 * rows * rank * width * parts,
            bytes_accessed=2 * parts * width * (rows + blocks * rank),
            transcendentals=0,
        ),
    )(low_t, acts)


def sum_kernel(blocks, count, has_extra, outs, groups, table_ref, *refs):
    held = refs[:count]
    if groups:
        kept, sems = refs[-2:]
        refs = refs[:-2]
    dests = refs[-outs:]
    outs = dests
    if groups:
        size = kept.shape[0] // groups
        outs = [kept.at[pl.ds(n * size, size)] for n in range(groups)]
        if len(dests) == 1:
            dests = [dests[0].at[pl.ds(n * size, size)] for n in range(groups)]
    copies = []
    extra_ref = refs[count] if has_extra else None
    targets = sum(out.shape[0] for out in outs)
    rank = outs[0].shape[1]
    base = blocks * count

    for n, out_ref in enumerate(outs):
        shift = n * out_ref.shape[0]

        def step(m, carry, out_ref=out_ref, shift=shift):
            at = base + shift + m
            low = 0
            for i, held_ref in enumerate(held):
                high = low + held_ref.shape[2]

                def add(j, total, i=i, held_ref=held_ref):
                    return total + held_ref[table_ref[i * blocks + j]].astype(F32)

                def add_extra(j, total, low=low, high=high):
                    return total + extra_ref[j, :, low:high].astype(F32)

                zero = jnp.zeros((rank, high - low), F32)
                total = lax.fori_loop(table_ref[at], table_ref[at + targets], add, zero)
                if has_extra:
                    total = lax.fori_loop(
                        table_ref[at + 2 * targets], table_ref[at + 3 * targets], add_extra, total
                    )
                out_ref[m, :, low:high] = total.astype(BF16)
                low = high
            return carry

        lax.fori_loop(0, out_ref.shape[0], step, 0)
        if groups:
            copies.append(pltpu.make_async_copy(out_ref, dests[n], sems.at[n]))
            copies[-1].start()
    for copy in copies:
        copy.wait()


def slot_sums(table, held, targets, hint, extra=None, outs=1, after=(), groups=0):
    blocks, rank, _ = held[0].shape
    width = sum(x.shape[2] for x in held)
    operands = list(held) + ([] if extra is None else [extra])
    shape = jax.ShapeDtypeStruct((targets // outs, rank, width), BF16)
    return pl.pallas_call(
        functools.partial(sum_kernel, blocks, len(held), extra is not None, outs, groups),
        out_shape=[shape] * outs,
        in_specs=[pl.BlockSpec(memory_space=pltpu.SMEM)]
        + [spec()] * len(operands)
        + [pl.BlockSpec(memory_space=pl.ANY)] * len(after),
        out_specs=[pl.BlockSpec(memory_space=pltpu.HBM) if groups else spec()] * outs,
        scratch_shapes=[
            pltpu.VMEM((targets, rank, width), BF16),
            pltpu.SemaphoreType.DMA((groups,)),
        ]
        if groups
        else [],
        compiler_params=params(),
        cost_estimate=pl.CostEstimate(flops=hint, bytes_accessed=hint, transcendentals=0),
    )(table, *operands, *after)


def place_kernel(*refs):
    landing_ref, got_ref, out_ref = refs[0], refs[1], refs[-1]
    for n in range(out_ref.shape[0]):
        spot = landing_ref[n]
        value = got_ref[0, jnp.maximum(spot, 0)]
        out_ref[n] = jnp.where(spot >= 0, value, jnp.zeros_like(value))


def place_all_kernel(got_ref, *refs):
    refs[-1][...] = got_ref[0]


def place(got, landing, slots, width, column, columns, chunk, into=None):
    parts, held, rank, _ = got.shape
    operands = [got] if landing is None else [landing, got]
    specs = [pl.BlockSpec((1, held, rank, width), lambda p: (p, 0, 0, column))]
    if landing is not None:
        specs = [pl.BlockSpec(memory_space=pltpu.SMEM)] + specs
    if into is not None:
        operands.append(into)
        specs.append(pl.BlockSpec(memory_space=pl.ANY))
    return pl.pallas_call(
        place_all_kernel if landing is None else place_kernel,
        grid=(parts,),
        out_shape=jax.ShapeDtypeStruct((slots, rank, columns), BF16),
        in_specs=specs,
        out_specs=pl.BlockSpec((slots, rank, width), lambda p: (0, 0, chunk * parts + p)),
        input_output_aliases={} if into is None else {len(operands) - 1: 0},
        compiler_params=params(),
        cost_estimate=pl.CostEstimate(
            flops=0, bytes_accessed=4 * parts * slots * rank * width, transcendentals=0
        ),
    )(*operands)


def lay_kernel(first, width, has_landing, *refs):
    landing_ref, refs = (refs[0], refs[1:]) if has_landing else (None, refs)
    got_ref, _, down_ref, up_ref, zero, sems = refs
    parts, held, rank, whole = got_ref.shape
    waits = []
    if has_landing:
        zero[...] = jnp.zeros_like(zero)
    for p in range(parts):
        for o, (out, low, high, at) in enumerate(
            [(down_ref, 0, width, first + p), (up_ref, width, whole, p)]
        ):
            columns = pl.ds(at * (high - low), high - low)
            if not has_landing:
                copy = pltpu.make_async_copy(
                    got_ref.at[p, :, :, low:high], out.at[:, :, columns], sems.at[o, p, 0]
                )
                copy.start()
                waits.append(copy)
                continue
            for n in range(out.shape[0]):
                to = out.at[n, :, columns]
                sem = sems.at[o, p, n]
                none = pltpu.make_async_copy(zero.at[:, : high - low], to, sem)

                @pl.when(landing_ref[n] >= 0)
                def _(p=p, n=n, to=to, sem=sem, low=low, high=high):
                    spot = jnp.maximum(landing_ref[n], 0)
                    pltpu.make_async_copy(got_ref.at[p, spot, :, low:high], to, sem).start()

                @pl.when(landing_ref[n] < 0)
                def _(none=none):
                    none.start()

                waits.append(none)
    for wait in waits:
        wait.wait()


def lay(got, landing, first, width, into, out_width):
    parts, _, rank, _ = got.shape
    anywhere = pl.BlockSpec(memory_space=pl.ANY)
    operands = ([] if landing is None else [landing]) + [got, into]
    specs = [] if landing is None else [pl.BlockSpec(memory_space=pltpu.SMEM)]
    return pl.pallas_call(
        functools.partial(lay_kernel, first, width, landing is not None),
        out_shape=[
            jax.ShapeDtypeStruct(into.shape, BF16),
            jax.ShapeDtypeStruct(into.shape[:2] + (out_width,), BF16),
        ],
        in_specs=specs + [anywhere, anywhere],
        out_specs=[anywhere, anywhere],
        input_output_aliases={len(operands) - 1: 0},
        scratch_shapes=[
            pltpu.VMEM((rank, width), BF16),
            pltpu.SemaphoreType.DMA((2, parts, into.shape[0])),
        ],
        compiler_params=params(),
        cost_estimate=pl.CostEstimate(flops=0, bytes_accessed=4 * got.size, transcendentals=0),
    )(*operands)


def body(copies, devices, acts, grad_out, low_acts, up_weight, block_adapter, block_fill, owner_slot):
    own_blocks = block_fill.shape[0]
    blocks, adapters = block_adapter.shape[0], owner_slot.shape[0]
    own_slots, rank, out_width = up_weight.shape
    model_width = acts.shape[1]
    half_devices = devices // 2
    half_blocks, half_slots = blocks // 2, adapters // 2
    groups = [list(range(half_devices)), list(range(half_devices, devices))]
    across = [(i, (i + half_devices) % devices) for i in range(devices)]
    half = lax.axis_index("dp") // half_devices

    def within(x):
        return lax.all_to_all(x, "dp", 0, 0, axis_index_groups=groups, tiled=True)

    def relative(x, k):
        return lax.ppermute(x, "dp", [(i, i ^ k) for i in range(devices)]) if k else x

    ids = jnp.arange(adapters, dtype=jnp.int32)
    slot_of = jnp.sum(
        jnp.where(block_adapter[:, None] == ids[None, :], owner_slot[None, :], 0), axis=1
    )

    place_in_half = lax.axis_index("dp") % half_devices
    by_permutes = half_devices <= 8 and out_width // half_devices % 128 == 0
    up_held = up_products(block_fill, low_acts.T, grad_out, half_devices)
    if by_permutes:
        up_pieces = [
            lax.dynamic_index_in_dim(up_held, place_in_half ^ k, 0, False)
            for k in range(half_devices)
        ]
        up_pieces = [relative(x, k) for k, x in enumerate(up_pieces)]
    else:
        up_pieces = [within(up_held).reshape(half_blocks, rank, -1)]

    lane_groups = min(devices // 4, out_width // 128)
    row_groups = devices // lane_groups
    rows, lanes = rank // row_groups, out_width // lane_groups
    pieces = cut(up_weight, devices, lane_groups, rows, lanes)
    part = lax.all_to_all(pieces, "dp", 0, 0, tiled=True).reshape(adapters, rows, lanes)
    picked = pick(slot_of, part).reshape(devices, own_blocks, rows, lanes)
    weights = lax.all_to_all(picked, "dp", 0, 0, tiled=True)

    mine = lax.dynamic_slice_in_dim(slot_of, half * half_blocks, half_blocks)
    spots = jnp.arange(half_blocks, dtype=jnp.int32)
    before = (mine[None, :] < mine[:, None]) | (
        (mine[None, :] == mine[:, None]) & (spots[None, :] < spots[:, None])
    )
    spot_of = jnp.sum(before.astype(jnp.int32), axis=1)
    order = jnp.sum(jnp.where(spot_of[None, :] == spots[:, None], spots[None, :], 0), axis=1)
    start = jnp.sum((mine[None, :] < ids[:, None]).astype(jnp.int32), axis=1)
    count = jnp.sum((mine[None, :] == ids[:, None]).astype(jnp.int32), axis=1)
    by_half = slot_of.reshape(2, half_blocks)
    has = jnp.any(by_half[:, :, None] == ids[None, None, :], axis=1)
    crosses = has & ((ids[None, :] // half_slots) != jnp.arange(2, dtype=jnp.int32)[:, None])
    earlier = (ids[None, :] < ids[:, None])[None, :, :]
    place_of = jnp.sum((crosses[:, None, :] & earlier).astype(jnp.int32), axis=2)
    used = jnp.any(has, axis=0).reshape(-1, own_slots)
    slot_ids = jnp.arange(own_slots, dtype=jnp.int32)
    rank_of = jnp.sum(
        (used[:, None, :] & (slot_ids[None, :] < slot_ids[:, None])[None]).astype(jnp.int32), axis=2
    )
    mine_needed = jnp.stack(
        [
            jnp.max(jnp.sum(crosses.astype(jnp.int32), axis=1)),
            jnp.max(jnp.sum(used.astype(jnp.int32), axis=1)),
        ]
    ).reshape(1, 2)
    needed = mine_needed
    for k in range(1, copies):
        shift = [(i, (i + k) % copies) for i in range(copies)]
        needed = jnp.maximum(needed, lax.ppermute(mine_needed, "groups", shift))
    needed, most = needed[0, 0], needed[0, 1]

    my_cross = lax.dynamic_index_in_dim(crosses, half, 0, False)
    my_place = lax.dynamic_index_in_dim(place_of, half, 0, False)
    hot = my_cross[None, :] & (my_place[None, :] == spots[:, None])
    send_first = jnp.sum(jnp.where(hot, start[None, :], 0), axis=1)
    send_last = jnp.sum(jnp.where(hot, (start + count)[None, :], 0), axis=1)

    own = half * half_slots
    keep_first = lax.dynamic_slice_in_dim(start, own, half_slots)
    keep_last = keep_first + lax.dynamic_slice_in_dim(count, own, half_slots)
    got = lax.dynamic_index_in_dim(crosses, 1 - half, 0, False)
    got = lax.dynamic_slice_in_dim(got, own, half_slots).astype(jnp.int32)
    got_first = lax.dynamic_index_in_dim(place_of, 1 - half, 0, False)
    got_first = lax.dynamic_slice_in_dim(got_first, own, half_slots)
    keep_table = jnp.concatenate([order, keep_first, keep_last, got_first, got_first + got])

    keep = jnp.stack([keep_first, keep_last, got_first, got_first + got])
    keep = keep.reshape(4, half_devices, 1, own_slots)
    half_used = lax.dynamic_slice_in_dim(used, half * half_devices, half_devices)
    half_rank = lax.dynamic_slice_in_dim(rank_of, half * half_devices, half_devices)
    chosen = half_used[:, None, :] & (half_rank[:, None, :] == slot_ids[None, :, None])
    packed = jnp.sum(jnp.where(chosen[None], keep, 0), axis=3)
    mine_at = lax.axis_index("dp")
    landing = jnp.where(
        lax.dynamic_index_in_dim(used, mine_at, 0, False),
        lax.dynamic_index_in_dim(rank_of, mine_at, 0, False),
        -1,
    )
    up_order = order
    if by_permutes:
        source, spot = order // own_blocks, order % own_blocks
        up_order = (source ^ place_in_half) * own_blocks + spot
    orders = jnp.concatenate([order, up_order])

    low_t = rank_cotangent(block_fill, weights, grad_out, lane_groups, rank, up_pieces)
    up_held = jnp.concatenate(up_pieces)
    first = within(products(low_t, acts, half_devices, 0))
    first = first.reshape(half_blocks, rank, -1)
    second = products(low_t, acts, half_devices, 1)
    width = second.shape[3]

    def rest(
        capacity, slots, first, up_held, second, orders, send_first, send_last, keep_table, packed,
        landing
    ):
        if slots < own_slots:
            ends = packed[:, :, :slots].reshape(-1)
        else:
            ends, landing = keep_table[half_blocks:], None
        keep_a_table = jnp.concatenate([orders[:half_blocks], ends])
        keep_b_table = jnp.concatenate([orders, ends])
        targets = half_devices * slots
        ends = jnp.concatenate([send_first[:capacity], send_last[:capacity]])
        send_a_table = jnp.concatenate([orders[:half_blocks], ends])
        send_b_table = jnp.concatenate([orders, ends])
        groups = GROUPS if by_permutes else 0
        both = [within(second).reshape(half_blocks, rank, -1), up_held]
        (sent_a,) = slot_sums(send_a_table, [first], capacity, SMALL)
        came_a = lax.ppermute(sent_a, "dp", across)
        (kept_a,) = slot_sums(keep_a_table, [first], targets, SMALL, came_a, 1, (), groups)
        (sent_b,) = slot_sums(send_b_table, both, capacity, SMALL, None, 1, (kept_a,))
        came_b = lax.ppermute(sent_b, "dp", across)
        done_a = within(kept_a.reshape(half_devices, slots, rank, -1))
        down = place(done_a, landing, own_slots, width, 0, model_width, 0)
        (kept_b,) = slot_sums(keep_b_table, both, targets, LARGE, came_b, 1, (), groups)
        done_b = within(kept_b.reshape(half_devices, slots, rank, -1))
        if by_permutes:
            return tuple(lay(done_b, landing, half_devices, width, down, out_width))
        up = done_b[:, :, :, width:].transpose(1, 2, 0, 3).reshape(own_slots, rank, out_width)
        return place(done_b, landing, own_slots, width, 0, model_width, 1, down), up

    limit = min(half_blocks, half_slots)
    capacities = sorted({-(-limit * k // 24) for k in (8, 9, 10, 12, 14, 24)})
    index = sum((needed > c).astype(jnp.int32) for c in capacities[:-1])
    sizes = [own_slots]
    if own_slots > 1 and by_permutes:
        sizes = [own_slots - 1, own_slots]
        index = 2 * index + (most >= own_slots).astype(jnp.int32)
        index = jnp.minimum(index, 2 * len(capacities) - 2)
    return lax.switch(
        index,
        [functools.partial(rest, c, n) for c in capacities[:-1] for n in sizes]
        + [functools.partial(rest, capacities[-1], own_slots)],
        first, up_held, second, orders, send_first, send_last, keep_table, packed, landing,
    )


def solution(mesh):
    placed = (
        P(("groups", "dp"), None),
        P(("groups", "dp"), None),
        P(("groups", "dp"), None),
        P("dp", None, None),
        P("groups"),
        P(("groups", "dp")),
        P(),
    )
    return jax.shard_map(
        functools.partial(body, mesh.shape["groups"], mesh.shape["dp"]),
        mesh=mesh,
        in_specs=placed,
        out_specs=(P(("groups", "dp"), None, None), P(("groups", "dp"), None, None)),
        check_vma=False,
    )
```

```python
import functools

import jax
import jax.numpy as jnp
from jax import lax
from jax.experimental import pallas as pl
from jax.experimental.pallas import tpu as pltpu
from jax.sharding import PartitionSpec as P

BLOCK = 128
SCALE = 2.0
CHUNKS = 2
PARTS_A_STEP = 4
GROUPS = 2
BF16 = jnp.bfloat16
F32 = jnp.float32
VMEM_LIMIT = 48 * 1024 * 1024
SMALL, LARGE = 1 << 20, 1 << 38


def params():
    return pltpu.CompilerParams(vmem_limit_bytes=VMEM_LIMIT)


def spec():
    return pl.BlockSpec(memory_space=pltpu.VMEM)


def cut_kernel(lane_groups, weight_ref, out_ref):
    parts, slots, rows, lanes = out_ref.shape
    for p in range(parts):
        g, l = p // lane_groups, p % lane_groups
        for n in range(slots):
            out_ref[p, n] = weight_ref[n, g * rows : (g + 1) * rows, l * lanes : (l + 1) * lanes]


def cut(weight, parts, lane_groups, rows, lanes):
    return pl.pallas_call(
        functools.partial(cut_kernel, lane_groups),
        out_shape=jax.ShapeDtypeStruct((parts, weight.shape[0], rows, lanes), BF16),
        in_specs=[spec()],
        out_specs=spec(),
        compiler_params=params(),
    )(weight)


def pick_kernel(slot_ref, parts_ref, out_ref):
    def step(b, carry):
        out_ref[b] = parts_ref[slot_ref[b]]
        return carry

    lax.fori_loop(0, out_ref.shape[0], step, 0)


def pick(slot_of, parts):
    blocks = slot_of.shape[0]
    return pl.pallas_call(
        pick_kernel,
        out_shape=jax.ShapeDtypeStruct((blocks,) + parts.shape[1:], BF16),
        in_specs=[pl.BlockSpec(memory_space=pltpu.SMEM), spec()],
        out_specs=spec(),
        compiler_params=params(),
    )(slot_of, parts)


def rank_kernel(lane_groups, fill_ref, parts_ref, grad_ref, *refs):
    out_ref, weight = refs[-2:]
    parts, blocks, rows, lanes = parts_ref.shape
    for b in range(blocks):
        for p in range(parts):
            g, l = p // lane_groups, p % lane_groups
            weight[b, g * rows : (g + 1) * rows, l * lanes : (l + 1) * lanes] = parts_ref[p, b]
    for b in range(blocks):
        turned = SCALE * lax.dot_general(
            weight[b],
            grad_ref[b * BLOCK : (b + 1) * BLOCK, :],
            (((1,), (1,)), ((), ())),
            preferred_element_type=F32,
        )
        live = lax.broadcasted_iota(jnp.int32, turned.shape, 1) < fill_ref[b]
        out_ref[b] = jnp.where(live, turned, 0.0).astype(BF16)


def rank_cotangent(fill, parts, grad, lane_groups, rank, after):
    blocks = fill.shape[0]
    return pl.pallas_call(
        functools.partial(rank_kernel, lane_groups),
        out_shape=jax.ShapeDtypeStruct((blocks, rank, BLOCK), BF16),
        in_specs=[pl.BlockSpec(memory_space=pltpu.SMEM), spec(), spec()]
        + [pl.BlockSpec(memory_space=pl.ANY)] * len(after),
        out_specs=spec(),
        scratch_shapes=[pltpu.VMEM((blocks, rank, grad.shape[1]), BF16)],
        compiler_params=params(),
    )(fill, parts, grad, *after)


def up_kernel(fill_ref, low_ref, grad_ref, out_ref):
    parts, blocks, rank, width = out_ref.shape
    for b in range(blocks):
        low = low_ref[:, b * BLOCK : (b + 1) * BLOCK].astype(F32)
        live = lax.broadcasted_iota(jnp.int32, low.shape, 1) < fill_ref[b]
        low = jnp.where(live, low, 0.0).astype(BF16)
        whole = SCALE * jnp.dot(
            low, grad_ref[b * BLOCK : (b + 1) * BLOCK, :], preferred_element_type=F32
        )
        for p in range(parts):
            out_ref[p, b] = whole[:, p * width : (p + 1) * width].astype(BF16)


def up_products(fill, low_t, grad, parts):
    blocks, rank = fill.shape[0], low_t.shape[0]
    return pl.pallas_call(
        up_kernel,
        out_shape=jax.ShapeDtypeStruct((parts, blocks, rank, grad.shape[1] // parts), BF16),
        in_specs=[pl.BlockSpec(memory_space=pltpu.SMEM), spec(), spec()],
        out_specs=spec(),
        compiler_params=params(),
    )(fill, low_t, grad)


def down_kernel(low_ref, acts_ref, out_ref):
    parts, blocks, _, width = out_ref.shape
    for p in range(parts):
        for b in range(blocks):
            out_ref[p, b] = jnp.dot(
                low_ref[b],
                acts_ref[b * BLOCK : (b + 1) * BLOCK, p * width : (p + 1) * width],
                preferred_element_type=F32,
            ).astype(BF16)


def products(low_t, acts, parts, chunk):
    blocks, rank, _ = low_t.shape
    rows, width = acts.shape[0], acts.shape[1] // (parts * CHUNKS)
    steps = max(parts // PARTS_A_STEP, 1)
    each = parts // steps
    return pl.pallas_call(
        down_kernel,
        grid=(steps,),
        out_shape=jax.ShapeDtypeStruct((parts, blocks, rank, width), BF16),
        in_specs=[
            pl.BlockSpec(low_t.shape, lambda p: (0, 0, 0)),
            pl.BlockSpec((rows, width * each), lambda p: (0, chunk * steps + p)),
        ],
        out_specs=pl.BlockSpec((each, blocks, rank, width), lambda p: (p, 0, 0, 0)),
        compiler_params=params(),
        cost_estimate=pl.CostEstimate(
            flops=2 * rows * rank * width * parts,
            bytes_accessed=2 * parts * width * (rows + blocks * rank),
            transcendentals=0,
        ),
    )(low_t, acts)


def sum_kernel(blocks, count, has_extra, outs, groups, table_ref, *refs):
    held = refs[:count]
    if groups:
        kept, sems = refs[-2:]
        refs = refs[:-2]
    dests = refs[-outs:]
    outs = dests
    if groups:
        size = kept.shape[0] // groups
        outs = [kept.at[pl.ds(n * size, size)] for n in range(groups)]
        if len(dests) == 1:
            dests = [dests[0].at[pl.ds(n * size, size)] for n in range(groups)]
    copies = []
    extra_ref = refs[count] if has_extra else None
    targets = sum(out.shape[0] for out in outs)
    rank = outs[0].shape[1]
    base = blocks * count

    for n, out_ref in enumerate(outs):
        shift = n * out_ref.shape[0]

        def step(m, carry, out_ref=out_ref, shift=shift):
            at = base + shift + m
            low = 0
            for i, held_ref in enumerate(held):
                high = low + held_ref.shape[2]

                def add(j, total, i=i, held_ref=held_ref):
                    return total + held_ref[table_ref[i * blocks + j]].astype(F32)

                def add_extra(j, total, low=low, high=high):
                    return total + extra_ref[j, :, low:high].astype(F32)

                zero = jnp.zeros((rank, high - low), F32)
                total = lax.fori_loop(table_ref[at], table_ref[at + targets], add, zero)
                if has_extra:
                    total = lax.fori_loop(
                        table_ref[at + 2 * targets], table_ref[at + 3 * targets], add_extra, total
                    )
                out_ref[m, :, low:high] = total.astype(BF16)
                low = high
            return carry

        lax.fori_loop(0, out_ref.shape[0], step, 0)
        if groups:
            copies.append(pltpu.make_async_copy(out_ref, dests[n], sems.at[n]))
            copies[-1].start()
    for copy in copies:
        copy.wait()


def slot_sums(table, held, targets, hint, extra=None, outs=1, after=(), groups=0):
    blocks, rank, _ = held[0].shape
    width = sum(x.shape[2] for x in held)
    operands = list(held) + ([] if extra is None else [extra])
    shape = jax.ShapeDtypeStruct((targets // outs, rank, width), BF16)
    return pl.pallas_call(
        functools.partial(sum_kernel, blocks, len(held), extra is not None, outs, groups),
        out_shape=[shape] * outs,
        in_specs=[pl.BlockSpec(memory_space=pltpu.SMEM)]
        + [spec()] * len(operands)
        + [pl.BlockSpec(memory_space=pl.ANY)] * len(after),
        out_specs=[pl.BlockSpec(memory_space=pltpu.HBM) if groups else spec()] * outs,
        scratch_shapes=[
            pltpu.VMEM((targets, rank, width), BF16),
            pltpu.SemaphoreType.DMA((groups,)),
        ]
        if groups
        else [],
        compiler_params=params(),
        cost_estimate=pl.CostEstimate(flops=hint, bytes_accessed=hint, transcendentals=0),
    )(table, *operands, *after)


def place_kernel(*refs):
    landing_ref, got_ref, out_ref = refs[0], refs[1], refs[-1]
    for n in range(out_ref.shape[0]):
        spot = landing_ref[n]
        value = got_ref[0, jnp.maximum(spot, 0)]
        out_ref[n] = jnp.where(spot >= 0, value, jnp.zeros_like(value))


def place_all_kernel(got_ref, *refs):
    refs[-1][...] = got_ref[0]


def place(got, landing, slots, width, column, columns, chunk, into=None):
    parts, held, rank, _ = got.shape
    operands = [got] if landing is None else [landing, got]
    specs = [pl.BlockSpec((1, held, rank, width), lambda p: (p, 0, 0, column))]
    if landing is not None:
        specs = [pl.BlockSpec(memory_space=pltpu.SMEM)] + specs
    if into is not None:
        operands.append(into)
        specs.append(pl.BlockSpec(memory_space=pl.ANY))
    return pl.pallas_call(
        place_all_kernel if landing is None else place_kernel,
        grid=(parts,),
        out_shape=jax.ShapeDtypeStruct((slots, rank, columns), BF16),
        in_specs=specs,
        out_specs=pl.BlockSpec((slots, rank, width), lambda p: (0, 0, chunk * parts + p)),
        input_output_aliases={} if into is None else {len(operands) - 1: 0},
        compiler_params=params(),
        cost_estimate=pl.CostEstimate(
            flops=0, bytes_accessed=4 * parts * slots * rank * width, transcendentals=0
        ),
    )(*operands)


def lay_kernel(first, width, has_landing, *refs):
    landing_ref, refs = (refs[0], refs[1:]) if has_landing else (None, refs)
    got_ref, _, down_ref, up_ref, zero, sems = refs
    parts, held, rank, whole = got_ref.shape
    waits = []
    if has_landing:
        zero[...] = jnp.zeros_like(zero)
    for p in range(parts):
        for o, (out, low, high, at) in enumerate(
            [(down_ref, 0, width, first + p), (up_ref, width, whole, p)]
        ):
            columns = pl.ds(at * (high - low), high - low)
            if not has_landing:
                copy = pltpu.make_async_copy(
                    got_ref.at[p, :, :, low:high], out.at[:, :, columns], sems.at[o, p, 0]
                )
                copy.start()
                waits.append(copy)
                continue
            for n in range(out.shape[0]):
                to = out.at[n, :, columns]
                sem = sems.at[o, p, n]
                none = pltpu.make_async_copy(zero.at[:, : high - low], to, sem)

                @pl.when(landing_ref[n] >= 0)
                def _(p=p, n=n, to=to, sem=sem, low=low, high=high):
                    spot = jnp.maximum(landing_ref[n], 0)
                    pltpu.make_async_copy(got_ref.at[p, spot, :, low:high], to, sem).start()

                @pl.when(landing_ref[n] < 0)
                def _(none=none):
                    none.start()

                waits.append(none)
    for wait in waits:
        wait.wait()


def lay(got, landing, first, width, into, out_width):
    parts, _, rank, _ = got.shape
    anywhere = pl.BlockSpec(memory_space=pl.ANY)
    operands = ([] if landing is None else [landing]) + [got, into]
    specs = [] if landing is None else [pl.BlockSpec(memory_space=pltpu.SMEM)]
    return pl.pallas_call(
        functools.partial(lay_kernel, first, width, landing is not None),
        out_shape=[
            jax.ShapeDtypeStruct(into.shape, BF16),
            jax.ShapeDtypeStruct(into.shape[:2] + (out_width,), BF16),
        ],
        in_specs=specs + [anywhere, anywhere],
        out_specs=[anywhere, anywhere],
        input_output_aliases={len(operands) - 1: 0},
        scratch_shapes=[
            pltpu.VMEM((rank, width), BF16),
            pltpu.SemaphoreType.DMA((2, parts, into.shape[0])),
        ],
        compiler_params=params(),
        cost_estimate=pl.CostEstimate(flops=0, bytes_accessed=4 * got.size, transcendentals=0),
    )(*operands)


def body(copies, devices, acts, grad_out, low_acts, up_weight, block_adapter, block_fill, owner_slot):
    own_blocks = block_fill.shape[0]
    blocks, adapters = block_adapter.shape[0], owner_slot.shape[0]
    own_slots, rank, out_width = up_weight.shape
    model_width = acts.shape[1]
    half_devices = devices // 2
    half_blocks, half_slots = blocks // 2, adapters // 2
    groups = [list(range(half_devices)), list(range(half_devices, devices))]
    across = [(i, (i + half_devices) % devices) for i in range(devices)]
    half = lax.axis_index("dp") // half_devices

    def within(x):
        return lax.all_to_all(x, "dp", 0, 0, axis_index_groups=groups, tiled=True)

    def relative(x, k):
        return lax.ppermute(x, "dp", [(i, i ^ k) for i in range(devices)]) if k else x

    ids = jnp.arange(adapters, dtype=jnp.int32)
    slot_of = jnp.sum(
        jnp.where(block_adapter[:, None] == ids[None, :], owner_slot[None, :], 0), axis=1
    )

    place_in_half = lax.axis_index("dp") % half_devices
    by_permutes = half_devices <= 8 and out_width // half_devices % 128 == 0
    up_held = up_products(block_fill, low_acts.T, grad_out, half_devices)
    if by_permutes:
        up_pieces = [
            lax.dynamic_index_in_dim(up_held, place_in_half ^ k, 0, False)
            for k in range(half_devices)
        ]
        up_pieces = [relative(x, k) for k, x in enumerate(up_pieces)]
    else:
        up_pieces = [within(up_held).reshape(half_blocks, rank, -1)]

    lane_groups = min(devices // 4, out_width // 128)
    row_groups = devices // lane_groups
    rows, lanes = rank // row_groups, out_width // lane_groups
    pieces = cut(up_weight, devices, lane_groups, rows, lanes)
    part = lax.all_to_all(pieces, "dp", 0, 0, tiled=True).reshape(adapters, rows, lanes)
    picked = pick(slot_of, part).reshape(devices, own_blocks, rows, lanes)
    weights = lax.all_to_all(picked, "dp", 0, 0, tiled=True)

    mine = lax.dynamic_slice_in_dim(slot_of, half * half_blocks, half_blocks)
    spots = jnp.arange(half_blocks, dtype=jnp.int32)
    before = (mine[None, :] < mine[:, None]) | (
        (mine[None, :] == mine[:, None]) & (spots[None, :] < spots[:, None])
    )
    spot_of = jnp.sum(before.astype(jnp.int32), axis=1)
    order = jnp.sum(jnp.where(spot_of[None, :] == spots[:, None], spots[None, :], 0), axis=1)
    start = jnp.sum((mine[None, :] < ids[:, None]).astype(jnp.int32), axis=1)
    count = jnp.sum((mine[None, :] == ids[:, None]).astype(jnp.int32), axis=1)
    by_half = slot_of.reshape(2, half_blocks)
    has = jnp.any(by_half[:, :, None] == ids[None, None, :], axis=1)
    crosses = has & ((ids[None, :] // half_slots) != jnp.arange(2, dtype=jnp.int32)[:, None])
    earlier = (ids[None, :] < ids[:, None])[None, :, :]
    place_of = jnp.sum((crosses[:, None, :] & earlier).astype(jnp.int32), axis=2)
    used = jnp.any(has, axis=0).reshape(-1, own_slots)
    slot_ids = jnp.arange(own_slots, dtype=jnp.int32)
    rank_of = jnp.sum(
        (used[:, None, :] & (slot_ids[None, :] < slot_ids[:, None])[None]).astype(jnp.int32), axis=2
    )
    mine_needed = jnp.stack(
        [
            jnp.max(jnp.sum(crosses.astype(jnp.int32), axis=1)),
            jnp.max(jnp.sum(used.astype(jnp.int32), axis=1)),
        ]
    ).reshape(1, 2)
    needed = mine_needed
    for k in range(1, copies):
        shift = [(i, (i + k) % copies) for i in range(copies)]
        needed = jnp.maximum(needed, lax.ppermute(mine_needed, "groups", shift))
    needed, most = needed[0, 0], needed[0, 1]

    my_cross = lax.dynamic_index_in_dim(crosses, half, 0, False)
    my_place = lax.dynamic_index_in_dim(place_of, half, 0, False)
    hot = my_cross[None, :] & (my_place[None, :] == spots[:, None])
    send_first = jnp.sum(jnp.where(hot, start[None, :], 0), axis=1)
    send_last = jnp.sum(jnp.where(hot, (start + count)[None, :], 0), axis=1)

    own = half * half_slots
    keep_first = lax.dynamic_slice_in_dim(start, own, half_slots)
    keep_last = keep_first + lax.dynamic_slice_in_dim(count, own, half_slots)
    got = lax.dynamic_index_in_dim(crosses, 1 - half, 0, False)
    got = lax.dynamic_slice_in_dim(got, own, half_slots).astype(jnp.int32)
    got_first = lax.dynamic_index_in_dim(place_of, 1 - half, 0, False)
    got_first = lax.dynamic_slice_in_dim(got_first, own, half_slots)
    keep_table = jnp.concatenate([order, keep_first, keep_last, got_first, got_first + got])

    keep = jnp.stack([keep_first, keep_last, got_first, got_first + got])
    keep = keep.reshape(4, half_devices, 1, own_slots)
    half_used = lax.dynamic_slice_in_dim(used, half * half_devices, half_devices)
    half_rank = lax.dynamic_slice_in_dim(rank_of, half * half_devices, half_devices)
    chosen = half_used[:, None, :] & (half_rank[:, None, :] == slot_ids[None, :, None])
    packed = jnp.sum(jnp.where(chosen[None], keep, 0), axis=3)
    mine_at = lax.axis_index("dp")
    landing = jnp.where(
        lax.dynamic_index_in_dim(used, mine_at, 0, False),
        lax.dynamic_index_in_dim(rank_of, mine_at, 0, False),
        -1,
    )
    up_order = order
    if by_permutes:
        source, spot = order // own_blocks, order % own_blocks
        up_order = (source ^ place_in_half) * own_blocks + spot
    orders = jnp.concatenate([order, up_order])

    low_t = rank_cotangent(block_fill, weights, grad_out, lane_groups, rank, up_pieces)
    up_held = jnp.concatenate(up_pieces)
    first = within(products(low_t, acts, half_devices, 0))
    first = first.reshape(half_blocks, rank, -1)
    second = products(low_t, acts, half_devices, 1)
    width = second.shape[3]

    def rest(
        capacity, slots, first, up_held, second, orders, send_first, send_last, keep_table, packed,
        landing
    ):
        if slots < own_slots:
            ends = packed[:, :, :slots].reshape(-1)
        else:
            ends, landing = keep_table[half_blocks:], None
        keep_a_table = jnp.concatenate([orders[:half_blocks], ends])
        keep_b_table = jnp.concatenate([orders, ends])
        targets = half_devices * slots
        ends = jnp.concatenate([send_first[:capacity], send_last[:capacity]])
        send_a_table = jnp.concatenate([orders[:half_blocks], ends])
        send_b_table = jnp.concatenate([orders, ends])
        groups = GROUPS if by_permutes else 0
        both = [within(second).reshape(half_blocks, rank, -1), up_held]
        (sent_a,) = slot_sums(send_a_table, [first], capacity, SMALL)
        came_a = lax.ppermute(sent_a, "dp", across)
        (kept_a,) = slot_sums(keep_a_table, [first], targets, SMALL, came_a, 1, (), groups)
        (sent_b,) = slot_sums(send_b_table, both, capacity, SMALL, None, 1, (kept_a,))
        came_b = lax.ppermute(sent_b, "dp", across)
        done_a = within(kept_a.reshape(half_devices, slots, rank, -1))
        down = place(done_a, landing, own_slots, width, 0, model_width, 0)
        (kept_b,) = slot_sums(keep_b_table, both, targets, LARGE, came_b, 1, (), groups)
        done_b = within(kept_b.reshape(half_devices, slots, rank, -1))
        if by_permutes:
            return tuple(lay(done_b, landing, half_devices, width, down, out_width))
        up = done_b[:, :, :, width:].transpose(1, 2, 0, 3).reshape(own_slots, rank, out_width)
        return place(done_b, landing, own_slots, width, 0, model_width, 1, down), up

    limit = min(half_blocks, half_slots)
    capacities = sorted({-(-limit * k // 24) for k in (8, 9, 10, 11, 12, 14, 24)})
    index = sum((needed > c).astype(jnp.int32) for c in capacities[:-1])
    sizes = [own_slots]
    if own_slots > 1 and by_permutes:
        sizes = [own_slots - 1, own_slots]
        index = 2 * index + (most >= own_slots).astype(jnp.int32)
        index = jnp.minimum(index, 2 * len(capacities) - 2)
    return lax.switch(
        index,
        [functools.partial(rest, c, n) for c in capacities[:-1] for n in sizes]
        + [functools.partial(rest, capacities[-1], own_slots)],
        first, up_held, second, orders, send_first, send_last, keep_table, packed, landing,
    )


def solution(mesh):
    placed = (
        P(("groups", "dp"), None),
        P(("groups", "dp"), None),
        P(("groups", "dp"), None),
        P("dp", None, None),
        P("groups"),
        P(("groups", "dp")),
        P(),
    )
    return jax.shard_map(
        functools.partial(body, mesh.shape["groups"], mesh.shape["dp"]),
        mesh=mesh,
        in_specs=placed,
        out_specs=(P(("groups", "dp"), None, None), P(("groups", "dp"), None, None)),
        check_vma=False,
    )
```
